32 devices in a mesh: fsdp: 16 (over z, x, core), tok: 2 (over y).
Axes of the slice: x: 2, y: 2, z: 4, core: 2. Of those that a mesh axis runs over, the one named last changes fastest.
Arguments:
- tokens: bfloat16 [2048, 2048], P('fsdp', 'tok'), may hold values from -6 to 6
- expert_ids: int32 [2048, 4], P('fsdp'), may hold values from 0 to 31, all different within a row; in each aligned block of 128 rows (0 to 127, 128 to 255, ...) at most 32 rows name the same one
- gate_probs: float32 [2048, 4], P('fsdp'), may hold values from 0.05 to 1
- w_gate: bfloat16 [32, 1408, 2048], P('fsdp', 'tok'), may hold values from -0.125 to 0.125
- w_up: bfloat16 [32, 1408, 2048], P('fsdp', 'tok'), may hold values from -0.125 to 0.125
- w_down: bfloat16 [32, 1408, 2048], P('fsdp', 'tok'), may hold values from -0.15625 to 0.15625
- grad_out: bfloat16 [2048, 2048], P('fsdp', 'tok'), may hold values from -6 to 6
Outputs:
- layer_out: bfloat16 [2048, 2048], P('fsdp', 'tok')
- d_tokens: bfloat16 [2048, 2048], P('fsdp', 'tok')
- d_gate_probs: float32 [2048, 4], P('fsdp')
- d_w_gate: float32 [32, 1408, 2048], P('fsdp', 'tok')
- d_w_up: float32 [32, 1408, 2048], P('fsdp', 'tok')
- d_w_down: float32 [32, 1408, 2048], P('fsdp', 'tok')
The draws below stay inside these ranges and needn't reach their ends.
Inputs may be any that keep to these rules, and one draw needn't show every extreme that they name: `expert_ids`: each token names 4 different experts. Among the tokens of one index of fsdp (aligned blocks of 128 tokens) no expert is named more than 32 times, a bound that some block reaches.
All inputs are finite; a program needn't handle non-finite values.
Results may differ from the reference program's by a relative error of at most 0.0064.
Values may be sent and summed in bfloat16 or wider, within the bound.
A program may use at most 128 MiB of HBM per device.

```python
import math
import jax
import jax.numpy as jnp
import numpy as np
from jax import lax

D = 2048
H = 1408
TOPK = 4
EXPERTS = 32
TOK_DEV = 128
CAP = 32
TOKENS = 2048
N_FSDP = 16


def steps_of(own_key, shape, pieces, low, largest):
    def one(dim, shards_of):
        steps = jax.random.uniform(jax.random.fold_in(jax.random.fold_in(own_key, 6), dim), (shards_of,), jnp.float32, low / len(pieces), largest / len(pieces))
        return jnp.repeat(jnp.exp(steps), shape[dim] // shards_of).reshape((-1,) + (1,) * (len(shape) - dim - 1))

    loudness = one(*pieces[0])
    for cut in pieces[1:]:
        loudness = loudness * one(*cut)
    return loudness


def shared_out(own_key, own, number, rows, number_of, top, bound, lean):
    order = jax.random.permutation(own_key, number_of)
    crowded, ordinary = shares(number_of, rows * top, bound, lean, True), shares(number_of, rows * top, bound, lean, False)
    places = jnp.arange(number_of)

    def named(tallies, turn):
        used = int((tallies > 0).sum())
        fixed = max(1, used // 4)
        moved = fixed + (places - fixed + turn * (used - fixed)) % max(1, number_of - fixed)
        return jnp.zeros((number_of,), jnp.int32).at[order[jnp.where(places < fixed, places, moved)]].set(jnp.asarray(tallies, jnp.int32))

    tallies = jnp.where(number % 4 == 0, named(crowded, number // 4), named(ordinary, number - number // 4 - 1))
    mixed = jax.random.permutation(jax.random.fold_in(own, 3), number_of)
    source_of, sink = mixed[0:number_of // 2 * 2:2], mixed[1:number_of // 2 * 2:2]
    slack = jnp.minimum(tallies[source_of] - 1, bound - tallies[sink]) // 2
    slack = jnp.where((source_of == order[0]) | (sink == order[0]) | (tallies[sink] == 0), 0, jnp.maximum(slack, 0))
    moved = jax.random.randint(jax.random.fold_in(own, 4), (number_of // 2,), 0, 1 << 20) % (slack + 1)
    tallies = tallies.at[source_of].add(-moved).at[sink].add(moved)
    members = jnp.searchsorted(jnp.cumsum(tallies), jnp.arange(rows * top), side="right").astype(jnp.int32)
    grid = members.reshape(top, rows).T
    grid = grid[jax.random.permutation(jax.random.fold_in(own, 1), rows)]
    turn = jax.random.randint(jax.random.fold_in(own, 2), (rows, 1), 0, top)
    return jnp.take_along_axis(grid, (jnp.arange(top)[None, :] + turn) % top, axis=1)


def shares(amount, total, reach, slope, full):
    loads = [(1 << 20) // math.isqrt(rank ** slope) + 1 for rank in range(1, amount + 1)]
    largest = reach if full else min(reach, max(-(-total // amount), total * loads[0] // sum(loads)))
    least = 1 if total - largest >= amount - 1 else 0
    given, rest = [largest] + [least] * (amount - 1), total - largest - least * (amount - 1)
    while rest > 0:
        movable = [i for i in range(1, amount) if given[i] < largest] or [i for i in range(1, amount) if given[i] < reach]
        pool, remaining = sum([loads[i] for i in movable]), rest
        for i in movable:
            addition = min(reach - given[i], max(1, remaining * loads[i] // pool), rest)
            given[i] = given[i] + addition
            rest = rest - addition
    return np.array(given)


def noise(stream_key, extent, spread, most, split=(), kind=jnp.bfloat16):
    values = spread * jax.random.normal(stream_key, extent, jnp.float32)
    if split:
        values = values * steps_of(stream_key, extent, split, -0.22, 0.18)
    return jnp.clip(values, -most, most).astype(kind)


def setup_inputs(seed: int = 0) -> dict:
    seeds = jax.random.split(jax.random.key(seed), 8)
    tokens = noise(seeds[0], (TOKENS, D), 1.0, 6.0, ((0, 16), (1, 2)))
    expert_ids_keys = jax.random.split(jax.random.fold_in(seeds[1], 1), TOKENS // TOK_DEV)
    expert_ids_turns = jax.random.permutation(jax.random.fold_in(seeds[1], 3), TOKENS // TOK_DEV)
    expert_ids = jax.vmap(lambda own, number: shared_out(jax.random.fold_in(seeds[1], 2), own, number, TOK_DEV, EXPERTS, TOPK, CAP, 2))(expert_ids_keys, expert_ids_turns).reshape((TOKENS, TOPK))
    gate_probs = jnp.clip(jnp.exp(math.log(1.0) - 2.9957323 * jax.random.uniform(seeds[2], (TOKENS, TOPK), jnp.float32) ** steps_of(seeds[2], (TOKENS, TOPK), ((0, 16),), -0.2, 0.2)), 0.05, 1.0)
    w_gate = noise(seeds[3], (EXPERTS, H, D), D ** -0.5, 0.125, ((0, 16), (1, 2)))
    w_up = noise(seeds[4], (EXPERTS, H, D), D ** -0.5, 0.125, ((0, 16), (1, 2)))
    w_down = noise(seeds[5], (EXPERTS, H, D), H ** -0.5, 0.15625, ((0, 16), (1, 2)))
    grad_out = noise(seeds[6], (TOKENS, D), 1.0, 6.0, ((0, 16), (1, 2)))
    return {"tokens": tokens, "expert_ids": expert_ids, "gate_probs": gate_probs, "w_gate": w_gate, "w_up": w_up, "w_down": w_down, "grad_out": grad_out}


def route_slots(expert_ids):
    blocks = expert_ids.reshape(N_FSDP, TOK_DEV * TOPK)
    onehot = (blocks[:, :, None] == jnp.arange(EXPERTS, dtype=jnp.int32)[None, None, :]).astype(jnp.int32)
    position = jnp.sum(jnp.cumsum(onehot, axis=1) * onehot, axis=2) - 1
    block_index = jnp.arange(N_FSDP, dtype=jnp.int32)[:, None]
    slot = blocks * (N_FSDP * CAP) + block_index * CAP + position
    return slot.reshape(-1).astype(jnp.int32)


def expert_pass(operands):
    inputs, weight_gate, weight_up, weight_down, d_out = operands
    gate = jnp.dot(inputs, weight_gate.T, preferred_element_type=jnp.float32)
    upper = jnp.dot(inputs, weight_up.T, preferred_element_type=jnp.float32)
    sigma = jax.nn.sigmoid(gate)
    active = gate * sigma
    hidden = (active * upper).astype(jnp.bfloat16)
    expert_out = jnp.dot(hidden, weight_down, preferred_element_type=jnp.float32).astype(jnp.bfloat16)
    d_hidden = jnp.dot(d_out, weight_down.T, preferred_element_type=jnp.float32)
    d_down = jnp.dot(hidden.T, d_out, preferred_element_type=jnp.float32)
    d_gate = (d_hidden * upper * sigma * (1.0 + gate * (1.0 - sigma))).astype(jnp.bfloat16)
    d_upper = (d_hidden * active).astype(jnp.bfloat16)
    d_wgate = jnp.dot(d_gate.T, inputs, preferred_element_type=jnp.float32)
    d_wup = jnp.dot(d_upper.T, inputs, preferred_element_type=jnp.float32)
    back = jnp.dot(d_gate, weight_gate, preferred_element_type=jnp.float32)
    back = back + jnp.dot(d_upper, weight_up, preferred_element_type=jnp.float32)
    d_inputs = back.astype(jnp.bfloat16)
    return expert_out, d_inputs, d_wgate, d_wup, d_down


def reference(tokens, expert_ids, gate_probs, w_gate, w_up, w_down, grad_out):
    slot = route_slots(expert_ids)
    owner = jnp.arange(TOKENS * TOPK, dtype=jnp.int32) // TOPK
    total = EXPERTS * N_FSDP * CAP
    expert_in = jnp.zeros((total, D), jnp.bfloat16).at[slot].set(tokens[owner]).reshape(EXPERTS, N_FSDP * CAP, D)
    probs = gate_probs[:, :, None]
    scaled = (probs * grad_out[:, None, :].astype(jnp.float32)).astype(jnp.bfloat16).reshape(TOKENS * TOPK, D)
    d_expert_out = jnp.zeros((total, D), jnp.bfloat16).at[slot].set(scaled).reshape(EXPERTS, N_FSDP * CAP, D)
    expert_out, d_expert_in, d_w_gate, d_w_up, d_w_down = lax.map(expert_pass, (expert_in, w_gate, w_up, w_down, d_expert_out))
    route_out = expert_out.reshape(total, D)[slot].reshape(TOKENS, TOPK, D).astype(jnp.float32)
    layer_out = jnp.sum(probs * route_out, axis=1).astype(jnp.bfloat16)
    d_gate_probs = jnp.sum(grad_out[:, None, :].astype(jnp.float32) * route_out, axis=2)
    route_grad = d_expert_in.reshape(total, D)[slot].reshape(TOKENS, TOPK, D).astype(jnp.float32)
    d_tokens = jnp.sum(route_grad, axis=1).astype(jnp.bfloat16)
    return (layer_out, d_tokens, d_gate_probs, d_w_gate, d_w_up, d_w_down)
```

```python
import jax
import jax.numpy as jnp
from jax import lax
from jax.experimental import pallas as pl
from jax.experimental.pallas import tpu as pltpu
from jax.sharding import PartitionSpec as P

CAP = 32
MESH = pl.DeviceIdType.MESH


def flip(bit, change):
    return 1 - bit if change else bit


class Place:
    def __init__(self):
        f = lax.axis_index("fsdp")
        self.t = lax.axis_index("tok")
        self.core = f % 2
        self.x = (f // 2) % 2
        self.z0 = (f // 4) % 2
        self.z1 = f // 8

    def block(self, dz=0, dx=0, dc=0):
        z = flip(self.z1, dz // 2) * 2 + flip(self.z0, dz % 2)
        return z * 4 + flip(self.x, dx) * 2 + flip(self.core, dc)

    def device(self, dz=0, dx=0, dy=0, dc=0):
        return (self.block(dz, dx, dc), flip(self.t, dy))

    def columns(self, dy, width):
        return pl.ds(pl.multiple_of(flip(self.t, dy) * width, width), width)

    def partners(self):
        return (
            [self.device(dz=d) for d in (1, 2, 3)]
            + [self.device(dz=d, dx=1) for d in range(4)]
            + [self.device(dy=1), self.device(dc=1)]
        )


def greet(place):
    barrier = pltpu.get_barrier_semaphore()
    partners = place.partners()
    for partner in partners:
        pl.semaphore_signal(barrier, inc=1, device_id=partner, device_id_type=MESH)
    pl.semaphore_wait(barrier, len(partners))


def arrive(ref, sem):
    pltpu.make_async_copy(ref, ref, sem).wait()


def layer_kernel(
    tok_in, grad_in, routes_in, wg_in, wu_in, wd_in,
    x_out, c_out, hid_out, dg_out, du_out, layer_out, dtok_out, dprob_out,
    g, x, xs, wg, wu, wd, act, wide, near, zbuf,
    routes, sel, back, row_prob, inverse, dr, drs, dpart, dbuf, dsum,
    own_sem, w_sem, zs_sem, xsend_sem, ysend_sem, recv_sem,
    rs_sem, rr_sem, px_sem, pr_sem, st_sem, sr_sem, ds_sem, dr_sem,
    xo_sem, ao_sem, ws_sem, wr_sem, ns_sem, nr_sem, ss_sem, sz_sem,
    qs_sem, qr_sem, credit,
):
    place = Place()
    f32, bf16 = jnp.float32, jnp.bfloat16
    rows, width = tok_in.shape
    full = 2 * width
    half = rows // 2
    local, hid = wg.shape[:2]
    topk = 4
    me = place.device

    def start(copy):
        copy.start()
        return copy

    def remote(source, target, ssem, rsem, to):
        return start(
            pltpu.make_async_remote_copy(
                src_ref=source, dst_ref=target, send_sem=ssem, recv_sem=rsem,
                device_id=to, device_id_type=MESH,
            )
        )

    own = [
        start(pltpu.make_async_copy(ref, g.at[0, 0, a, :, place.columns(0, width)], own_sem.at[a]))
        for a, ref in enumerate((tok_in, grad_in))
    ]
    loads = {}
    for l in range(local):
        for i, (ref, to) in enumerate(((wg_in, wg), (wu_in, wu), (wd_in, wd))):
            loads[i, l] = start(pltpu.make_async_copy(ref.at[l], to.at[l], w_sem.at[i, l]))
    greet(place)
    sent = {}

    for dz in range(4):
        for dx in range(2):
            if dz or dx:
                j = dz * 2 + dx
                sent["r", j] = remote(routes_in, routes.at[j], rs_sem.at[j], rr_sem.at[j], me(dz, dx))
    routes[0] = routes_in[...]
    for copy in own:
        copy.wait()

    def piece(h, dz, dx, dy):
        return g.at[dz, dx, :, pl.ds(h * half, half), place.columns(dy, width)]

    def by_z(h, dz):
        sent["z", h, dz] = remote(
            piece(h, 0, 0, 0), piece(h, dz, 0, 0), zs_sem.at[h, dz], recv_sem.at[h, dz, 0, 0], me(dz)
        )

    def by_x(h, dz, dy):
        sent["x", h, dz, dy] = remote(
            piece(h, dz, 0, dy), piece(h, dz, 1, dy), xsend_sem.at[h, dz, dy],
            recv_sem.at[h, dz, 1, dy], me(0, 1),
        )

    def by_y(h, dz, dx):
        sent["y", h, dz, dx] = remote(
            piece(h, dz, dx, 0), piece(h, dz, dx, 0), ysend_sem.at[h, dz, dx],
            recv_sem.at[h, dz, dx, 1], me(0, 0, 1),
        )

    def got(h, dz, dx, dy):
        arrive(piece(h, dz, dx, dy), recv_sem.at[h, dz, dx, dy])

    def column(dz):
        for h in range(2):
            if dz:
                got(h, dz, 0, 0)
            if h == 0:
                by_x(h, dz, 0)
                by_y(h, dz, 0)
            else:
                by_y(h, dz, 0)
                by_x(h, dz, 0)

    def plane(dz):
        got(0, dz, 1, 0)
        by_y(0, dz, 1)
        got(1, dz, 0, 1)
        by_x(1, dz, 1)

    def last(dz):
        got(0, dz, 0, 1)
        got(1, dz, 1, 0)
        got(0, dz, 1, 1)
        got(1, dz, 1, 1)

    experts = [
        (place.block(0, 0, e // local) * local + e % local).astype(f32) for e in range(2 * local)
    ]

    def build(j):
        names = routes[j, :topk, :]
        probs = routes[j, topk:, :]
        before = (
            lax.broadcasted_iota(jnp.int32, (rows, rows), 0)
            < lax.broadcasted_iota(jnp.int32, (rows, rows), 1)
        ).astype(f32).astype(bf16)
        hits, prob = [], []
        for e in experts:
            chosen = names == e
            hits.append(jnp.max(jnp.where(chosen, 1.0, 0.0), axis=0, keepdims=True))
            prob.append(jnp.sum(jnp.where(chosen, probs, 0.0), axis=0, keepdims=True))
        hit = jnp.concatenate(hits + [jnp.zeros((4, rows), f32)], axis=0)
        spot = jnp.dot(hit.astype(bf16), before, preferred_element_type=f32)
        spot = jnp.where(hit > 0.0, spot, -1.0)
        number = lax.broadcasted_iota(jnp.int32, (CAP, rows), 0).astype(f32)
        ones, high, low, full_prob, inv = [], [], [], [], []
        for e in range(2 * local):
            filled = jnp.broadcast_to(spot[e : e + 1], (CAP, rows)) == number
            top = prob[e].astype(bf16).astype(f32)
            ones.append(jnp.where(filled, 1.0, 0.0))
            high.append(jnp.where(filled, top, 0.0))
            low.append(jnp.where(filled, prob[e] - top, 0.0))
            full_prob.append(jnp.where(filled, prob[e], 0.0))
            inv.append(jnp.where(hits[e] > 0.0, 1.0 / jnp.maximum(prob[e], 1e-30), 0.0))
        ones = jnp.concatenate(ones, axis=0)
        sel[j] = ones.astype(bf16)
        back[j, 0] = ones.T.astype(bf16)
        back[j, 1] = jnp.concatenate(high, axis=0).T.astype(bf16)
        back[j, 2] = jnp.concatenate(low, axis=0).T.astype(bf16)
        row_prob[j] = jnp.sum(jnp.concatenate(full_prob, axis=0), axis=1, keepdims=True)
        inverse[j] = jnp.concatenate(inv + [jnp.zeros((4, rows), f32)], axis=0)

    def build_all(first, end):
        for j in range(first, end):
            if j:
                arrive(routes.at[j], rr_sem.at[j])

        @pl.loop(first, end)
        def _(j):
            build(j)

    tile = 512

    def select(dz):
        @pl.loop(0, 2)
        def _(dx):
            j = dz * 2 + dx
            at = pl.ds(pl.multiple_of(dx * CAP, CAP), CAP)

            @pl.loop(0, full // tile)
            def _(n):
                cols = pl.ds(pl.multiple_of(n * tile, tile), tile)
                for a in range(2):
                    picked = jnp.dot(sel[j], g[dz, dx, a, :, cols], preferred_element_type=f32)
                    if a:
                        picked = picked * row_prob[j]
                    picked = picked.astype(bf16)
                    for l in range(local):
                        x[a, l, dz, at, cols] = picked[l * CAP : (l + 1) * CAP]
                        m = local + l
                        xs[a, l, dz, at, cols] = picked[m * CAP : (m + 1) * CAP]

        sent["p", dz] = remote(
            xs.at[:, :, dz], x.at[:, :, dz, pl.ds(half, half)], px_sem.at[dz], pr_sem.at[dz], me(0, 0, 0, 1)
        )

    def packed(dz):
        arrive(x.at[:, :, dz, pl.ds(half, half)], pr_sem.at[dz])
        for a, ref in enumerate((x_out, c_out)):
            sent["xo", a, dz] = start(
                pltpu.make_async_copy(x.at[a, :, dz], ref.at[:, dz], xo_sem.at[a, dz])
            )

    nt = (((1,), (1,)), ((), ()))
    tiles = [(h, min(256, hid - h)) for h in range(0, hid, 256)]

    def forward(dz, l):
        if dz == 0:
            for i in range(3):
                loads[i, l].wait()
        total = jnp.zeros((rows, 1), f32)
        for h, n in tiles:
            at = pl.ds(h, n)
            gate = lax.dot_general(x[0, l, dz], wg[l, at, :], nt, preferred_element_type=f32)
            upper = lax.dot_general(x[0, l, dz], wu[l, at, :], nt, preferred_element_type=f32)
            d_hidden = lax.dot_general(x[1, l, dz], wd[l, at, :], nt, preferred_element_type=f32)
            sigma = jax.nn.sigmoid(gate)
            active = gate * sigma
            hidden = active * upper
            total = total + jnp.sum(hidden * d_hidden, axis=1, keepdims=True)
            act[0, l, dz, :, at] = hidden.astype(bf16)
            act[1, l, dz, :, at] = (d_hidden * upper * sigma * (1.0 + gate * (1.0 - sigma))).astype(bf16)
            act[2, l, dz, :, at] = (d_hidden * active).astype(bf16)
        total = jnp.broadcast_to(total, (rows, rows))
        for dx in range(2):
            dr[dz, dx, l * CAP : (l + 1) * CAP, :] = total[dx * CAP : (dx + 1) * CAP]
            drs[dz, dx, l * CAP : (l + 1) * CAP, :] = total[half + dx * CAP : half + (dx + 1) * CAP]

    def handed(dz):
        for i, ref in enumerate((hid_out, dg_out, du_out)):
            sent["ao", i, dz] = start(
                pltpu.make_async_copy(act.at[i, :, dz], ref.at[:, dz], ao_sem.at[i, dz])
            )
        sent["d", dz] = remote(
            drs.at[dz], dr.at[dz, :, pl.ds(half, half)], ds_sem.at[dz], dr_sem.at[dz], me(0, 0, 0, 1)
        )
        sent.pop(("xo", 0, dz)).wait()
        sent.pop(("xo", 1, dz)).wait()
        pl.semaphore_signal(credit.at[dz], inc=1, device_id=me(0, 0, 0, 1), device_id_type=MESH)
        sent.pop(("p", dz)).wait_send()

    def backward(dz, l):
        mine = pl.ds(l * CAP, CAP)

        @pl.loop(0, full // tile)
        def _(n):
            cols = pl.ds(pl.multiple_of(n * tile, tile), tile)
            out = jnp.dot(act[0, l, dz], wd[l, :, cols], preferred_element_type=f32)
            back_rows = jnp.dot(act[1, l, dz], wg[l, :, cols], preferred_element_type=f32)
            back_rows = back_rows + jnp.dot(act[2, l, dz], wu[l, :, cols], preferred_element_type=f32)
            for a, value in enumerate((out.astype(bf16), back_rows.astype(bf16))):
                for dx in range(2):
                    x[a, dx, dz, mine, cols] = value[dx * CAP : (dx + 1) * CAP]
                    xs[a, dx, dz, mine, cols] = value[half + dx * CAP : half + (dx + 1) * CAP]

    def returned(dz):
        pl.semaphore_wait(credit.at[dz], 1)
        sent["s", dz] = remote(
            xs.at[:, :, dz], x.at[:, :, dz, pl.ds(half, half)], st_sem.at[dz], sr_sem.at[dz], me(0, 0, 0, 1)
        )

    def put_back(dz):
        for h in range(2):
            for key in (("x", h, dz, 0), ("y", h, dz, 0)):
                sent.pop(key).wait_send()
        sent.pop(("y", 0, dz, 1)).wait_send()
        sent.pop(("x", 1, dz, 1)).wait_send()
        if dz == 0:
            for h in range(2):
                for d in range(1, 4):
                    sent.pop(("z", h, d)).wait_send()
        arrive(x.at[:, :, dz, pl.ds(half, half)], sr_sem.at[dz])
        arrive(dr.at[dz, :, pl.ds(half, half)], dr_sem.at[dz])

        @pl.loop(0, 2)
        def _(dx):
            j = dz * 2 + dx

            @pl.loop(0, full // tile)
            def _(n):
                cols = pl.ds(pl.multiple_of(n * tile, tile), tile)
                out = jnp.dot(back[j, 1], x[0, dx, dz, :, cols], preferred_element_type=f32)
                out = out + jnp.dot(back[j, 2], x[0, dx, dz, :, cols], preferred_element_type=f32)
                g[dz, dx, 0, :, cols] = out.astype(bf16)
                into = jnp.dot(back[j, 0], x[1, dx, dz, :, cols], preferred_element_type=f32)
                g[dz, dx, 1, :, cols] = into.astype(bf16)

            names = routes[j, :topk, :]
            weighted = dr[dz, dx] * sel[j].astype(f32)
            total = jnp.zeros((topk, rows), f32)
            for e, name in enumerate(experts):
                value = jnp.sum(weighted[e * CAP : (e + 1) * CAP], axis=0, keepdims=True)
                value = value * inverse[j, e : e + 1, :]
                total = total + jnp.where(names == name, value, 0.0)
            dpart[j] = jnp.concatenate([total, jnp.zeros((8 - topk, rows), f32)], axis=0)

        for dx in range(2):
            j = dz * 2 + dx
            if j:
                sent["q", j] = remote(dpart.at[j], dbuf.at[j], qs_sem.at[j], qr_sem.at[j], me(dz, dx))

    def send_wide(dz):
        for h in range(2):
            across = me(0, 0, 1) if h == 0 else me(0, 1)
            for other in (1, 0):
                dx, dy = (other, 1) if h == 0 else (1, other)
                sent["w", h, dz, other] = remote(
                    piece(h, dz, dx, dy), wide.at[h, dz, other], ws_sem.at[h, dz, other],
                    wr_sem.at[h, dz, other], across,
                )

    def add(target, source):
        for a in range(2):
            @pl.loop(0, half // 16)
            def _(i):
                at = pl.ds(pl.multiple_of(i * 16, 16), 16)
                target[a, at, :] = target[a, at, :] + source[a, at, :]

    def send_near(dz):
        for other in (1, 0):
            for h in range(2):
                dx, dy = (other, 0) if h == 0 else (0, other)
                arrive(wide.at[h, dz, other], wr_sem.at[h, dz, other])
                add(wide.at[h, dz, other], piece(h, dz, dx, dy))
                if other:
                    along = me(0, 1) if h == 0 else me(0, 0, 1)
                    sent["n", h, dz] = remote(
                        wide.at[h, dz, 1], near.at[h, dz], ns_sem.at[h, dz], nr_sem.at[h, dz], along
                    )

    def send_z(dz):
        for h in range(2):
            arrive(near.at[h, dz], nr_sem.at[h, dz])
            add(near.at[h, dz], wide.at[h, dz, 0])
            if dz:
                sent["f", h, dz] = remote(
                    near.at[h, dz], zbuf.at[h, dz - 1], ss_sem.at[h, dz], sz_sem.at[h, dz], me(dz)
                )

    for h in range(2):
        by_z(h, 1)
    column(0)
    for dz in (2, 3):
        for h in range(2):
            by_z(h, dz)
    build_all(0, 8)
    plane(0)
    column(1)
    last(0)
    for dz in range(4):
        select(dz)
        if dz < 3:
            plane(dz + 1)
        packed(dz)
        forward(dz, 0)
        if dz < 2:
            column(dz + 2)
        forward(dz, 1)
        handed(dz)
        if dz == 2:
            send_wide(1)
        backward(dz, 0)
        backward(dz, 1)
        returned(dz)
        if dz == 3:
            send_near(1)
        put_back(dz)
        if dz < 3:
            last(dz + 1)
        if dz >= 2:
            send_wide(dz)
    send_near(2)
    send_z(1)
    send_wide(0)
    send_near(3)
    send_z(2)

    total = dpart[0]
    for j in range(1, 8):
        arrive(dbuf.at[j], qr_sem.at[j])
        total = total + dbuf[j]
    dsum[0] = total
    peer = remote(dsum.at[0], dsum.at[1], qs_sem.at[0], qr_sem.at[0], me(0, 0, 1))

    send_near(0)
    send_z(3)
    send_z(0)
    arrive(dsum.at[1], qr_sem.at[0])
    dprob_out[...] = dsum[0] + dsum[1]
    for dz in (1, 2, 3):
        for h in range(2):
            arrive(zbuf.at[h, dz - 1], sz_sem.at[h, dz])
    for a, ref in enumerate((layer_out, dtok_out)):
        for h in range(2):
            @pl.loop(0, half // 16)
            def _(i):
                at = pl.ds(pl.multiple_of(i * 16, 16), 16)
                total = near[h, 0, a, at, :].astype(f32)
                for dz in (1, 2, 3):
                    total = total + zbuf[h, dz - 1, a, at, :].astype(f32)
                to = pl.ds(pl.multiple_of(h * half + i * 16, 16), 16)
                ref[to, :] = total.astype(bf16)
    peer.wait_send()
    for key, copy in sent.items():
        if key[0] == "ao":
            copy.wait()
        else:
            copy.wait_send()


def layer(tokens, grad_out, routes, w_gate, w_up, w_down):
    rows, width = tokens.shape
    local, hid, full = w_gate.shape
    half = rows // 2
    bf16, f32 = jnp.bfloat16, jnp.float32
    any_space = pl.BlockSpec(memory_space=pl.ANY)
    vmem = pl.BlockSpec(memory_space=pltpu.VMEM)
    shape = jax.ShapeDtypeStruct
    packed = shape((local, 4, rows, full), bf16)
    acts = shape((local, 4, rows, hid), bf16)
    out = shape((rows, width), bf16)
    dma = pltpu.SemaphoreType.DMA
    return pl.pallas_call(
        layer_kernel,
        out_shape=(packed, packed, acts, acts, acts, out, out, shape((8, rows), f32)),
        in_specs=[any_space, any_space, vmem, any_space, any_space, any_space],
        out_specs=[any_space] * 5 + [vmem] * 3,
        scratch_shapes=[
            pltpu.VMEM((4, 2, 2, rows, full), bf16),
            pltpu.VMEM((2, 2, 4, rows, full), bf16),
            pltpu.VMEM((2, 2, 4, half, full), bf16),
            pltpu.VMEM((local, hid, full), bf16),
            pltpu.VMEM((local, hid, full), bf16),
            pltpu.VMEM((local, hid, full), bf16),
            pltpu.VMEM((3, local, 4, rows, hid), bf16),
            pltpu.VMEM((2, 4, 2, 2, half, width), bf16),
            pltpu.VMEM((2, 4, 2, half, width), bf16),
            pltpu.VMEM((2, 3, 2, half, width), bf16),
            pltpu.VMEM((8, 8, rows), f32),
            pltpu.VMEM((8, rows, rows), bf16),
            pltpu.VMEM((8, 3, rows, rows), bf16),
            pltpu.VMEM((8, rows, 1), f32),
            pltpu.VMEM((8, 8, rows), f32),
            pltpu.VMEM((4, 2, rows, rows), f32),
            pltpu.VMEM((4, 2, half, rows), f32),
            pltpu.VMEM((8, 8, rows), f32),
            pltpu.VMEM((8, 8, rows), f32),
            pltpu.VMEM((2, 8, rows), f32),
            dma((2,)), dma((3, local)), dma((2, 4)), dma((2, 4, 2)), dma((2, 4, 2)), dma((2, 4, 2, 2)),
            dma((8,)), dma((8,)), dma((4,)), dma((4,)), dma((4,)), dma((4,)), dma((4,)), dma((4,)),
            dma((2, 4)), dma((3, 4)), dma((2, 4, 2)), dma((2, 4, 2)), dma((2, 4)), dma((2, 4)),
            dma((2, 4)), dma((2, 4)), dma((8,)), dma((8,)),
            pltpu.SemaphoreType.REGULAR((4,)),
        ],
        compiler_params=pltpu.CompilerParams(
            collective_id=0, has_side_effects=True, vmem_limit_bytes=61 * 2**20
        ),
    )(tokens, grad_out, routes, w_gate, w_up, w_down)


def by_one_kernel(tokens, expert_ids, gate_probs, w_gate, w_up, w_down, grad_out):
    topk = expert_ids.shape[1]
    local, hid, full = w_gate.shape
    f32 = jnp.float32
    routes = jnp.concatenate([expert_ids.astype(f32).T, gate_probs.T], axis=0)
    x, c, hidden, d_gate, d_up, layer_out, d_tokens, d_prob = layer(
        tokens, grad_out, routes, w_gate, w_up, w_down
    )
    x, c = (v.reshape(local, -1, full) for v in (x, c))
    hidden, d_gate, d_up = (v.reshape(local, -1, hid) for v in (hidden, d_gate, d_up))

    def weight(rows, values):
        return jnp.einsum("erh,erd->ehd", rows, values, preferred_element_type=f32)

    return (
        layer_out, d_tokens, d_prob[:topk].T,
        weight(d_gate, x), weight(d_up, x), weight(hidden, c),
    )


def gather_any(value):
    wide = lax.all_gather(value, "tok", axis=1, tiled=True)
    return lax.all_gather(wide, "fsdp", axis=0, tiled=False)


def scatter_any(value):
    blocks, rows, full = value.shape
    mine = lax.psum_scatter(
        value.reshape(blocks * rows, full), "fsdp", scatter_dimension=0, tiled=True
    )
    return lax.psum_scatter(mine, "tok", scatter_dimension=1, tiled=True)


def on_device(tokens, expert_ids, gate_probs, w_gate, w_up, w_down, grad_out):
    tok_rows, topk = expert_ids.shape
    local = w_gate.shape[0]
    f32 = jnp.float32
    me = lax.axis_index("fsdp")

    routes = jnp.concatenate([expert_ids.astype(f32).T, gate_probs.T], axis=0)
    routes = lax.all_gather(routes, "fsdp", axis=0, tiled=False)
    all_tokens, all_grads = gather_any(tokens), gather_any(grad_out)
    blocks = all_tokens.shape[0]

    names = routes[:, :topk]
    mine = (me * local + jnp.arange(local, dtype=jnp.int32)).astype(f32)
    chosen = names[None] == mine[:, None, None, None]
    hit = jnp.any(chosen, axis=2)
    prob = jnp.sum(jnp.where(chosen, routes[None, :, topk:], 0.0), axis=2)
    before = jnp.triu(jnp.ones((tok_rows, tok_rows), jnp.bfloat16), 1)
    place = jnp.einsum("ebs,st->ebt", hit.astype(jnp.bfloat16), before, preferred_element_type=f32)
    place = jnp.where(hit, place, -1.0)
    filled = place[:, :, None, :] == jnp.arange(CAP, dtype=jnp.int32).astype(f32)[None, None, :, None]
    select = filled.astype(jnp.bfloat16)
    row_prob = jnp.sum(jnp.where(filled, prob[:, :, None, :], 0.0), axis=3)
    row_prob = row_prob.reshape(local, blocks * CAP, 1)

    def pick(values):
        rows = jnp.einsum("ebrt,btd->ebrd", select, values, preferred_element_type=f32)
        return rows.astype(jnp.bfloat16).reshape(local, blocks * CAP, values.shape[-1])

    def place_back(rows):
        rows = rows.astype(jnp.bfloat16).reshape(local, blocks, CAP, rows.shape[-1])
        values = jnp.einsum("ebrt,ebrd->btd", select, rows, preferred_element_type=f32)
        return values.astype(jnp.bfloat16)

    inputs = pick(all_tokens)
    cotangent = pick(all_grads)
    gate = jnp.einsum("erd,ehd->erh", inputs, w_gate, preferred_element_type=f32)
    upper = jnp.einsum("erd,ehd->erh", inputs, w_up, preferred_element_type=f32)
    raw = jnp.einsum("erd,ehd->erh", cotangent, w_down, preferred_element_type=f32)
    sigma = jax.nn.sigmoid(gate)
    active = gate * sigma
    hidden = active * upper
    weighted = (row_prob * hidden).astype(jnp.bfloat16)
    d_hidden = row_prob * raw
    d_gate = (d_hidden * upper * sigma * (1.0 + gate * (1.0 - sigma))).astype(jnp.bfloat16)
    d_upper = (d_hidden * active).astype(jnp.bfloat16)
    d_rows = jnp.sum(hidden * raw, axis=2).reshape(local, blocks, CAP)

    out_rows = jnp.einsum("erh,ehd->erd", weighted, w_down, preferred_element_type=f32)
    in_rows = jnp.einsum("erh,ehd->erd", d_gate, w_gate, preferred_element_type=f32)
    in_rows = in_rows + jnp.einsum("erh,ehd->erd", d_upper, w_up, preferred_element_type=f32)
    part_out, part_in = place_back(out_rows), place_back(in_rows)
    layer_out, d_tokens = scatter_any(part_out), scatter_any(part_in)

    d_w_down = jnp.einsum("erh,erd->ehd", weighted, cotangent, preferred_element_type=f32)
    d_w_gate = jnp.einsum("erh,erd->ehd", d_gate, inputs, preferred_element_type=f32)
    d_w_up = jnp.einsum("erh,erd->ehd", d_upper, inputs, preferred_element_type=f32)

    d_prob = jnp.sum(jnp.where(filled, d_rows[:, :, :, None], 0.0), axis=2)
    d_prob = jnp.sum(jnp.where(chosen, d_prob[:, :, None, :], 0.0), axis=0)
    d_prob = d_prob.reshape(blocks, topk * tok_rows)
    d_prob = lax.all_to_all(d_prob, "fsdp", split_axis=0, concat_axis=0, tiled=True)
    d_prob = jnp.sum(d_prob, axis=0)
    size = lax.axis_size("tok")
    mine_only = d_prob
    for turn in range(1, size):
        pairs = [(i, (i + turn) % size) for i in range(size)]
        d_prob = d_prob + lax.ppermute(mine_only, "tok", pairs)
    d_gate_probs = d_prob.reshape(topk, tok_rows).T
    return (layer_out, d_tokens, d_gate_probs, d_w_gate, d_w_up, d_w_down)


def solution(mesh):
    by_kernel = mesh.shape["fsdp"] == 16 and mesh.shape["tok"] == 2
    return jax.shard_map(
        by_one_kernel if by_kernel else on_device,
        mesh=mesh,
        in_specs=(
            P("fsdp", "tok"),
            P("fsdp", None),
            P("fsdp", None),
            P("fsdp", "tok", None),
            P("fsdp", "tok", None),
            P("fsdp", "tok", None),
            P("fsdp", "tok"),
        ),
        out_specs=(
            P("fsdp", "tok"),
            P("fsdp", "tok"),
            P("fsdp", None),
            P("fsdp", "tok", None),
            P("fsdp", "tok", None),
            P("fsdp", "tok", None),
        ),
        check_vma=False,
    )
```

```python
import jax
import jax.numpy as jnp
from jax import lax
from jax.experimental import pallas as pl
from jax.experimental.pallas import tpu as pltpu
from jax.sharding import PartitionSpec as P

CAP = 32
MESH = pl.DeviceIdType.MESH


def flip(bit, change):
    return 1 - bit if change else bit


class Place:
    def __init__(self):
        f = lax.axis_index("fsdp")
        self.t = lax.axis_index("tok")
        self.core = f % 2
        self.x = (f // 2) % 2
        self.z0 = (f // 4) % 2
        self.z1 = f // 8

        self.inner = self.z0 + self.z1 - 2 * self.z0 * self.z1

    def index(self, z1, z0, dx, dc):
        return (z1 * 2 + z0) * 4 + flip(self.x, dx) * 2 + flip(self.core, dc)

    def block(self, dx=0, dc=0):
        return self.index(self.z1, self.z0, dx, dc)

    def far(self, slot, dx=0):
        if slot < 2:
            z1, z0 = self.z1, flip(self.z0, slot)
        else:
            turn = self.inner if slot == 2 else 1 - self.inner
            z1, z0 = 1 - self.z1, self.z0 + turn - 2 * self.z0 * turn
        return (self.index(z1, z0, dx, 0), self.t)

    def slot_there(self, slot):
        return slot if slot < 2 else 3 - self.inner

    def inward(self):
        z = self.inner * (2 - self.z1) + (1 - self.inner) * (1 + self.z1)
        return (z * 4 + self.x * 2 + self.core, self.t)

    def outward(self):
        return (3 * self.z1 * 4 + self.x * 2 + self.core, self.t)

    def device(self, dx=0, dy=0, dc=0):
        return (self.block(dx, dc), flip(self.t, dy))

    def columns(self, dy, width):
        return pl.ds(pl.multiple_of(flip(self.t, dy) * width, width), width)

    def partners(self):
        return (
            [self.far(slot) for slot in (1, 2, 3)]
            + [self.far(slot, 1) for slot in range(4)]
            + [self.device(dy=1), self.device(dc=1)]
        )


def greet(place):
    barrier = pltpu.get_barrier_semaphore()
    partners = place.partners()
    for partner in partners:
        pl.semaphore_signal(barrier, inc=1, device_id=partner, device_id_type=MESH)
    pl.semaphore_wait(barrier, len(partners))


def arrive(ref, sem):
    pltpu.make_async_copy(ref, ref, sem).wait()


def layer_kernel(
    tok_in, grad_in, routes_in, wg_in, wu_in, wd_in,
    x_out, c_out, hid_out, dg_out, du_out, far_out, layer_out, dtok_out, dprob_out,
    g, x, xs, wg, wu, wd, act, wide, near, zbuf,
    routes, sel, back, row_prob, inverse, dr, drs, dpart, dbuf, dsum,
    own_sem, w_sem, zs_sem, xsend_sem, ysend_sem, recv_sem,
    rs_sem, rr_sem, px_sem, pr_sem, st_sem, sr_sem, ds_sem, dr_sem,
    xo_sem, ao_sem, ws_sem, wr_sem, ns_sem, nr_sem, ss_sem, sz_sem,
    qs_sem, qr_sem, far_sem, credit,
):
    place = Place()
    f32, bf16 = jnp.float32, jnp.bfloat16
    rows, width = tok_in.shape
    full = 2 * width
    half = rows // 2
    local, hid = wg.shape[:2]
    topk = 4
    me = place.device

    def start(copy):
        copy.start()
        return copy

    def remote(source, target, ssem, rsem, to):
        return start(
            pltpu.make_async_remote_copy(
                src_ref=source, dst_ref=target, send_sem=ssem, recv_sem=rsem,
                device_id=to, device_id_type=MESH,
            )
        )

    own = [
        start(pltpu.make_async_copy(ref, g.at[0, 0, a, :, place.columns(0, width)], own_sem.at[a]))
        for a, ref in enumerate((tok_in, grad_in))
    ]
    greet(place)
    sent = {}

    for dz in range(4):
        for dx in range(2):
            if dz or dx:
                j = dz * 2 + dx
                there = place.slot_there(dz) * 2 + dx
                sent["r", j] = remote(
                    routes_in, routes.at[there], rs_sem.at[j], rr_sem.at[there], place.far(dz, dx)
                )
    routes[0] = routes_in[...]
    for copy in own:
        copy.wait()

    def piece(h, dz, dx, dy):
        return g.at[dz, dx, :, pl.ds(h * half, half), place.columns(dy, width)]

    def by_z(h, to, slot, there, k):
        return start(
            pltpu.make_async_remote_copy(
                src_ref=piece(h, slot, 0, 0), dst_ref=piece(h, there, 0, 0),
                send_sem=zs_sem.at[h, k], recv_sem=recv_sem.at[h, there, 0, 0],
                device_id=to, device_id_type=MESH,
            )
        )

    inner = place.inner == 1

    def own_z():
        for h in range(2):
            sent["z", h, 0] = by_z(h, place.inward(), 0, 1 + place.inner, 0)

            @pl.when(inner)
            def _():
                by_z(h, place.outward(), 0, 1, 4)

    def pass_on(slot):
        @pl.when(inner)
        def _():
            for h in range(2):
                got(h, slot, 0, 0)
                if slot == 1:
                    by_z(h, place.inward(), 1, 3, 1)
                else:
                    by_z(h, place.outward(), slot, slot, slot)

    def passed_on(k):
        slot = k % 4

        @pl.when(inner)
        def _():
            for h in range(2):
                pltpu.make_async_copy(piece(h, slot, 0, 0), piece(h, slot, 0, 0), zs_sem.at[h, k]).wait()

    def by_x(h, dz, dy):
        sent["x", h, dz, dy] = remote(
            piece(h, dz, 0, dy), piece(h, dz, 1, dy), xsend_sem.at[h, dz, dy],
            recv_sem.at[h, dz, 1, dy], me(1),
        )

    def by_y(h, dz, dx):
        sent["y", h, dz, dx] = remote(
            piece(h, dz, dx, 0), piece(h, dz, dx, 0), ysend_sem.at[h, dz, dx],
            recv_sem.at[h, dz, dx, 1], me(0, 1),
        )

    def got(h, dz, dx, dy):
        arrive(piece(h, dz, dx, dy), recv_sem.at[h, dz, dx, dy])

    def column(dz):
        for h in range(2):
            if dz:
                @pl.when(jnp.logical_not(inner))
                def _():
                    got(h, dz, 0, 0)

            if h == 0:
                by_x(h, dz, 0)
                by_y(h, dz, 0)
            else:
                by_y(h, dz, 0)
                by_x(h, dz, 0)

    def plane(dz):
        got(0, dz, 1, 0)
        by_y(0, dz, 1)
        got(1, dz, 0, 1)
        by_x(1, dz, 1)

    def last(dz):
        got(0, dz, 0, 1)
        got(1, dz, 1, 0)
        got(0, dz, 1, 1)
        got(1, dz, 1, 1)

    experts = [
        (place.block(0, e // local) * local + e % local).astype(f32) for e in range(2 * local)
    ]

    def build(j):
        names = routes[j, :topk, :]
        probs = routes[j, topk:, :]
        before = (
            lax.broadcasted_iota(jnp.int32, (rows, rows), 0)
            < lax.broadcasted_iota(jnp.int32, (rows, rows), 1)
        ).astype(f32).astype(bf16)
        hits, prob = [], []
        for e in experts:
            chosen = names == e
            hits.append(jnp.max(jnp.where(chosen, 1.0, 0.0), axis=0, keepdims=True))
            prob.append(jnp.sum(jnp.where(chosen, probs, 0.0), axis=0, keepdims=True))
        hit = jnp.concatenate(hits + [jnp.zeros((4, rows), f32)], axis=0)
        spot = jnp.dot(hit.astype(bf16), before, preferred_element_type=f32)
        spot = jnp.where(hit > 0.0, spot, -1.0)
        number = lax.broadcasted_iota(jnp.int32, (CAP, rows), 0).astype(f32)
        ones, high, low, full_prob, inv = [], [], [], [], []
        for e in range(2 * local):
            filled = jnp.broadcast_to(spot[e : e + 1], (CAP, rows)) == number
            top = prob[e].astype(bf16).astype(f32)
            ones.append(jnp.where(filled, 1.0, 0.0))
            high.append(jnp.where(filled, top, 0.0))
            low.append(jnp.where(filled, prob[e] - top, 0.0))
            full_prob.append(jnp.where(filled, prob[e], 0.0))
            inv.append(jnp.where(hits[e] > 0.0, 1.0 / jnp.maximum(prob[e], 1e-30), 0.0))
        ones = jnp.concatenate(ones, axis=0)
        sel[j] = ones.astype(bf16)
        back[j, 0] = ones.T.astype(bf16)
        back[j, 1] = jnp.concatenate(high, axis=0).T.astype(bf16)
        back[j, 2] = jnp.concatenate(low, axis=0).T.astype(bf16)
        row_prob[j] = jnp.sum(jnp.concatenate(full_prob, axis=0), axis=1, keepdims=True)
        inverse[j] = jnp.concatenate(inv + [jnp.zeros((4, rows), f32)], axis=0)

    def build_all(first, end):
        for j in range(first, end):
            if j:
                arrive(routes.at[j], rr_sem.at[j])

        @pl.loop(first, end)
        def _(j):
            build(j)

    tile = 512

    def select(dz):
        @pl.loop(0, 2)
        def _(dx):
            j = dz * 2 + dx
            at = pl.ds(pl.multiple_of(dx * CAP, CAP), CAP)

            @pl.loop(0, full // tile)
            def _(n):
                cols = pl.ds(pl.multiple_of(n * tile, tile), tile)
                for a in range(2):
                    picked = jnp.dot(sel[j], g[dz, dx, a, :, cols], preferred_element_type=f32)
                    if a:
                        picked = picked * row_prob[j]
                    picked = picked.astype(bf16)
                    for l in range(local):
                        x[a, l, dz, at, cols] = picked[l * CAP : (l + 1) * CAP]
                        m = local + l
                        xs[a, l, dz, at, cols] = picked[m * CAP : (m + 1) * CAP]

        sent["p", dz] = remote(
            xs.at[:, :, dz], x.at[:, :, dz, pl.ds(half, half)], px_sem.at[dz], pr_sem.at[dz], me(0, 0, 1)
        )

    def packed(dz):
        arrive(x.at[:, :, dz, pl.ds(half, half)], pr_sem.at[dz])
        for a, ref in enumerate((x_out, c_out)):
            sent["xo", a, dz] = start(
                pltpu.make_async_copy(x.at[a, :, dz], ref.at[:, dz], xo_sem.at[a, dz])
            )

    nt = (((1,), (1,)), ((), ()))
    tiles = [(h, min(256, hid - h)) for h in range(0, hid, 256)]

    def forward(dz, l):
        if dz == 0:
            for i in range(3):
                loads[i, l].wait()
        total = jnp.zeros((rows, 1), f32)
        for h, n in tiles:
            at = pl.ds(h, n)
            gate = lax.dot_general(x[0, l, dz], wg[l, at, :], nt, preferred_element_type=f32)
            upper = lax.dot_general(x[0, l, dz], wu[l, at, :], nt, preferred_element_type=f32)
            d_hidden = lax.dot_general(x[1, l, dz], wd[l, at, :], nt, preferred_element_type=f32)
            sigma = jax.nn.sigmoid(gate)
            active = gate * sigma
            hidden = active * upper
            total = total + jnp.sum(hidden * d_hidden, axis=1, keepdims=True)
            act[0, l, dz, :, at] = hidden.astype(bf16)
            act[1, l, dz, :, at] = (d_hidden * upper * sigma * (1.0 + gate * (1.0 - sigma))).astype(bf16)
            act[2, l, dz, :, at] = (d_hidden * active).astype(bf16)
        total = jnp.broadcast_to(total, (rows, rows))
        for dx in range(2):
            dr[dz, dx, l * CAP : (l + 1) * CAP, :] = total[dx * CAP : (dx + 1) * CAP]
            drs[dz, dx, l * CAP : (l + 1) * CAP, :] = total[half + dx * CAP : half + (dx + 1) * CAP]

    def handed(dz):
        for i, ref in enumerate((hid_out, dg_out, du_out)):
            sent["ao", i, dz] = start(
                pltpu.make_async_copy(act.at[i, :, dz], ref.at[:, dz], ao_sem.at[i, dz])
            )
        sent["d", dz] = remote(
            drs.at[dz], dr.at[dz, :, pl.ds(half, half)], ds_sem.at[dz], dr_sem.at[dz], me(0, 0, 1)
        )
        sent.pop(("xo", 0, dz)).wait()
        sent.pop(("xo", 1, dz)).wait()
        pl.semaphore_signal(credit.at[dz], inc=1, device_id=me(0, 0, 1), device_id_type=MESH)
        sent.pop(("p", dz)).wait_send()

    def backward(dz, l):
        mine = pl.ds(l * CAP, CAP)

        @pl.loop(0, full // tile)
        def _(n):
            cols = pl.ds(pl.multiple_of(n * tile, tile), tile)
            out = jnp.dot(act[0, l, dz], wd[l, :, cols], preferred_element_type=f32)
            back_rows = jnp.dot(act[1, l, dz], wg[l, :, cols], preferred_element_type=f32)
            back_rows = back_rows + jnp.dot(act[2, l, dz], wu[l, :, cols], preferred_element_type=f32)
            for a, value in enumerate((out.astype(bf16), back_rows.astype(bf16))):
                for dx in range(2):
                    x[a, dx, dz, mine, cols] = value[dx * CAP : (dx + 1) * CAP]
                    xs[a, dx, dz, mine, cols] = value[half + dx * CAP : half + (dx + 1) * CAP]

    def returned(dz):
        pl.semaphore_wait(credit.at[dz], 1)
        sent["s", dz] = remote(
            xs.at[:, :, dz], x.at[:, :, dz, pl.ds(half, half)], st_sem.at[dz], sr_sem.at[dz], me(0, 0, 1)
        )

    def put_back(dz):
        for h in range(2):
            for key in (("x", h, dz, 0), ("y", h, dz, 0)):
                sent.pop(key).wait_send()
        sent.pop(("y", 0, dz, 1)).wait_send()
        sent.pop(("x", 1, dz, 1)).wait_send()
        if dz == 0:
            for h in range(2):
                sent.pop(("z", h, 0)).wait_send()
            passed_on(4)
        else:
            passed_on(dz)
        arrive(x.at[:, :, dz, pl.ds(half, half)], sr_sem.at[dz])
        arrive(dr.at[dz, :, pl.ds(half, half)], dr_sem.at[dz])

        @pl.loop(0, 2)
        def _(dx):
            j = dz * 2 + dx

            @pl.loop(0, full // tile)
            def _(n):
                cols = pl.ds(pl.multiple_of(n * tile, tile), tile)
                out = jnp.dot(back[j, 1], x[0, dx, dz, :, cols], preferred_element_type=f32)
                out = out + jnp.dot(back[j, 2], x[0, dx, dz, :, cols], preferred_element_type=f32)
                g[dz, dx, 0, :, cols] = out.astype(bf16)
                into = jnp.dot(back[j, 0], x[1, dx, dz, :, cols], preferred_element_type=f32)
                g[dz, dx, 1, :, cols] = into.astype(bf16)

            names = routes[j, :topk, :]
            weighted = dr[dz, dx] * sel[j].astype(f32)
            total = jnp.zeros((topk, rows), f32)
            for e, name in enumerate(experts):
                value = jnp.sum(weighted[e * CAP : (e + 1) * CAP], axis=0, keepdims=True)
                value = value * inverse[j, e : e + 1, :]
                total = total + jnp.where(names == name, value, 0.0)
            dpart[j] = jnp.concatenate([total, jnp.zeros((8 - topk, rows), f32)], axis=0)

        for dx in range(2):
            j = dz * 2 + dx
            if j:
                there = place.slot_there(dz) * 2 + dx
                sent["q", j] = remote(
                    dpart.at[j], dbuf.at[there], qs_sem.at[j], qr_sem.at[there], place.far(dz, dx)
                )

    def send_wide(dz):
        for h in range(2):
            across = me(0, 1) if h == 0 else me(1)
            for other in (1, 0):
                dx, dy = (other, 1) if h == 0 else (1, other)
                sent["w", h, dz, other] = remote(
                    piece(h, dz, dx, dy), wide.at[h, dz, other], ws_sem.at[h, dz, other],
                    wr_sem.at[h, dz, other], across,
                )

    def add(target, source):
        for a in range(2):
            @pl.loop(0, half // 16)
            def _(i):
                at = pl.ds(pl.multiple_of(i * 16, 16), 16)
                target[a, at, :] = target[a, at, :] + source[a, at, :]

    def send_near(dz):
        for other in (1, 0):
            for h in range(2):
                dx, dy = (other, 0) if h == 0 else (0, other)
                arrive(wide.at[h, dz, other], wr_sem.at[h, dz, other])
                add(wide.at[h, dz, other], piece(h, dz, dx, dy))
                if other:
                    along = me(1) if h == 0 else me(0, 1)
                    sent["n", h, dz] = remote(
                        wide.at[h, dz, 1], near.at[h, dz], ns_sem.at[h, dz], nr_sem.at[h, dz], along
                    )

    def send_z(dz):
        for h in range(2):
            arrive(near.at[h, dz], nr_sem.at[h, dz])
            add(near.at[h, dz], wide.at[h, dz, 0])
            if dz == 3:
                rows_there = pl.ds(h * half, half)
                sent["far", h] = start(
                    pltpu.make_async_copy(near.at[h, 3], far_out.at[:, rows_there], far_sem.at[h])
                )
            elif dz:
                there = place.slot_there(dz)
                sent["f", h, dz] = remote(
                    near.at[h, dz], zbuf.at[h, there - 1], ss_sem.at[h, dz], sz_sem.at[h, there],
                    place.far(dz),
                )

    own_z()
    column(0)
    loads = {}
    for l in range(local):
        for i, (ref, to) in enumerate(((wg_in, wg), (wu_in, wu), (wd_in, wd))):
            loads[i, l] = start(pltpu.make_async_copy(ref.at[l], to.at[l], w_sem.at[i, l]))
    build_all(0, 8)
    plane(0)
    pass_on(1)
    column(1)
    pass_on(2)
    last(0)
    select(0)
    for dz in range(4):
        if dz < 3:
            plane(dz + 1)
        if dz == 0:
            pass_on(3)
        packed(dz)
        forward(dz, 0)
        if dz < 2:
            column(dz + 2)
        if dz == 3:
            send_near(1)
        forward(dz, 1)
        handed(dz)
        backward(dz, 0)
        if dz == 3:
            send_near(2)
            send_z(1)
        backward(dz, 1)
        returned(dz)
        if dz < 3:
            last(dz + 1)
            select(dz + 1)
        put_back(dz)
        if dz:
            send_wide(dz)
    send_wide(0)
    send_z(2)
    send_near(3)
    send_z(3)

    total = dpart[0]
    for j in range(1, 8):
        arrive(dbuf.at[j], qr_sem.at[j])
        total = total + dbuf[j]
    dsum[0] = total
    peer = remote(dsum.at[0], dsum.at[1], qs_sem.at[0], qr_sem.at[0], me(0, 1))

    send_near(0)
    send_z(0)
    arrive(dsum.at[1], qr_sem.at[0])
    dprob_out[...] = dsum[0] + dsum[1]
    for h in range(2):
        arrive(zbuf.at[h, 0], sz_sem.at[h, 1])

    def finish(others):
        for a, ref in enumerate((layer_out, dtok_out)):
            for h in range(2):
                @pl.loop(0, half // 16)
                def _(i):
                    at = pl.ds(pl.multiple_of(i * 16, 16), 16)
                    total = near[h, 0, a, at, :].astype(f32)
                    for dz in others:
                        total = total + zbuf[h, dz - 1, a, at, :].astype(f32)
                    to = pl.ds(pl.multiple_of(h * half + i * 16, 16), 16)
                    ref[to, :] = total

    @pl.when(inner)
    def _():
        for dz in (2, 3):
            for h in range(2):
                arrive(zbuf.at[h, dz - 1], sz_sem.at[h, dz])
        finish((1, 2, 3))

    @pl.when(jnp.logical_not(inner))
    def _():
        finish((1,))

    peer.wait_send()
    for key, copy in sent.items():
        if key[0] in ("ao", "far"):
            copy.wait()
        else:
            copy.wait_send()


def layer(tokens, grad_out, routes, w_gate, w_up, w_down):
    rows, width = tokens.shape
    local, hid, full = w_gate.shape
    half = rows // 2
    bf16, f32 = jnp.bfloat16, jnp.float32
    any_space = pl.BlockSpec(memory_space=pl.ANY)
    vmem = pl.BlockSpec(memory_space=pltpu.VMEM)
    shape = jax.ShapeDtypeStruct
    packed = shape((local, 4, rows, full), bf16)
    acts = shape((local, 4, rows, hid), bf16)
    out = shape((rows, width), f32)
    far = shape((2, rows, width), bf16)
    dma = pltpu.SemaphoreType.DMA
    return pl.pallas_call(
        layer_kernel,
        out_shape=(packed, packed, acts, acts, acts, far, out, out, shape((8, rows), f32)),
        in_specs=[any_space, any_space, vmem, any_space, any_space, any_space],
        out_specs=[any_space] * 6 + [vmem] * 3,
        scratch_shapes=[
            pltpu.VMEM((4, 2, 2, rows, full), bf16),
            pltpu.VMEM((2, 2, 4, rows, full), bf16),
            pltpu.VMEM((2, 2, 4, half, full), bf16),
            pltpu.VMEM((local, hid, full), bf16),
            pltpu.VMEM((local, hid, full), bf16),
            pltpu.VMEM((local, hid, full), bf16),
            pltpu.VMEM((3, local, 4, rows, hid), bf16),
            pltpu.VMEM((2, 4, 2, 2, half, width), bf16),
            pltpu.VMEM((2, 4, 2, half, width), bf16),
            pltpu.VMEM((2, 3, 2, half, width), bf16),
            pltpu.VMEM((8, 8, rows), f32),
            pltpu.VMEM((8, rows, rows), bf16),
            pltpu.VMEM((8, 3, rows, rows), bf16),
            pltpu.VMEM((8, rows, 1), f32),
            pltpu.VMEM((8, 8, rows), f32),
            pltpu.VMEM((4, 2, rows, rows), f32),
            pltpu.VMEM((4, 2, half, rows), f32),
            pltpu.VMEM((8, 8, rows), f32),
            pltpu.VMEM((8, 8, rows), f32),
            pltpu.VMEM((2, 8, rows), f32),
            dma((2,)), dma((3, local)), dma((2, 5)), dma((2, 4, 2)), dma((2, 4, 2)), dma((2, 4, 2, 2)),
            dma((8,)), dma((8,)), dma((4,)), dma((4,)), dma((4,)), dma((4,)), dma((4,)), dma((4,)),
            dma((2, 4)), dma((3, 4)), dma((2, 4, 2)), dma((2, 4, 2)), dma((2, 4)), dma((2, 4)),
            dma((2, 4)), dma((2, 4)), dma((8,)), dma((8,)), dma((2,)),
            pltpu.SemaphoreType.REGULAR((4,)),
        ],
        compiler_params=pltpu.CompilerParams(
            collective_id=0, has_side_effects=True, vmem_limit_bytes=61 * 2**20
        ),
    )(tokens, grad_out, routes, w_gate, w_up, w_down)


def weight_kernel(hid, dg, du, x, c, wg_out, wu_out, wd_out, turned):
    @pl.when(pl.program_id(1) == 0)
    def _():
        for i, ref in enumerate((hid, dg, du)):
            turned[i] = ref[0].T

    for i, rows, out in ((1, x, wg_out), (2, x, wu_out), (0, c, wd_out)):
        out[0] = jnp.dot(turned[i], rows[0], preferred_element_type=jnp.float32)


def weights(hidden, d_gate, d_up, x, c):
    local, rows, hid = hidden.shape
    full = x.shape[2]
    tile = 512
    acts = pl.BlockSpec((1, rows, hid), lambda l, n: (l, 0, 0))
    ins = pl.BlockSpec((1, rows, tile), lambda l, n: (l, 0, n))
    out = pl.BlockSpec((1, hid, tile), lambda l, n: (l, 0, n))
    return pl.pallas_call(
        weight_kernel,
        grid=(local, full // tile),
        out_shape=[jax.ShapeDtypeStruct((local, hid, full), jnp.float32)] * 3,
        in_specs=[acts] * 3 + [ins] * 2,
        out_specs=[out] * 3,
        scratch_shapes=[pltpu.VMEM((3, hid, rows), jnp.bfloat16)],
        compiler_params=pltpu.CompilerParams(vmem_limit_bytes=60 * 2**20),
        cost_estimate=pl.CostEstimate(
            flops=6 * local * hid * rows * full, bytes_accessed=12 * local * hid * full, transcendentals=0
        ),
    )(hidden, d_gate, d_up, x, c)


def by_one_kernel(tokens, expert_ids, gate_probs, w_gate, w_up, w_down, grad_out):
    topk = expert_ids.shape[1]
    local, hid, full = w_gate.shape
    f32 = jnp.float32
    routes = jnp.concatenate([expert_ids.astype(f32).T, gate_probs.T], axis=0)
    x, c, hidden, d_gate, d_up, far, layer_out, d_tokens, d_prob = layer(
        tokens, grad_out, routes, w_gate, w_up, w_down
    )
    x, c = (v.reshape(local, -1, full) for v in (x, c))
    hidden, d_gate, d_up = (v.reshape(local, -1, hid) for v in (hidden, d_gate, d_up))

    ends = [(z * 4 + i, (3 - z) * 4 + i) for z in (0, 3) for i in range(4)]
    inners = [(z * 4 + i, (6 - 3 * z) * 4 + i) for z in (1, 2) for i in range(4)]
    far = [lax.ppermute(far, "fsdp", pairs) for pairs in (ends, inners)]
    d_w_gate, d_w_up, d_w_down = weights(hidden, d_gate, d_up, x, c)
    layer_out, d_tokens = (
        (own + far[0][a].astype(f32) + far[1][a].astype(f32)).astype(tokens.dtype)
        for a, own in enumerate((layer_out, d_tokens))
    )
    return (layer_out, d_tokens, d_prob[:topk].T, d_w_gate, d_w_up, d_w_down)


def gather_any(value):
    wide = lax.all_gather(value, "tok", axis=1, tiled=True)
    return lax.all_gather(wide, "fsdp", axis=0, tiled=False)


def scatter_any(value):
    blocks, rows, full = value.shape
    mine = lax.psum_scatter(
        value.reshape(blocks * rows, full), "fsdp", scatter_dimension=0, tiled=True
    )
    return lax.psum_scatter(mine, "tok", scatter_dimension=1, tiled=True)


def on_device(tokens, expert_ids, gate_probs, w_gate, w_up, w_down, grad_out):
    tok_rows, topk = expert_ids.shape
    local = w_gate.shape[0]
    f32 = jnp.float32
    me = lax.axis_index("fsdp")

    routes = jnp.concatenate([expert_ids.astype(f32).T, gate_probs.T], axis=0)
    routes = lax.all_gather(routes, "fsdp", axis=0, tiled=False)
    all_tokens, all_grads = gather_any(tokens), gather_any(grad_out)
    blocks = all_tokens.shape[0]

    names = routes[:, :topk]
    mine = (me * local + jnp.arange(local, dtype=jnp.int32)).astype(f32)
    chosen = names[None] == mine[:, None, None, None]
    hit = jnp.any(chosen, axis=2)
    prob = jnp.sum(jnp.where(chosen, routes[None, :, topk:], 0.0), axis=2)
    before = jnp.triu(jnp.ones((tok_rows, tok_rows), jnp.bfloat16), 1)
    place = jnp.einsum("ebs,st->ebt", hit.astype(jnp.bfloat16), before, preferred_element_type=f32)
    place = jnp.where(hit, place, -1.0)
    filled = place[:, :, None, :] == jnp.arange(CAP, dtype=jnp.int32).astype(f32)[None, None, :, None]
    select = filled.astype(jnp.bfloat16)
    row_prob = jnp.sum(jnp.where(filled, prob[:, :, None, :], 0.0), axis=3)
    row_prob = row_prob.reshape(local, blocks * CAP, 1)

    def pick(values):
        rows = jnp.einsum("ebrt,btd->ebrd", select, values, preferred_element_type=f32)
        return rows.astype(jnp.bfloat16).reshape(local, blocks * CAP, values.shape[-1])

    def place_back(rows):
        rows = rows.astype(jnp.bfloat16).reshape(local, blocks, CAP, rows.shape[-1])
        values = jnp.einsum("ebrt,ebrd->btd", select, rows, preferred_element_type=f32)
        return values.astype(jnp.bfloat16)

    inputs = pick(all_tokens)
    cotangent = pick(all_grads)
    gate = jnp.einsum("erd,ehd->erh", inputs, w_gate, preferred_element_type=f32)
    upper = jnp.einsum("erd,ehd->erh", inputs, w_up, preferred_element_type=f32)
    raw = jnp.einsum("erd,ehd->erh", cotangent, w_down, preferred_element_type=f32)
    sigma = jax.nn.sigmoid(gate)
    active = gate * sigma
    hidden = active * upper
    weighted = (row_prob * hidden).astype(jnp.bfloat16)
    d_hidden = row_prob * raw
    d_gate = (d_hidden * upper * sigma * (1.0 + gate * (1.0 - sigma))).astype(jnp.bfloat16)
    d_upper = (d_hidden * active).astype(jnp.bfloat16)
    d_rows = jnp.sum(hidden * raw, axis=2).reshape(local, blocks, CAP)

    out_rows = jnp.einsum("erh,ehd->erd", weighted, w_down, preferred_element_type=f32)
    in_rows = jnp.einsum("erh,ehd->erd", d_gate, w_gate, preferred_element_type=f32)
    in_rows = in_rows + jnp.einsum("erh,ehd->erd", d_upper, w_up, preferred_element_type=f32)
    part_out, part_in = place_back(out_rows), place_back(in_rows)
    layer_out, d_tokens = scatter_any(part_out), scatter_any(part_in)

    d_w_down = jnp.einsum("erh,erd->ehd", weighted, cotangent, preferred_element_type=f32)
    d_w_gate = jnp.einsum("erh,erd->ehd", d_gate, inputs, preferred_element_type=f32)
    d_w_up = jnp.einsum("erh,erd->ehd", d_upper, inputs, preferred_element_type=f32)

    d_prob = jnp.sum(jnp.where(filled, d_rows[:, :, :, None], 0.0), axis=2)
    d_prob = jnp.sum(jnp.where(chosen, d_prob[:, :, None, :], 0.0), axis=0)
    d_prob = d_prob.reshape(blocks, topk * tok_rows)
    d_prob = lax.all_to_all(d_prob, "fsdp", split_axis=0, concat_axis=0, tiled=True)
    d_prob = jnp.sum(d_prob, axis=0)
    size = lax.axis_size("tok")
    mine_only = d_prob
    for turn in range(1, size):
        pairs = [(i, (i + turn) % size) for i in range(size)]
        d_prob = d_prob + lax.ppermute(mine_only, "tok", pairs)
    d_gate_probs = d_prob.reshape(topk, tok_rows).T
    return (layer_out, d_tokens, d_gate_probs, d_w_gate, d_w_up, d_w_down)


def solution(mesh):
    by_kernel = mesh.shape["fsdp"] == 16 and mesh.shape["tok"] == 2
    return jax.shard_map(
        by_one_kernel if by_kernel else on_device,
        mesh=mesh,
        in_specs=(
            P("fsdp", "tok"),
            P("fsdp", None),
            P("fsdp", None),
            P("fsdp", "tok", None),
            P("fsdp", "tok", None),
            P("fsdp", "tok", None),
            P("fsdp", "tok"),
        ),
        out_specs=(
            P("fsdp", "tok"),
            P("fsdp", "tok"),
            P("fsdp", None),
            P("fsdp", "tok", None),
            P("fsdp", "tok", None),
            P("fsdp", "tok", None),
        ),
        check_vma=False,
    )
```

```python
import functools

import jax
import jax.numpy as jnp
from jax import lax
from jax.experimental import pallas as pl
from jax.experimental.pallas import tpu as pltpu
from jax.sharding import PartitionSpec as P

CAP = 32
MESH = pl.DeviceIdType.MESH


def flip(bit, change):
    return 1 - bit if change else bit


class Place:
    def __init__(self):
        f = lax.axis_index("fsdp")
        self.t = lax.axis_index("tok")
        self.core = f % 2
        self.x = (f // 2) % 2
        self.z0 = (f // 4) % 2
        self.z1 = f // 8

        self.inner = self.z0 + self.z1 - 2 * self.z0 * self.z1

    def index(self, z1, z0, dx, dc):
        return (z1 * 2 + z0) * 4 + flip(self.x, dx) * 2 + flip(self.core, dc)

    def block(self, dx=0, dc=0):
        return self.index(self.z1, self.z0, dx, dc)

    def far(self, slot, dx=0):
        if slot < 2:
            z1, z0 = self.z1, flip(self.z0, slot)
        else:
            turn = self.inner if slot == 2 else 1 - self.inner
            z1, z0 = 1 - self.z1, self.z0 + turn - 2 * self.z0 * turn
        return (self.index(z1, z0, dx, 0), self.t)

    def slot_there(self, slot):
        return slot if slot < 2 else 3 - self.inner

    def inward(self):
        z = self.inner * (2 - self.z1) + (1 - self.inner) * (1 + self.z1)
        return (z * 4 + self.x * 2 + self.core, self.t)

    def outward(self):
        return (3 * self.z1 * 4 + self.x * 2 + self.core, self.t)

    def device(self, dx=0, dy=0, dc=0):
        return (self.block(dx, dc), flip(self.t, dy))

    def columns(self, dy, width):
        return pl.ds(pl.multiple_of(flip(self.t, dy) * width, width), width)

    def partners(self):
        return (
            [self.far(slot) for slot in (1, 2, 3)]
            + [self.far(slot, 1) for slot in range(4)]
            + [self.device(dy=1), self.device(dc=1)]
        )


def greet(place):
    barrier = pltpu.get_barrier_semaphore()
    partners = place.partners()
    for partner in partners:
        pl.semaphore_signal(barrier, inc=1, device_id=partner, device_id_type=MESH)
    pl.semaphore_wait(barrier, len(partners))


def arrive(ref, sem):
    pltpu.make_async_copy(ref, ref, sem).wait()


def layer_kernel(
    tok_in, grad_in, routes_in, wg_in, wu_in, wd_in,
    x_out, c_out, hid_out, dg_out, du_out, far_out, give0, give1, keep0, keep1, layer_out, dtok_out, dprob_out,
    g, x, xs, wg, wu, wd, act, wide, near, zbuf,
    routes, sel, back, row_prob, inverse, dr, drs, dpart, dbuf, dsum,
    own_sem, w_sem, zs_sem, xsend_sem, ysend_sem, recv_sem,
    rs_sem, rr_sem, px_sem, pr_sem, st_sem, sr_sem, ds_sem, dr_sem,
    xo_sem, ao_sem, ws_sem, wr_sem, ns_sem, nr_sem, ss_sem, sz_sem,
    qs_sem, qr_sem, far_sem, own_out_sem, credit,
):
    place = Place()
    f32, bf16 = jnp.float32, jnp.bfloat16
    rows, width = tok_in.shape
    full = 2 * width
    half = rows // 2
    local, hid = wg.shape[:2]
    topk = 4
    me = place.device

    def start(copy):
        copy.start()
        return copy

    def remote(source, target, ssem, rsem, to):
        return start(
            pltpu.make_async_remote_copy(
                src_ref=source, dst_ref=target, send_sem=ssem, recv_sem=rsem,
                device_id=to, device_id_type=MESH,
            )
        )

    own = [
        start(pltpu.make_async_copy(ref, g.at[0, 0, a, :, place.columns(0, width)], own_sem.at[a]))
        for a, ref in enumerate((tok_in, grad_in))
    ]
    greet(place)
    sent = {}

    for dz in range(4):
        for dx in range(2):
            if dz or dx:
                j = dz * 2 + dx
                there = place.slot_there(dz) * 2 + dx
                sent["r", j] = remote(
                    routes_in, routes.at[there], rs_sem.at[j], rr_sem.at[there], place.far(dz, dx)
                )
    routes[0] = routes_in[...]
    for copy in own:
        copy.wait()

    def piece(h, dz, dx, dy):
        return g.at[dz, dx, :, pl.ds(h * half, half), place.columns(dy, width)]

    def by_z(h, to, slot, there, k):
        return start(
            pltpu.make_async_remote_copy(
                src_ref=piece(h, slot, 0, 0), dst_ref=piece(h, there, 0, 0),
                send_sem=zs_sem.at[h, k], recv_sem=recv_sem.at[h, there, 0, 0],
                device_id=to, device_id_type=MESH,
            )
        )

    inner = place.inner == 1

    def own_z():
        for h in range(2):
            sent["z", h, 0] = by_z(h, place.inward(), 0, 1 + place.inner, 0)

            @pl.when(inner)
            def _():
                by_z(h, place.outward(), 0, 1, 4)

    def pass_on(slot):
        @pl.when(inner)
        def _():
            for h in range(2):
                got(h, slot, 0, 0)
                if slot == 1:
                    by_z(h, place.inward(), 1, 3, 1)
                else:
                    by_z(h, place.outward(), slot, slot, slot)

    def passed_on(k):
        slot = k % 4

        @pl.when(inner)
        def _():
            for h in range(2):
                pltpu.make_async_copy(piece(h, slot, 0, 0), piece(h, slot, 0, 0), zs_sem.at[h, k]).wait()

    def by_x(h, dz, dy):
        sent["x", h, dz, dy] = remote(
            piece(h, dz, 0, dy), piece(h, dz, 1, dy), xsend_sem.at[h, dz, dy],
            recv_sem.at[h, dz, 1, dy], me(1),
        )

    def by_y(h, dz, dx):
        sent["y", h, dz, dx] = remote(
            piece(h, dz, dx, 0), piece(h, dz, dx, 0), ysend_sem.at[h, dz, dx],
            recv_sem.at[h, dz, dx, 1], me(0, 1),
        )

    def got(h, dz, dx, dy):
        arrive(piece(h, dz, dx, dy), recv_sem.at[h, dz, dx, dy])

    def column(dz):
        for h in range(2):
            if dz:
                @pl.when(jnp.logical_not(inner))
                def _():
                    got(h, dz, 0, 0)

            if h == 0:
                by_x(h, dz, 0)
                by_y(h, dz, 0)
            else:
                by_y(h, dz, 0)
                by_x(h, dz, 0)

    def plane(dz):
        got(0, dz, 1, 0)
        by_y(0, dz, 1)
        got(1, dz, 0, 1)
        by_x(1, dz, 1)

    def last(dz):
        got(0, dz, 0, 1)
        got(1, dz, 1, 0)
        got(0, dz, 1, 1)
        got(1, dz, 1, 1)

    experts = [
        (place.block(0, e // local) * local + e % local).astype(f32) for e in range(2 * local)
    ]

    def build(j):
        names = routes[j, :topk, :]
        probs = routes[j, topk:, :]
        before = (
            lax.broadcasted_iota(jnp.int32, (rows, rows), 0)
            < lax.broadcasted_iota(jnp.int32, (rows, rows), 1)
        ).astype(f32).astype(bf16)
        hits, prob = [], []
        for e in experts:
            chosen = names == e
            hits.append(jnp.max(jnp.where(chosen, 1.0, 0.0), axis=0, keepdims=True))
            prob.append(jnp.sum(jnp.where(chosen, probs, 0.0), axis=0, keepdims=True))
        hit = jnp.concatenate(hits + [jnp.zeros((4, rows), f32)], axis=0)
        spot = jnp.dot(hit.astype(bf16), before, preferred_element_type=f32)
        spot = jnp.where(hit > 0.0, spot, -1.0)
        number = lax.broadcasted_iota(jnp.int32, (CAP, rows), 0).astype(f32)
        ones, high, low, full_prob, inv = [], [], [], [], []
        for e in range(2 * local):
            filled = jnp.broadcast_to(spot[e : e + 1], (CAP, rows)) == number
            top = prob[e].astype(bf16).astype(f32)
            ones.append(jnp.where(filled, 1.0, 0.0))
            high.append(jnp.where(filled, top, 0.0))
            low.append(jnp.where(filled, prob[e] - top, 0.0))
            full_prob.append(jnp.where(filled, prob[e], 0.0))
            inv.append(jnp.where(hits[e] > 0.0, 1.0 / jnp.maximum(prob[e], 1e-30), 0.0))
        ones = jnp.concatenate(ones, axis=0)
        sel[j] = ones.astype(bf16)
        back[j, 0] = ones.T.astype(bf16)
        back[j, 1] = jnp.concatenate(high, axis=0).T.astype(bf16)
        back[j, 2] = jnp.concatenate(low, axis=0).T.astype(bf16)
        row_prob[j] = jnp.sum(jnp.concatenate(full_prob, axis=0), axis=1, keepdims=True)
        inverse[j] = jnp.concatenate(inv + [jnp.zeros((4, rows), f32)], axis=0)

    def build_all(first, end):
        for j in range(first, end):
            if j:
                arrive(routes.at[j], rr_sem.at[j])

        @pl.loop(first, end)
        def _(j):
            build(j)

    tile = 512

    def select(dz):
        @pl.loop(0, 2)
        def _(dx):
            j = dz * 2 + dx
            at = pl.ds(pl.multiple_of(dx * CAP, CAP), CAP)

            @pl.loop(0, full // tile)
            def _(n):
                cols = pl.ds(pl.multiple_of(n * tile, tile), tile)
                for a in range(2):
                    picked = jnp.dot(sel[j], g[dz, dx, a, :, cols], preferred_element_type=f32)
                    if a:
                        picked = picked * row_prob[j]
                    picked = picked.astype(bf16)
                    for l in range(local):
                        x[a, l, dz, at, cols] = picked[l * CAP : (l + 1) * CAP]
                        m = local + l
                        xs[a, l, dz, at, cols] = picked[m * CAP : (m + 1) * CAP]

        sent["p", dz] = remote(
            xs.at[:, :, dz], x.at[:, :, dz, pl.ds(half, half)], px_sem.at[dz], pr_sem.at[dz], me(0, 0, 1)
        )

    def packed(dz):
        arrive(x.at[:, :, dz, pl.ds(half, half)], pr_sem.at[dz])
        for a, ref in enumerate((x_out, c_out)):
            sent["xo", a, dz] = start(
                pltpu.make_async_copy(x.at[a, :, dz], ref.at[:, dz], xo_sem.at[a, dz])
            )

    nt = (((1,), (1,)), ((), ()))
    tiles = [(h, min(256, hid - h)) for h in range(0, hid, 256)]

    def forward(dz, l):
        if dz == 0:
            for i in range(3):
                loads[i, l].wait()
        total = jnp.zeros((rows, 1), f32)
        for h, n in tiles:
            at = pl.ds(h, n)
            gate = lax.dot_general(x[0, l, dz], wg[l, at, :], nt, preferred_element_type=f32)
            upper = lax.dot_general(x[0, l, dz], wu[l, at, :], nt, preferred_element_type=f32)
            d_hidden = lax.dot_general(x[1, l, dz], wd[l, at, :], nt, preferred_element_type=f32)
            sigma = jax.nn.sigmoid(gate)
            active = gate * sigma
            hidden = active * upper
            total = total + jnp.sum(hidden * d_hidden, axis=1, keepdims=True)
            act[0, l, dz, :, at] = hidden.astype(bf16)
            act[1, l, dz, :, at] = (d_hidden * upper * sigma * (1.0 + gate * (1.0 - sigma))).astype(bf16)
            act[2, l, dz, :, at] = (d_hidden * active).astype(bf16)
        total = jnp.broadcast_to(total, (rows, rows))
        for dx in range(2):
            dr[dz, dx, l * CAP : (l + 1) * CAP, :] = total[dx * CAP : (dx + 1) * CAP]
            drs[dz, dx, l * CAP : (l + 1) * CAP, :] = total[half + dx * CAP : half + (dx + 1) * CAP]

    def handed(dz):
        for i, ref in enumerate((hid_out, dg_out, du_out)):
            sent["ao", i, dz] = start(
                pltpu.make_async_copy(act.at[i, :, dz], ref.at[:, dz], ao_sem.at[i, dz])
            )
        sent["d", dz] = remote(
            drs.at[dz], dr.at[dz, :, pl.ds(half, half)], ds_sem.at[dz], dr_sem.at[dz], me(0, 0, 1)
        )
        sent.pop(("xo", 0, dz)).wait()
        sent.pop(("xo", 1, dz)).wait()
        pl.semaphore_signal(credit.at[dz], inc=1, device_id=me(0, 0, 1), device_id_type=MESH)
        sent.pop(("p", dz)).wait_send()

    def backward(dz, l):
        mine = pl.ds(l * CAP, CAP)

        @pl.loop(0, full // tile)
        def _(n):
            cols = pl.ds(pl.multiple_of(n * tile, tile), tile)
            out = jnp.dot(act[0, l, dz], wd[l, :, cols], preferred_element_type=f32)
            back_rows = jnp.dot(act[1, l, dz], wg[l, :, cols], preferred_element_type=f32)
            back_rows = back_rows + jnp.dot(act[2, l, dz], wu[l, :, cols], preferred_element_type=f32)
            for a, value in enumerate((out.astype(bf16), back_rows.astype(bf16))):
                for dx in range(2):
                    x[a, dx, dz, mine, cols] = value[dx * CAP : (dx + 1) * CAP]
                    xs[a, dx, dz, mine, cols] = value[half + dx * CAP : half + (dx + 1) * CAP]

    def returned(dz):
        pl.semaphore_wait(credit.at[dz], 1)
        sent["s", dz] = remote(
            xs.at[:, :, dz], x.at[:, :, dz, pl.ds(half, half)], st_sem.at[dz], sr_sem.at[dz], me(0, 0, 1)
        )

    def put_back(dz):
        for h in range(2):
            for key in (("x", h, dz, 0), ("y", h, dz, 0)):
                sent.pop(key).wait_send()
        sent.pop(("y", 0, dz, 1)).wait_send()
        sent.pop(("x", 1, dz, 1)).wait_send()
        if dz == 0:
            for h in range(2):
                sent.pop(("z", h, 0)).wait_send()
            passed_on(4)
        else:
            passed_on(dz)
        arrive(x.at[:, :, dz, pl.ds(half, half)], sr_sem.at[dz])
        arrive(dr.at[dz, :, pl.ds(half, half)], dr_sem.at[dz])

        @pl.loop(0, 2)
        def _(dx):
            j = dz * 2 + dx

            @pl.loop(0, full // tile)
            def _(n):
                cols = pl.ds(pl.multiple_of(n * tile, tile), tile)
                out = jnp.dot(back[j, 1], x[0, dx, dz, :, cols], preferred_element_type=f32)
                out = out + jnp.dot(back[j, 2], x[0, dx, dz, :, cols], preferred_element_type=f32)
                g[dz, dx, 0, :, cols] = out.astype(bf16)
                into = jnp.dot(back[j, 0], x[1, dx, dz, :, cols], preferred_element_type=f32)
                g[dz, dx, 1, :, cols] = into.astype(bf16)

            names = routes[j, :topk, :]
            weighted = dr[dz, dx] * sel[j].astype(f32)
            total = jnp.zeros((topk, rows), f32)
            for e, name in enumerate(experts):
                value = jnp.sum(weighted[e * CAP : (e + 1) * CAP], axis=0, keepdims=True)
                value = value * inverse[j, e : e + 1, :]
                total = total + jnp.where(names == name, value, 0.0)
            dpart[j] = jnp.concatenate([total, jnp.zeros((8 - topk, rows), f32)], axis=0)

        for dx in range(2):
            j = dz * 2 + dx
            if j:
                there = place.slot_there(dz) * 2 + dx
                sent["q", j] = remote(
                    dpart.at[j], dbuf.at[there], qs_sem.at[j], qr_sem.at[there], place.far(dz, dx)
                )

    def send_wide(dz):
        for h in range(2):
            across = me(0, 1) if h == 0 else me(1)
            for other in (1, 0):
                dx, dy = (other, 1) if h == 0 else (1, other)
                sent["w", h, dz, other] = remote(
                    piece(h, dz, dx, dy), wide.at[h, dz, other], ws_sem.at[h, dz, other],
                    wr_sem.at[h, dz, other], across,
                )

    def add(target, source):
        for a in range(2):
            @pl.loop(0, half // 16)
            def _(i):
                at = pl.ds(pl.multiple_of(i * 16, 16), 16)
                target[a, at, :] = target[a, at, :] + source[a, at, :]

    def send_near(dz):
        for other in (1, 0):
            for h in range(2):
                dx, dy = (other, 0) if h == 0 else (0, other)
                arrive(wide.at[h, dz, other], wr_sem.at[h, dz, other])
                add(wide.at[h, dz, other], piece(h, dz, dx, dy))
                if other:
                    along = me(1) if h == 0 else me(0, 1)
                    sent["n", h, dz] = remote(
                        wide.at[h, dz, 1], near.at[h, dz], ns_sem.at[h, dz], nr_sem.at[h, dz], along
                    )

    def send_z(dz):
        for h in range(2):
            arrive(near.at[h, dz], nr_sem.at[h, dz])
            add(near.at[h, dz], wide.at[h, dz, 0])
            if dz == 3:
                rows_there = pl.ds(h * half, half)
                sent["far", h] = start(
                    pltpu.make_async_copy(near.at[h, 3], far_out.at[:, rows_there], far_sem.at[h])
                )
            elif dz:
                there = place.slot_there(dz)
                sent["f", h, dz] = remote(
                    near.at[h, dz], zbuf.at[h, there - 1], ss_sem.at[h, dz], sz_sem.at[h, there],
                    place.far(dz),
                )

    def leave_own():
        gives, keeps = (give0, give1), (keep0, keep1)
        for h in range(2):
            for far, refs in ((1, gives), (0, keeps)):
                for other in range(2):
                    dx, dy = (other, far) if h == 0 else (far, other)
                    sent["own", h, far, other] = start(
                        pltpu.make_async_copy(
                            piece(h, 0, dx, dy), refs[h].at[other], own_out_sem.at[h, far, other]
                        )
                    )

    own_z()
    column(0)
    loads = {}
    for l in range(local):
        for i, (ref, to) in enumerate(((wg_in, wg), (wu_in, wu), (wd_in, wd))):
            loads[i, l] = start(pltpu.make_async_copy(ref.at[l], to.at[l], w_sem.at[i, l]))
    build_all(0, 8)
    plane(0)
    pass_on(1)
    column(1)
    pass_on(2)
    last(0)
    select(0)
    for dz in range(4):
        if dz < 3:
            plane(dz + 1)
        if dz == 0:
            pass_on(3)
        packed(dz)
        forward(dz, 0)
        if dz < 2:
            column(dz + 2)
        if dz == 3:
            send_near(1)
        forward(dz, 1)
        handed(dz)
        backward(dz, 0)
        if dz == 3:
            send_near(2)
            send_z(1)
        backward(dz, 1)
        returned(dz)
        if dz < 3:
            last(dz + 1)
            select(dz + 1)
        put_back(dz)
        if dz:
            send_wide(dz)
        else:
            leave_own()
    send_z(2)
    send_near(3)
    send_z(3)

    total = dpart[0]
    for j in range(1, 8):
        arrive(dbuf.at[j], qr_sem.at[j])
        total = total + dbuf[j]
    dsum[0] = total
    peer = remote(dsum.at[0], dsum.at[1], qs_sem.at[0], qr_sem.at[0], me(0, 1))

    arrive(dsum.at[1], qr_sem.at[0])
    dprob_out[...] = dsum[0] + dsum[1]
    for h in range(2):
        arrive(zbuf.at[h, 0], sz_sem.at[h, 1])

    def finish(others):
        for a, ref in enumerate((layer_out, dtok_out)):
            for h in range(2):
                @pl.loop(0, half // 16)
                def _(i):
                    at = pl.ds(pl.multiple_of(i * 16, 16), 16)
                    total = zbuf[h, 0, a, at, :].astype(f32)
                    for dz in others:
                        total = total + zbuf[h, dz - 1, a, at, :].astype(f32)
                    to = pl.ds(pl.multiple_of(h * half + i * 16, 16), 16)
                    ref[to, :] = total

    @pl.when(inner)
    def _():
        for dz in (2, 3):
            for h in range(2):
                arrive(zbuf.at[h, dz - 1], sz_sem.at[h, dz])
        finish((2, 3))

    @pl.when(jnp.logical_not(inner))
    def _():
        finish(())

    peer.wait_send()
    for key, copy in sent.items():
        if key[0] in ("ao", "far", "own"):
            copy.wait()
        else:
            copy.wait_send()


def layer(tokens, grad_out, routes, w_gate, w_up, w_down):
    rows, width = tokens.shape
    local, hid, full = w_gate.shape
    half = rows // 2
    bf16, f32 = jnp.bfloat16, jnp.float32
    any_space = pl.BlockSpec(memory_space=pl.ANY)
    vmem = pl.BlockSpec(memory_space=pltpu.VMEM)
    shape = jax.ShapeDtypeStruct
    packed = shape((local, 4, rows, full), bf16)
    acts = shape((local, 4, rows, hid), bf16)
    out = shape((rows, width), f32)
    far = shape((2, rows, width), bf16)
    quarter = shape((2, 2, half, width), bf16)
    dma = pltpu.SemaphoreType.DMA
    return pl.pallas_call(
        layer_kernel,
        out_shape=(packed, packed, acts, acts, acts, far) + (quarter,) * 4 + (out, out, shape((8, rows), f32)),
        in_specs=[any_space, any_space, vmem, any_space, any_space, any_space],
        out_specs=[any_space] * 10 + [vmem] * 3,
        scratch_shapes=[
            pltpu.VMEM((4, 2, 2, rows, full), bf16),
            pltpu.VMEM((2, 2, 4, rows, full), bf16),
            pltpu.VMEM((2, 2, 4, half, full), bf16),
            pltpu.VMEM((local, hid, full), bf16),
            pltpu.VMEM((local, hid, full), bf16),
            pltpu.VMEM((local, hid, full), bf16),
            pltpu.VMEM((3, local, 4, rows, hid), bf16),
            pltpu.VMEM((2, 4, 2, 2, half, width), bf16),
            pltpu.VMEM((2, 4, 2, half, width), bf16),
            pltpu.VMEM((2, 3, 2, half, width), bf16),
            pltpu.VMEM((8, 8, rows), f32),
            pltpu.VMEM((8, rows, rows), bf16),
            pltpu.VMEM((8, 3, rows, rows), bf16),
            pltpu.VMEM((8, rows, 1), f32),
            pltpu.VMEM((8, 8, rows), f32),
            pltpu.VMEM((4, 2, rows, rows), f32),
            pltpu.VMEM((4, 2, half, rows), f32),
            pltpu.VMEM((8, 8, rows), f32),
            pltpu.VMEM((8, 8, rows), f32),
            pltpu.VMEM((2, 8, rows), f32),
            dma((2,)), dma((3, local)), dma((2, 5)), dma((2, 4, 2)), dma((2, 4, 2)), dma((2, 4, 2, 2)),
            dma((8,)), dma((8,)), dma((4,)), dma((4,)), dma((4,)), dma((4,)), dma((4,)), dma((4,)),
            dma((2, 4)), dma((3, 4)), dma((2, 4, 2)), dma((2, 4, 2)), dma((2, 4)), dma((2, 4)),
            dma((2, 4)), dma((2, 4)), dma((8,)), dma((8,)), dma((2,)), dma((2, 2, 2)),
            pltpu.SemaphoreType.REGULAR((4,)),
        ],
        compiler_params=pltpu.CompilerParams(
            collective_id=0, has_side_effects=True, vmem_limit_bytes=61 * 2**20
        ),
    )(tokens, grad_out, routes, w_gate, w_up, w_down)


def weight_kernel(count, *refs):
    acts, rows, outs, turned = refs[:count], refs[count], refs[count + 1 : -1], refs[-1]

    @pl.when(pl.program_id(1) == 0)
    def _():
        for i, ref in enumerate(acts):
            turned[i] = ref[0].T

    for i, out in enumerate(outs):
        out[0] = jnp.dot(turned[i], rows[0], preferred_element_type=jnp.float32)


def weights(acts, values):
    local, rows, hid = acts[0].shape
    full = values.shape[2]
    count, tile = len(acts), 512
    of_act = pl.BlockSpec((1, rows, hid), lambda l, n: (l, 0, 0))
    of_rows = pl.BlockSpec((1, rows, tile), lambda l, n: (l, 0, n))
    out = pl.BlockSpec((1, hid, tile), lambda l, n: (l, 0, n))
    return pl.pallas_call(
        functools.partial(weight_kernel, count),
        grid=(local, full // tile),
        out_shape=[jax.ShapeDtypeStruct((local, hid, full), jnp.float32)] * count,
        in_specs=[of_act] * count + [of_rows],
        out_specs=[out] * count,
        scratch_shapes=[pltpu.VMEM((count, hid, rows), jnp.bfloat16)],
        compiler_params=pltpu.CompilerParams(vmem_limit_bytes=60 * 2**20),
        cost_estimate=pl.CostEstimate(
            flops=2 * count * local * hid * rows * full,
            bytes_accessed=5 * count * local * hid * full,
            transcendentals=0,
        ),
    )(*acts, values)


def by_one_kernel(tokens, expert_ids, gate_probs, w_gate, w_up, w_down, grad_out):
    topk = expert_ids.shape[1]
    local, hid, full = w_gate.shape
    f32 = jnp.float32
    routes = jnp.concatenate([expert_ids.astype(f32).T, gate_probs.T], axis=0)
    x, c, hidden, d_gate, d_up, far, *own, part_out, part_in, d_prob = layer(
        tokens, grad_out, routes, w_gate, w_up, w_down
    )
    x, c = (v.reshape(local, -1, full) for v in (x, c))
    hidden, d_gate, d_up = (v.reshape(local, -1, hid) for v in (hidden, d_gate, d_up))

    blocks = lax.axis_size("fsdp")
    by_y = functools.partial(lax.ppermute, axis_name="tok", perm=[(0, 1), (1, 0)])
    by_x = functools.partial(
        lax.ppermute, axis_name="fsdp", perm=[(i, i + 2 - i // 2 % 2 * 4) for i in range(blocks)]
    )
    give0, give1, keep0, keep1 = own
    near0, near1 = by_y(give0), by_x(give1)
    ends = [(z * 4 + i, (3 - z) * 4 + i) for z in (0, 3) for i in range(4)]
    inners = [(z * 4 + i, (6 - 3 * z) * 4 + i) for z in (1, 2) for i in range(4)]
    far = [lax.ppermute(far, "fsdp", pairs) for pairs in (ends, inners)]
    d_w_gate, d_w_up = weights((d_gate, d_up), x)
    sum0, sum1 = near0 + keep0, near1 + keep1
    sum0, sum1, hidden = lax.optimization_barrier((sum0, sum1, hidden))
    near0, near1 = by_x(sum0[1]), by_y(sum1[1])
    (d_w_down,) = weights((hidden,), c)

    def total(a, part):
        halves = [near[a].astype(f32) + held[0, a].astype(f32) for near, held in ((near0, sum0), (near1, sum1))]
        value = part + jnp.concatenate(halves, axis=0) + far[0][a].astype(f32) + far[1][a].astype(f32)
        return value.astype(tokens.dtype)

    layer_out, d_tokens = total(0, part_out), total(1, part_in)
    return (layer_out, d_tokens, d_prob[:topk].T, d_w_gate, d_w_up, d_w_down)


def gather_any(value):
    wide = lax.all_gather(value, "tok", axis=1, tiled=True)
    return lax.all_gather(wide, "fsdp", axis=0, tiled=False)


def scatter_any(value):
    blocks, rows, full = value.shape
    mine = lax.psum_scatter(
        value.reshape(blocks * rows, full), "fsdp", scatter_dimension=0, tiled=True
    )
    return lax.psum_scatter(mine, "tok", scatter_dimension=1, tiled=True)


def on_device(tokens, expert_ids, gate_probs, w_gate, w_up, w_down, grad_out):
    tok_rows, topk = expert_ids.shape
    local = w_gate.shape[0]
    f32 = jnp.float32
    me = lax.axis_index("fsdp")

    routes = jnp.concatenate([expert_ids.astype(f32).T, gate_probs.T], axis=0)
    routes = lax.all_gather(routes, "fsdp", axis=0, tiled=False)
    all_tokens, all_grads = gather_any(tokens), gather_any(grad_out)
    blocks = all_tokens.shape[0]

    names = routes[:, :topk]
    mine = (me * local + jnp.arange(local, dtype=jnp.int32)).astype(f32)
    chosen = names[None] == mine[:, None, None, None]
    hit = jnp.any(chosen, axis=2)
    prob = jnp.sum(jnp.where(chosen, routes[None, :, topk:], 0.0), axis=2)
    before = jnp.triu(jnp.ones((tok_rows, tok_rows), jnp.bfloat16), 1)
    place = jnp.einsum("ebs,st->ebt", hit.astype(jnp.bfloat16), before, preferred_element_type=f32)
    place = jnp.where(hit, place, -1.0)
    filled = place[:, :, None, :] == jnp.arange(CAP, dtype=jnp.int32).astype(f32)[None, None, :, None]
    select = filled.astype(jnp.bfloat16)
    row_prob = jnp.sum(jnp.where(filled, prob[:, :, None, :], 0.0), axis=3)
    row_prob = row_prob.reshape(local, blocks * CAP, 1)

    def pick(values):
        rows = jnp.einsum("ebrt,btd->ebrd", select, values, preferred_element_type=f32)
        return rows.astype(jnp.bfloat16).reshape(local, blocks * CAP, values.shape[-1])

    def place_back(rows):
        rows = rows.astype(jnp.bfloat16).reshape(local, blocks, CAP, rows.shape[-1])
        values = jnp.einsum("ebrt,ebrd->btd", select, rows, preferred_element_type=f32)
        return values.astype(jnp.bfloat16)

    inputs = pick(all_tokens)
    cotangent = pick(all_grads)
    gate = jnp.einsum("erd,ehd->erh", inputs, w_gate, preferred_element_type=f32)
    upper = jnp.einsum("erd,ehd->erh", inputs, w_up, preferred_element_type=f32)
    raw = jnp.einsum("erd,ehd->erh", cotangent, w_down, preferred_element_type=f32)
    sigma = jax.nn.sigmoid(gate)
    active = gate * sigma
    hidden = active * upper
    weighted = (row_prob * hidden).astype(jnp.bfloat16)
    d_hidden = row_prob * raw
    d_gate = (d_hidden * upper * sigma * (1.0 + gate * (1.0 - sigma))).astype(jnp.bfloat16)
    d_upper = (d_hidden * active).astype(jnp.bfloat16)
    d_rows = jnp.sum(hidden * raw, axis=2).reshape(local, blocks, CAP)

    out_rows = jnp.einsum("erh,ehd->erd", weighted, w_down, preferred_element_type=f32)
    in_rows = jnp.einsum("erh,ehd->erd", d_gate, w_gate, preferred_element_type=f32)
    in_rows = in_rows + jnp.einsum("erh,ehd->erd", d_upper, w_up, preferred_element_type=f32)
    part_out, part_in = place_back(out_rows), place_back(in_rows)
    layer_out, d_tokens = scatter_any(part_out), scatter_any(part_in)

    d_w_down = jnp.einsum("erh,erd->ehd", weighted, cotangent, preferred_element_type=f32)
    d_w_gate = jnp.einsum("erh,erd->ehd", d_gate, inputs, preferred_element_type=f32)
    d_w_up = jnp.einsum("erh,erd->ehd", d_upper, inputs, preferred_element_type=f32)

    d_prob = jnp.sum(jnp.where(filled, d_rows[:, :, :, None], 0.0), axis=2)
    d_prob = jnp.sum(jnp.where(chosen, d_prob[:, :, None, :], 0.0), axis=0)
    d_prob = d_prob.reshape(blocks, topk * tok_rows)
    d_prob = lax.all_to_all(d_prob, "fsdp", split_axis=0, concat_axis=0, tiled=True)
    d_prob = jnp.sum(d_prob, axis=0)
    size = lax.axis_size("tok")
    mine_only = d_prob
    for turn in range(1, size):
        pairs = [(i, (i + turn) % size) for i in range(size)]
        d_prob = d_prob + lax.ppermute(mine_only, "tok", pairs)
    d_gate_probs = d_prob.reshape(topk, tok_rows).T
    return (layer_out, d_tokens, d_gate_probs, d_w_gate, d_w_up, d_w_down)


def solution(mesh):
    by_kernel = mesh.shape["fsdp"] == 16 and mesh.shape["tok"] == 2
    return jax.shard_map(
        by_one_kernel if by_kernel else on_device,
        mesh=mesh,
        in_specs=(
            P("fsdp", "tok"),
            P("fsdp", None),
            P("fsdp", None),
            P("fsdp", "tok", None),
            P("fsdp", "tok", None),
            P("fsdp", "tok", None),
            P("fsdp", "tok"),
        ),
        out_specs=(
            P("fsdp", "tok"),
            P("fsdp", "tok"),
            P("fsdp", None),
            P("fsdp", "tok", None),
            P("fsdp", "tok", None),
            P("fsdp", "tok", None),
        ),
        check_vma=False,
    )
```

```python
import functools

import jax
import jax.numpy as jnp
from jax import lax
from jax.experimental import pallas as pl
from jax.experimental.pallas import tpu as pltpu
from jax.sharding import PartitionSpec as P

CAP = 32
MESH = pl.DeviceIdType.MESH


def flip(bit, change):
    return 1 - bit if change else bit


class Place:
    def __init__(self):
        f = lax.axis_index("fsdp")
        self.t = lax.axis_index("tok")
        self.core = f % 2
        self.x = (f // 2) % 2
        self.z0 = (f // 4) % 2
        self.z1 = f // 8

        self.inner = self.z0 + self.z1 - 2 * self.z0 * self.z1

    def index(self, z1, z0, dx, dc):
        return (z1 * 2 + z0) * 4 + flip(self.x, dx) * 2 + flip(self.core, dc)

    def block(self, dx=0, dc=0):
        return self.index(self.z1, self.z0, dx, dc)

    def far(self, slot, dx=0):
        if slot < 2:
            z1, z0 = self.z1, flip(self.z0, slot)
        else:
            turn = self.inner if slot == 2 else 1 - self.inner
            z1, z0 = 1 - self.z1, self.z0 + turn - 2 * self.z0 * turn
        return (self.index(z1, z0, dx, 0), self.t)

    def slot_there(self, slot):
        return slot if slot < 2 else 3 - self.inner

    def inward(self):
        z = self.inner * (2 - self.z1) + (1 - self.inner) * (1 + self.z1)
        return (z * 4 + self.x * 2 + self.core, self.t)

    def outward(self):
        return (3 * self.z1 * 4 + self.x * 2 + self.core, self.t)

    def device(self, dx=0, dy=0, dc=0):
        return (self.block(dx, dc), flip(self.t, dy))

    def columns(self, dy, width):
        return pl.ds(pl.multiple_of(flip(self.t, dy) * width, width), width)

    def partners(self):
        return (
            [self.far(slot) for slot in (1, 2, 3)]
            + [self.far(slot, 1) for slot in range(4)]
            + [self.device(dy=1), self.device(dc=1)]
        )


def greet(place):
    barrier = pltpu.get_barrier_semaphore()
    partners = place.partners()
    for partner in partners:
        pl.semaphore_signal(barrier, inc=1, device_id=partner, device_id_type=MESH)
    pl.semaphore_wait(barrier, len(partners))


def arrive(ref, sem):
    pltpu.make_async_copy(ref, ref, sem).wait()


def layer_kernel(
    tok_in, grad_in, routes_in, wg_in, wu_in, wd_in,
    x_out, c_out, hid_out, dg_out, du_out, far_out, give0, give1, keep0, keep1, layer_out, dtok_out, dprob_out,
    g, x, xs, wg, wu, wd, act, turned, wide, near, zbuf,
    routes, sel, back, row_prob, inverse, dr, drs, dpart, dbuf, dsum,
    own_sem, w_sem, zs_sem, xsend_sem, ysend_sem, recv_sem,
    rs_sem, rr_sem, px_sem, pr_sem, st_sem, sr_sem, ds_sem, dr_sem,
    xo_sem, ao_sem, ws_sem, wr_sem, ns_sem, nr_sem, ss_sem, sz_sem,
    qs_sem, qr_sem, far_sem, own_out_sem, credit,
):
    place = Place()
    f32, bf16 = jnp.float32, jnp.bfloat16
    rows, width = tok_in.shape
    full = 2 * width
    half = rows // 2
    local, hid = wg.shape[:2]
    topk = 4
    me = place.device

    def start(copy):
        copy.start()
        return copy

    def remote(source, target, ssem, rsem, to):
        return start(
            pltpu.make_async_remote_copy(
                src_ref=source, dst_ref=target, send_sem=ssem, recv_sem=rsem,
                device_id=to, device_id_type=MESH,
            )
        )

    own = [
        start(pltpu.make_async_copy(ref, g.at[0, 0, a, :, place.columns(0, width)], own_sem.at[a]))
        for a, ref in enumerate((tok_in, grad_in))
    ]
    greet(place)
    sent = {}

    for dz in range(4):
        for dx in range(2):
            if dz or dx:
                j = dz * 2 + dx
                there = place.slot_there(dz) * 2 + dx
                sent["r", j] = remote(
                    routes_in, routes.at[there], rs_sem.at[j], rr_sem.at[there], place.far(dz, dx)
                )
    routes[0] = routes_in[...]
    for copy in own:
        copy.wait()

    def piece(h, dz, dx, dy):
        return g.at[dz, dx, :, pl.ds(h * half, half), place.columns(dy, width)]

    def by_z(h, to, slot, there, k):
        return start(
            pltpu.make_async_remote_copy(
                src_ref=piece(h, slot, 0, 0), dst_ref=piece(h, there, 0, 0),
                send_sem=zs_sem.at[h, k], recv_sem=recv_sem.at[h, there, 0, 0],
                device_id=to, device_id_type=MESH,
            )
        )

    inner = place.inner == 1

    def own_z():
        for h in range(2):
            sent["z", h, 0] = by_z(h, place.inward(), 0, 1 + place.inner, 0)

            @pl.when(inner)
            def _():
                by_z(h, place.outward(), 0, 1, 4)

    def pass_on(slot):
        @pl.when(inner)
        def _():
            for h in range(2):
                got(h, slot, 0, 0)
                if slot == 1:
                    by_z(h, place.inward(), 1, 3, 1)
                else:
                    by_z(h, place.outward(), slot, slot, slot)

    def passed_on(k):
        slot = k % 4

        @pl.when(inner)
        def _():
            for h in range(2):
                pltpu.make_async_copy(piece(h, slot, 0, 0), piece(h, slot, 0, 0), zs_sem.at[h, k]).wait()

    def by_x(h, dz, dy):
        sent["x", h, dz, dy] = remote(
            piece(h, dz, 0, dy), piece(h, dz, 1, dy), xsend_sem.at[h, dz, dy],
            recv_sem.at[h, dz, 1, dy], me(1),
        )

    def by_y(h, dz, dx):
        sent["y", h, dz, dx] = remote(
            piece(h, dz, dx, 0), piece(h, dz, dx, 0), ysend_sem.at[h, dz, dx],
            recv_sem.at[h, dz, dx, 1], me(0, 1),
        )

    def got(h, dz, dx, dy):
        arrive(piece(h, dz, dx, dy), recv_sem.at[h, dz, dx, dy])

    def column(dz):
        for h in range(2):
            if dz:
                @pl.when(jnp.logical_not(inner))
                def _():
                    got(h, dz, 0, 0)

            if h == 0:
                by_x(h, dz, 0)
                by_y(h, dz, 0)
            else:
                by_y(h, dz, 0)
                by_x(h, dz, 0)

    def plane(dz):
        got(0, dz, 1, 0)
        by_y(0, dz, 1)
        got(1, dz, 0, 1)
        by_x(1, dz, 1)

    def last(dz):
        got(0, dz, 0, 1)
        got(1, dz, 1, 0)
        got(0, dz, 1, 1)
        got(1, dz, 1, 1)

    experts = [
        (place.block(0, e // local) * local + e % local).astype(f32) for e in range(2 * local)
    ]

    def build(j):
        names = routes[j, :topk, :]
        probs = routes[j, topk:, :]
        before = (
            lax.broadcasted_iota(jnp.int32, (rows, rows), 0)
            < lax.broadcasted_iota(jnp.int32, (rows, rows), 1)
        ).astype(f32).astype(bf16)
        hits, prob = [], []
        for e in experts:
            chosen = names == e
            hits.append(jnp.max(jnp.where(chosen, 1.0, 0.0), axis=0, keepdims=True))
            prob.append(jnp.sum(jnp.where(chosen, probs, 0.0), axis=0, keepdims=True))
        hit = jnp.concatenate(hits + [jnp.zeros((4, rows), f32)], axis=0)
        spot = jnp.dot(hit.astype(bf16), before, preferred_element_type=f32)
        spot = jnp.where(hit > 0.0, spot, -1.0)
        number = lax.broadcasted_iota(jnp.int32, (CAP, rows), 0).astype(f32)
        ones, high, low, full_prob, inv = [], [], [], [], []
        for e in range(2 * local):
            filled = jnp.broadcast_to(spot[e : e + 1], (CAP, rows)) == number
            top = prob[e].astype(bf16).astype(f32)
            ones.append(jnp.where(filled, 1.0, 0.0))
            high.append(jnp.where(filled, top, 0.0))
            low.append(jnp.where(filled, prob[e] - top, 0.0))
            full_prob.append(jnp.where(filled, prob[e], 0.0))
            inv.append(jnp.where(hits[e] > 0.0, 1.0 / jnp.maximum(prob[e], 1e-30), 0.0))
        ones = jnp.concatenate(ones, axis=0)
        sel[j] = ones.astype(bf16)
        back[j, 0] = ones.T.astype(bf16)
        back[j, 1] = jnp.concatenate(high, axis=0).T.astype(bf16)
        back[j, 2] = jnp.concatenate(low, axis=0).T.astype(bf16)
        row_prob[j] = jnp.sum(jnp.concatenate(full_prob, axis=0), axis=1, keepdims=True)
        inverse[j] = jnp.concatenate(inv + [jnp.zeros((4, rows), f32)], axis=0)

    def build_all(first, end):
        for j in range(first, end):
            if j:
                arrive(routes.at[j], rr_sem.at[j])

        @pl.loop(first, end)
        def _(j):
            build(j)

    tile = 512

    def select(dz):
        @pl.loop(0, 2)
        def _(dx):
            j = dz * 2 + dx
            at = pl.ds(pl.multiple_of(dx * CAP, CAP), CAP)

            @pl.loop(0, full // tile)
            def _(n):
                cols = pl.ds(pl.multiple_of(n * tile, tile), tile)
                for a in range(2):
                    picked = jnp.dot(sel[j], g[dz, dx, a, :, cols], preferred_element_type=f32)
                    if a:
                        picked = picked * row_prob[j]
                    picked = picked.astype(bf16)
                    for l in range(local):
                        x[a, l, dz, at, cols] = picked[l * CAP : (l + 1) * CAP]
                        m = local + l
                        xs[a, l, dz, at, cols] = picked[m * CAP : (m + 1) * CAP]

        sent["p", dz] = remote(
            xs.at[:, :, dz], x.at[:, :, dz, pl.ds(half, half)], px_sem.at[dz], pr_sem.at[dz], me(0, 0, 1)
        )

    def packed(dz):
        arrive(x.at[:, :, dz, pl.ds(half, half)], pr_sem.at[dz])
        for a, ref in enumerate((x_out, c_out)):
            sent["xo", a, dz] = start(
                pltpu.make_async_copy(x.at[a, :, dz], ref.at[:, dz], xo_sem.at[a, dz])
            )

    nt = (((1,), (1,)), ((), ()))
    tiles = [(h, min(256, hid - h)) for h in range(0, hid, 256)]

    def forward(dz, l):
        if dz == 0:
            for i in range(3):
                loads[i, l].wait()
        total = jnp.zeros((rows, 1), f32)
        for h, n in tiles:
            at = pl.ds(h, n)
            gate = lax.dot_general(x[0, l, dz], wg[l, at, :], nt, preferred_element_type=f32)
            upper = lax.dot_general(x[0, l, dz], wu[l, at, :], nt, preferred_element_type=f32)
            d_hidden = lax.dot_general(x[1, l, dz], wd[l, at, :], nt, preferred_element_type=f32)
            sigma = jax.nn.sigmoid(gate)
            active = gate * sigma
            hidden = active * upper
            total = total + jnp.sum(hidden * d_hidden, axis=1, keepdims=True)
            act[0, l, dz, :, at] = hidden.astype(bf16)
            act[1, l, dz, :, at] = (d_hidden * upper * sigma * (1.0 + gate * (1.0 - sigma))).astype(bf16)
            act[2, l, dz, :, at] = (d_hidden * active).astype(bf16)
        total = jnp.broadcast_to(total, (rows, rows))
        for dx in range(2):
            dr[dz, dx, l * CAP : (l + 1) * CAP, :] = total[dx * CAP : (dx + 1) * CAP]
            drs[dz, dx, l * CAP : (l + 1) * CAP, :] = total[half + dx * CAP : half + (dx + 1) * CAP]

    def handed(dz):
        sent["d", dz] = remote(
            drs.at[dz], dr.at[dz, :, pl.ds(half, half)], ds_sem.at[dz], dr_sem.at[dz], me(0, 0, 1)
        )
        sent.pop(("xo", 0, dz)).wait()
        sent.pop(("xo", 1, dz)).wait()
        pl.semaphore_signal(credit.at[dz], inc=1, device_id=me(0, 0, 1), device_id_type=MESH)
        sent.pop(("p", dz)).wait_send()

    def turn(dz):
        refs = (hid_out, dg_out, du_out)
        for i, ref in enumerate(refs):
            if dz:
                sent.pop(("ao", i, dz - 1)).wait()
            for l in range(local):
                turned[i, l] = act[i, l, dz].T
            sent["ao", i, dz] = start(
                pltpu.make_async_copy(
                    turned.at[i], ref.at[:, :, pl.ds(dz * rows, rows)], ao_sem.at[i, dz]
                )
            )

    def backward(dz, l):
        mine = pl.ds(l * CAP, CAP)

        @pl.loop(0, full // tile)
        def _(n):
            cols = pl.ds(pl.multiple_of(n * tile, tile), tile)
            out = jnp.dot(act[0, l, dz], wd[l, :, cols], preferred_element_type=f32)
            back_rows = jnp.dot(act[1, l, dz], wg[l, :, cols], preferred_element_type=f32)
            back_rows = back_rows + jnp.dot(act[2, l, dz], wu[l, :, cols], preferred_element_type=f32)
            for a, value in enumerate((out.astype(bf16), back_rows.astype(bf16))):
                for dx in range(2):
                    x[a, dx, dz, mine, cols] = value[dx * CAP : (dx + 1) * CAP]
                    xs[a, dx, dz, mine, cols] = value[half + dx * CAP : half + (dx + 1) * CAP]

    def returned(dz):
        pl.semaphore_wait(credit.at[dz], 1)
        sent["s", dz] = remote(
            xs.at[:, :, dz], x.at[:, :, dz, pl.ds(half, half)], st_sem.at[dz], sr_sem.at[dz], me(0, 0, 1)
        )

    def put_back(dz):
        for h in range(2):
            for key in (("x", h, dz, 0), ("y", h, dz, 0)):
                sent.pop(key).wait_send()
        sent.pop(("y", 0, dz, 1)).wait_send()
        sent.pop(("x", 1, dz, 1)).wait_send()
        if dz == 0:
            for h in range(2):
                sent.pop(("z", h, 0)).wait_send()
            passed_on(4)
        else:
            passed_on(dz)
        arrive(x.at[:, :, dz, pl.ds(half, half)], sr_sem.at[dz])
        arrive(dr.at[dz, :, pl.ds(half, half)], dr_sem.at[dz])

        @pl.loop(0, 2)
        def _(dx):
            j = dz * 2 + dx

            @pl.loop(0, full // tile)
            def _(n):
                cols = pl.ds(pl.multiple_of(n * tile, tile), tile)
                out = jnp.dot(back[j, 1], x[0, dx, dz, :, cols], preferred_element_type=f32)
                out = out + jnp.dot(back[j, 2], x[0, dx, dz, :, cols], preferred_element_type=f32)
                g[dz, dx, 0, :, cols] = out.astype(bf16)
                into = jnp.dot(back[j, 0], x[1, dx, dz, :, cols], preferred_element_type=f32)
                g[dz, dx, 1, :, cols] = into.astype(bf16)

            names = routes[j, :topk, :]
            weighted = dr[dz, dx] * sel[j].astype(f32)
            total = jnp.zeros((topk, rows), f32)
            for e, name in enumerate(experts):
                value = jnp.sum(weighted[e * CAP : (e + 1) * CAP], axis=0, keepdims=True)
                value = value * inverse[j, e : e + 1, :]
                total = total + jnp.where(names == name, value, 0.0)
            dpart[j] = jnp.concatenate([total, jnp.zeros((8 - topk, rows), f32)], axis=0)

        for dx in range(2):
            j = dz * 2 + dx
            if j:
                there = place.slot_there(dz) * 2 + dx
                sent["q", j] = remote(
                    dpart.at[j], dbuf.at[there], qs_sem.at[j], qr_sem.at[there], place.far(dz, dx)
                )

    def send_wide(dz):
        for h in range(2):
            across = me(0, 1) if h == 0 else me(1)
            for other in (1, 0):
                dx, dy = (other, 1) if h == 0 else (1, other)
                sent["w", h, dz, other] = remote(
                    piece(h, dz, dx, dy), wide.at[h, dz, other], ws_sem.at[h, dz, other],
                    wr_sem.at[h, dz, other], across,
                )

    def add(target, source):
        for a in range(2):
            @pl.loop(0, half // 16)
            def _(i):
                at = pl.ds(pl.multiple_of(i * 16, 16), 16)
                target[a, at, :] = target[a, at, :] + source[a, at, :]

    def send_near(dz):
        for other in (1, 0):
            for h in range(2):
                dx, dy = (other, 0) if h == 0 else (0, other)
                arrive(wide.at[h, dz, other], wr_sem.at[h, dz, other])
                add(wide.at[h, dz, other], piece(h, dz, dx, dy))
                if other:
                    along = me(1) if h == 0 else me(0, 1)
                    sent["n", h, dz] = remote(
                        wide.at[h, dz, 1], near.at[h, dz], ns_sem.at[h, dz], nr_sem.at[h, dz], along
                    )

    def send_z(dz):
        for h in range(2):
            arrive(near.at[h, dz], nr_sem.at[h, dz])
            add(near.at[h, dz], wide.at[h, dz, 0])
            if dz == 3:
                rows_there = pl.ds(h * half, half)
                sent["far", h] = start(
                    pltpu.make_async_copy(near.at[h, 3], far_out.at[:, rows_there], far_sem.at[h])
                )
            elif dz:
                there = place.slot_there(dz)
                sent["f", h, dz] = remote(
                    near.at[h, dz], zbuf.at[h, there - 1], ss_sem.at[h, dz], sz_sem.at[h, there],
                    place.far(dz),
                )

    def leave_own():
        gives, keeps = (give0, give1), (keep0, keep1)
        for h in range(2):
            for far, refs in ((1, gives), (0, keeps)):
                for other in range(2):
                    dx, dy = (other, far) if h == 0 else (far, other)
                    sent["own", h, far, other] = start(
                        pltpu.make_async_copy(
                            piece(h, 0, dx, dy), refs[h].at[other], own_out_sem.at[h, far, other]
                        )
                    )

    own_z()
    column(0)
    loads = {}
    for l in range(local):
        for i, (ref, to) in enumerate(((wg_in, wg), (wu_in, wu), (wd_in, wd))):
            loads[i, l] = start(pltpu.make_async_copy(ref.at[l], to.at[l], w_sem.at[i, l]))
    build_all(0, 8)
    plane(0)
    pass_on(1)
    column(1)
    pass_on(2)
    last(0)
    select(0)
    for dz in range(4):
        if dz < 3:
            plane(dz + 1)
        if dz == 0:
            pass_on(3)
        packed(dz)
        forward(dz, 0)
        if dz < 2:
            column(dz + 2)
        if dz == 3:
            send_near(1)
        forward(dz, 1)
        handed(dz)
        backward(dz, 0)
        if dz == 3:
            send_near(2)
            send_z(1)
        backward(dz, 1)
        returned(dz)
        if dz < 3:
            last(dz + 1)
            select(dz + 1)
        put_back(dz)
        if dz:
            send_wide(dz)
        else:
            leave_own()
        turn(dz)
    send_z(2)
    send_near(3)
    send_z(3)

    total = dpart[0]
    for j in range(1, 8):
        arrive(dbuf.at[j], qr_sem.at[j])
        total = total + dbuf[j]
    dsum[0] = total
    peer = remote(dsum.at[0], dsum.at[1], qs_sem.at[0], qr_sem.at[0], me(0, 1))

    arrive(dsum.at[1], qr_sem.at[0])
    dprob_out[...] = dsum[0] + dsum[1]
    for h in range(2):
        arrive(zbuf.at[h, 0], sz_sem.at[h, 1])

    def finish(others):
        for a, ref in enumerate((layer_out, dtok_out)):
            for h in range(2):
                @pl.loop(0, half // 16)
                def _(i):
                    at = pl.ds(pl.multiple_of(i * 16, 16), 16)
                    total = zbuf[h, 0, a, at, :].astype(f32)
                    for dz in others:
                        total = total + zbuf[h, dz - 1, a, at, :].astype(f32)
                    to = pl.ds(pl.multiple_of(h * half + i * 16, 16), 16)
                    ref[to, :] = total

    @pl.when(inner)
    def _():
        for dz in (2, 3):
            for h in range(2):
                arrive(zbuf.at[h, dz - 1], sz_sem.at[h, dz])
        finish((2, 3))

    @pl.when(jnp.logical_not(inner))
    def _():
        finish(())

    peer.wait_send()
    for key, copy in sent.items():
        if key[0] in ("ao", "far", "own"):
            copy.wait()
        else:
            copy.wait_send()


def layer(tokens, grad_out, routes, w_gate, w_up, w_down):
    rows, width = tokens.shape
    local, hid, full = w_gate.shape
    half = rows // 2
    bf16, f32 = jnp.bfloat16, jnp.float32
    any_space = pl.BlockSpec(memory_space=pl.ANY)
    vmem = pl.BlockSpec(memory_space=pltpu.VMEM)
    shape = jax.ShapeDtypeStruct
    packed = shape((local, 4, rows, full), bf16)
    acts = shape((local, hid, 4 * rows), bf16)
    out = shape((rows, width), f32)
    far = shape((2, rows, width), bf16)
    quarter = shape((2, 2, half, width), bf16)
    dma = pltpu.SemaphoreType.DMA
    return pl.pallas_call(
        layer_kernel,
        out_shape=(packed, packed, acts, acts, acts, far) + (quarter,) * 4 + (out, out, shape((8, rows), f32)),
        in_specs=[any_space, any_space, vmem, any_space, any_space, any_space],
        out_specs=[any_space] * 10 + [vmem] * 3,
        scratch_shapes=[
            pltpu.VMEM((4, 2, 2, rows, full), bf16),
            pltpu.VMEM((2, 2, 4, rows, full), bf16),
            pltpu.VMEM((2, 2, 4, half, full), bf16),
            pltpu.VMEM((local, hid, full), bf16),
            pltpu.VMEM((local, hid, full), bf16),
            pltpu.VMEM((local, hid, full), bf16),
            pltpu.VMEM((3, local, 4, rows, hid), bf16),
            pltpu.VMEM((3, local, hid, rows), bf16),
            pltpu.VMEM((2, 4, 2, 2, half, width), bf16),
            pltpu.VMEM((2, 4, 2, half, width), bf16),
            pltpu.VMEM((2, 3, 2, half, width), bf16),
            pltpu.VMEM((8, 8, rows), f32),
            pltpu.VMEM((8, rows, rows), bf16),
            pltpu.VMEM((8, 3, rows, rows), bf16),
            pltpu.VMEM((8, rows, 1), f32),
            pltpu.VMEM((8, 8, rows), f32),
            pltpu.VMEM((4, 2, rows, rows), f32),
            pltpu.VMEM((4, 2, half, rows), f32),
            pltpu.VMEM((8, 8, rows), f32),
            pltpu.VMEM((8, 8, rows), f32),
            pltpu.VMEM((2, 8, rows), f32),
            dma((2,)), dma((3, local)), dma((2, 5)), dma((2, 4, 2)), dma((2, 4, 2)), dma((2, 4, 2, 2)),
            dma((8,)), dma((8,)), dma((4,)), dma((4,)), dma((4,)), dma((4,)), dma((4,)), dma((4,)),
            dma((2, 4)), dma((3, 4)), dma((2, 4, 2)), dma((2, 4, 2)), dma((2, 4)), dma((2, 4)),
            dma((2, 4)), dma((2, 4)), dma((8,)), dma((8,)), dma((2,)), dma((2, 2, 2)),
            pltpu.SemaphoreType.REGULAR((4,)),
        ],
        compiler_params=pltpu.CompilerParams(
            collective_id=0, has_side_effects=True, vmem_limit_bytes=61 * 2**20
        ),
    )(tokens, grad_out, routes, w_gate, w_up, w_down)


def weight_kernel(count, *refs):
    acts, rows, outs = refs[:count], refs[count], refs[count + 1 :]
    for act, out in zip(acts, outs):
        out[0] = jnp.dot(act[0], rows[0], preferred_element_type=jnp.float32)


def weights(acts, values):
    local, hid, rows = acts[0].shape
    full = values.shape[2]
    count, tile = len(acts), 512
    of_act = pl.BlockSpec((1, hid, rows), lambda l, n: (l, 0, 0))
    of_rows = pl.BlockSpec((1, rows, tile), lambda l, n: (l, 0, n))
    out = pl.BlockSpec((1, hid, tile), lambda l, n: (l, 0, n))
    return pl.pallas_call(
        functools.partial(weight_kernel, count),
        grid=(local, full // tile),
        out_shape=[jax.ShapeDtypeStruct((local, hid, full), jnp.float32)] * count,
        in_specs=[of_act] * count + [of_rows],
        out_specs=[out] * count,
        compiler_params=pltpu.CompilerParams(vmem_limit_bytes=60 * 2**20),
        cost_estimate=pl.CostEstimate(
            flops=2 * count * local * hid * rows * full,
            bytes_accessed=5 * count * local * hid * full,
            transcendentals=0,
        ),
    )(*acts, values)


def by_one_kernel(tokens, expert_ids, gate_probs, w_gate, w_up, w_down, grad_out):
    topk = expert_ids.shape[1]
    local, hid, full = w_gate.shape
    f32 = jnp.float32
    routes = jnp.concatenate([expert_ids.astype(f32).T, gate_probs.T], axis=0)
    x, c, hidden, d_gate, d_up, far, *own, part_out, part_in, d_prob = layer(
        tokens, grad_out, routes, w_gate, w_up, w_down
    )
    x, c = (v.reshape(local, -1, full) for v in (x, c))

    blocks = lax.axis_size("fsdp")
    by_y = functools.partial(lax.ppermute, axis_name="tok", perm=[(0, 1), (1, 0)])
    by_x = functools.partial(
        lax.ppermute, axis_name="fsdp", perm=[(i, i + 2 - i // 2 % 2 * 4) for i in range(blocks)]
    )
    give0, give1, keep0, keep1 = own
    near0, near1 = by_y(give0), by_x(give1)
    ends = [(z * 4 + i, (3 - z) * 4 + i) for z in (0, 3) for i in range(4)]
    inners = [(z * 4 + i, (6 - 3 * z) * 4 + i) for z in (1, 2) for i in range(4)]
    far = [lax.ppermute(far, "fsdp", pairs) for pairs in (ends, inners)]
    d_w_gate, d_w_up = weights((d_gate, d_up), x)
    sum0, sum1 = near0 + keep0, near1 + keep1
    sum0, sum1, hidden = lax.optimization_barrier((sum0, sum1, hidden))
    near0, near1 = by_x(sum0[1]), by_y(sum1[1])
    d_w_down = jnp.einsum("lhr,lrd->lhd", hidden, c, preferred_element_type=f32)

    def total(a, part):
        halves = [near[a].astype(f32) + held[0, a].astype(f32) for near, held in ((near0, sum0), (near1, sum1))]
        value = part + jnp.concatenate(halves, axis=0) + far[0][a].astype(f32) + far[1][a].astype(f32)
        return value.astype(tokens.dtype)

    layer_out, d_tokens = total(0, part_out), total(1, part_in)
    return (layer_out, d_tokens, d_prob[:topk].T, d_w_gate, d_w_up, d_w_down)


def gather_any(value):
    wide = lax.all_gather(value, "tok", axis=1, tiled=True)
    return lax.all_gather(wide, "fsdp", axis=0, tiled=False)


def scatter_any(value):
    blocks, rows, full = value.shape
    mine = lax.psum_scatter(
        value.reshape(blocks * rows, full), "fsdp", scatter_dimension=0, tiled=True
    )
    return lax.psum_scatter(mine, "tok", scatter_dimension=1, tiled=True)


def on_device(tokens, expert_ids, gate_probs, w_gate, w_up, w_down, grad_out):
    tok_rows, topk = expert_ids.shape
    local = w_gate.shape[0]
    f32 = jnp.float32
    me = lax.axis_index("fsdp")

    routes = jnp.concatenate([expert_ids.astype(f32).T, gate_probs.T], axis=0)
    routes = lax.all_gather(routes, "fsdp", axis=0, tiled=False)
    all_tokens, all_grads = gather_any(tokens), gather_any(grad_out)
    blocks = all_tokens.shape[0]

    names = routes[:, :topk]
    mine = (me * local + jnp.arange(local, dtype=jnp.int32)).astype(f32)
    chosen = names[None] == mine[:, None, None, None]
    hit = jnp.any(chosen, axis=2)
    prob = jnp.sum(jnp.where(chosen, routes[None, :, topk:], 0.0), axis=2)
    before = jnp.triu(jnp.ones((tok_rows, tok_rows), jnp.bfloat16), 1)
    place = jnp.einsum("ebs,st->ebt", hit.astype(jnp.bfloat16), before, preferred_element_type=f32)
    place = jnp.where(hit, place, -1.0)
    filled = place[:, :, None, :] == jnp.arange(CAP, dtype=jnp.int32).astype(f32)[None, None, :, None]
    select = filled.astype(jnp.bfloat16)
    row_prob = jnp.sum(jnp.where(filled, prob[:, :, None, :], 0.0), axis=3)
    row_prob = row_prob.reshape(local, blocks * CAP, 1)

    def pick(values):
        rows = jnp.einsum("ebrt,btd->ebrd", select, values, preferred_element_type=f32)
        return rows.astype(jnp.bfloat16).reshape(local, blocks * CAP, values.shape[-1])

    def place_back(rows):
        rows = rows.astype(jnp.bfloat16).reshape(local, blocks, CAP, rows.shape[-1])
        values = jnp.einsum("ebrt,ebrd->btd", select, rows, preferred_element_type=f32)
        return values.astype(jnp.bfloat16)

    inputs = pick(all_tokens)
    cotangent = pick(all_grads)
    gate = jnp.einsum("erd,ehd->erh", inputs, w_gate, preferred_element_type=f32)
    upper = jnp.einsum("erd,ehd->erh", inputs, w_up, preferred_element_type=f32)
    raw = jnp.einsum("erd,ehd->erh", cotangent, w_down, preferred_element_type=f32)
    sigma = jax.nn.sigmoid(gate)
    active = gate * sigma
    hidden = active * upper
    weighted = (row_prob * hidden).astype(jnp.bfloat16)
    d_hidden = row_prob * raw
    d_gate = (d_hidden * upper * sigma * (1.0 + gate * (1.0 - sigma))).astype(jnp.bfloat16)
    d_upper = (d_hidden * active).astype(jnp.bfloat16)
    d_rows = jnp.sum(hidden * raw, axis=2).reshape(local, blocks, CAP)

    out_rows = jnp.einsum("erh,ehd->erd", weighted, w_down, preferred_element_type=f32)
    in_rows = jnp.einsum("erh,ehd->erd", d_gate, w_gate, preferred_element_type=f32)
    in_rows = in_rows + jnp.einsum("erh,ehd->erd", d_upper, w_up, preferred_element_type=f32)
    part_out, part_in = place_back(out_rows), place_back(in_rows)
    layer_out, d_tokens = scatter_any(part_out), scatter_any(part_in)

    d_w_down = jnp.einsum("erh,erd->ehd", weighted, cotangent, preferred_element_type=f32)
    d_w_gate = jnp.einsum("erh,erd->ehd", d_gate, inputs, preferred_element_type=f32)
    d_w_up = jnp.einsum("erh,erd->ehd", d_upper, inputs, preferred_element_type=f32)

    d_prob = jnp.sum(jnp.where(filled, d_rows[:, :, :, None], 0.0), axis=2)
    d_prob = jnp.sum(jnp.where(chosen, d_prob[:, :, None, :], 0.0), axis=0)
    d_prob = d_prob.reshape(blocks, topk * tok_rows)
    d_prob = lax.all_to_all(d_prob, "fsdp", split_axis=0, concat_axis=0, tiled=True)
    d_prob = jnp.sum(d_prob, axis=0)
    size = lax.axis_size("tok")
    mine_only = d_prob
    for turn in range(1, size):
        pairs = [(i, (i + turn) % size) for i in range(size)]
        d_prob = d_prob + lax.ppermute(mine_only, "tok", pairs)
    d_gate_probs = d_prob.reshape(topk, tok_rows).T
    return (layer_out, d_tokens, d_gate_probs, d_w_gate, d_w_up, d_w_down)


def solution(mesh):
    by_kernel = mesh.shape["fsdp"] == 16 and mesh.shape["tok"] == 2
    return jax.shard_map(
        by_one_kernel if by_kernel else on_device,
        mesh=mesh,
        in_specs=(
            P("fsdp", "tok"),
            P("fsdp", None),
            P("fsdp", None),
            P("fsdp", "tok", None),
            P("fsdp", "tok", None),
            P("fsdp", "tok", None),
            P("fsdp", "tok"),
        ),
        out_specs=(
            P("fsdp", "tok"),
            P("fsdp", "tok"),
            P("fsdp", None),
            P("fsdp", "tok", None),
            P("fsdp", "tok", None),
            P("fsdp", "tok", None),
        ),
        check_vma=False,
    )
```

```python
import functools

import jax
import jax.numpy as jnp
from jax import lax
from jax.experimental import pallas as pl
from jax.experimental.pallas import tpu as pltpu
from jax.sharding import PartitionSpec as P

CAP = 32
MESH = pl.DeviceIdType.MESH


def flip(bit, change):
    return 1 - bit if change else bit


class Place:
    def __init__(self):
        f = lax.axis_index("fsdp")
        self.t = lax.axis_index("tok")
        self.core = f % 2
        self.x = (f // 2) % 2
        self.z0 = (f // 4) % 2
        self.z1 = f // 8

        self.inner = self.z0 + self.z1 - 2 * self.z0 * self.z1

    def index(self, z1, z0, dx, dc):
        return (z1 * 2 + z0) * 4 + flip(self.x, dx) * 2 + flip(self.core, dc)

    def block(self, dx=0, dc=0):
        return self.index(self.z1, self.z0, dx, dc)

    def far(self, slot, dx=0):
        if slot < 2:
            z1, z0 = self.z1, flip(self.z0, slot)
        else:
            turn = self.inner if slot == 2 else 1 - self.inner
            z1, z0 = 1 - self.z1, self.z0 + turn - 2 * self.z0 * turn
        return (self.index(z1, z0, dx, 0), self.t)

    def slot_there(self, slot):
        return slot if slot < 2 else 3 - self.inner

    def inward(self):
        z = self.inner * (2 - self.z1) + (1 - self.inner) * (1 + self.z1)
        return (z * 4 + self.x * 2 + self.core, self.t)

    def outward(self):
        return (3 * self.z1 * 4 + self.x * 2 + self.core, self.t)

    def device(self, dx=0, dy=0, dc=0):
        return (self.block(dx, dc), flip(self.t, dy))

    def columns(self, dy, width):
        return pl.ds(pl.multiple_of(flip(self.t, dy) * width, width), width)

    def partners(self):
        return (
            [self.far(slot) for slot in (1, 2, 3)]
            + [self.far(slot, 1) for slot in range(4)]
            + [self.device(dy=1), self.device(dc=1)]
        )


def greet(place):
    barrier = pltpu.get_barrier_semaphore()
    partners = place.partners()
    for partner in partners:
        pl.semaphore_signal(barrier, inc=1, device_id=partner, device_id_type=MESH)
    pl.semaphore_wait(barrier, len(partners))


def arrive(ref, sem):
    pltpu.make_async_copy(ref, ref, sem).wait()


def layer_kernel(
    tok_in, grad_in, routes_in, wg_in, wu_in, wd_in,
    x_out, c_out, hid_out, dg_out, du_out, far_out, give0, give1, keep0, keep1, layer_out, dtok_out, dprob_out,
    g, x, xs, wg, wu, wd, act, turned, wide, near, zbuf,
    routes, sel, back, row_prob, inverse, dr, drs, dpart, dbuf, dsum,
    own_sem, w_sem, zs_sem, xsend_sem, ysend_sem, recv_sem,
    rs_sem, rr_sem, px_sem, pr_sem, st_sem, sr_sem, ds_sem, dr_sem,
    xo_sem, ao_sem, ws_sem, wr_sem, ns_sem, nr_sem, ss_sem, sz_sem,
    qs_sem, qr_sem, far_sem, own_out_sem, credit,
):
    place = Place()
    f32, bf16 = jnp.float32, jnp.bfloat16
    rows, width = tok_in.shape
    full = 2 * width
    half = rows // 2
    local, hid = wg.shape[:2]
    topk = 4
    me = place.device

    def start(copy):
        copy.start()
        return copy

    def remote(source, target, ssem, rsem, to):
        return start(
            pltpu.make_async_remote_copy(
                src_ref=source, dst_ref=target, send_sem=ssem, recv_sem=rsem,
                device_id=to, device_id_type=MESH,
            )
        )

    own = [
        start(pltpu.make_async_copy(ref, g.at[0, 0, a, :, place.columns(0, width)], own_sem.at[a]))
        for a, ref in enumerate((tok_in, grad_in))
    ]
    greet(place)
    sent = {}

    for dz in range(4):
        for dx in range(2):
            if dz or dx:
                j = dz * 2 + dx
                there = place.slot_there(dz) * 2 + dx
                sent["r", j] = remote(
                    routes_in, routes.at[there], rs_sem.at[j], rr_sem.at[there], place.far(dz, dx)
                )
    routes[0] = routes_in[...]
    for copy in own:
        copy.wait()

    def piece(h, dz, dx, dy):
        return g.at[dz, dx, :, pl.ds(h * half, half), place.columns(dy, width)]

    def by_z(h, to, slot, there, k):
        return start(
            pltpu.make_async_remote_copy(
                src_ref=piece(h, slot, 0, 0), dst_ref=piece(h, there, 0, 0),
                send_sem=zs_sem.at[h, k], recv_sem=recv_sem.at[h, there, 0, 0],
                device_id=to, device_id_type=MESH,
            )
        )

    inner = place.inner == 1

    def own_z():
        for h in range(2):
            sent["z", h, 0] = by_z(h, place.inward(), 0, 1 + place.inner, 0)

            @pl.when(inner)
            def _():
                by_z(h, place.outward(), 0, 1, 4)

    def pass_on(slot):
        @pl.when(inner)
        def _():
            for h in range(2):
                got(h, slot, 0, 0)
                if slot == 1:
                    by_z(h, place.inward(), 1, 3, 1)
                else:
                    by_z(h, place.outward(), slot, slot, slot)

    def passed_on(k):
        slot = k % 4

        @pl.when(inner)
        def _():
            for h in range(2):
                pltpu.make_async_copy(piece(h, slot, 0, 0), piece(h, slot, 0, 0), zs_sem.at[h, k]).wait()

    def by_x(h, dz, dy):
        sent["x", h, dz, dy] = remote(
            piece(h, dz, 0, dy), piece(h, dz, 1, dy), xsend_sem.at[h, dz, dy],
            recv_sem.at[h, dz, 1, dy], me(1),
        )

    def by_y(h, dz, dx):
        sent["y", h, dz, dx] = remote(
            piece(h, dz, dx, 0), piece(h, dz, dx, 0), ysend_sem.at[h, dz, dx],
            recv_sem.at[h, dz, dx, 1], me(0, 1),
        )

    def got(h, dz, dx, dy):
        arrive(piece(h, dz, dx, dy), recv_sem.at[h, dz, dx, dy])

    def column(dz):
        for h in range(2):
            if dz:
                @pl.when(jnp.logical_not(inner))
                def _():
                    got(h, dz, 0, 0)

            if h == 0:
                by_x(h, dz, 0)
                by_y(h, dz, 0)
            else:
                by_y(h, dz, 0)
                by_x(h, dz, 0)

    def plane(dz):
        got(0, dz, 1, 0)
        by_y(0, dz, 1)
        got(1, dz, 0, 1)
        by_x(1, dz, 1)

    def last(dz):
        got(0, dz, 0, 1)
        got(1, dz, 1, 0)
        got(0, dz, 1, 1)
        got(1, dz, 1, 1)

    experts = [
        (place.block(0, e // local) * local + e % local).astype(f32) for e in range(2 * local)
    ]

    def build(j):
        names = routes[j, :topk, :]
        probs = routes[j, topk:, :]
        before = (
            lax.broadcasted_iota(jnp.int32, (rows, rows), 0)
            < lax.broadcasted_iota(jnp.int32, (rows, rows), 1)
        ).astype(f32).astype(bf16)
        hits, prob = [], []
        for e in experts:
            chosen = names == e
            hits.append(jnp.max(jnp.where(chosen, 1.0, 0.0), axis=0, keepdims=True))
            prob.append(jnp.sum(jnp.where(chosen, probs, 0.0), axis=0, keepdims=True))
        hit = jnp.concatenate(hits + [jnp.zeros((4, rows), f32)], axis=0)
        spot = jnp.dot(hit.astype(bf16), before, preferred_element_type=f32)
        spot = jnp.where(hit > 0.0, spot, -1.0)
        number = lax.broadcasted_iota(jnp.int32, (CAP, rows), 0).astype(f32)
        ones, high, low, full_prob, inv = [], [], [], [], []
        for e in range(2 * local):
            filled = jnp.broadcast_to(spot[e : e + 1], (CAP, rows)) == number
            top = prob[e].astype(bf16).astype(f32)
            ones.append(jnp.where(filled, 1.0, 0.0))
            high.append(jnp.where(filled, top, 0.0))
            low.append(jnp.where(filled, prob[e] - top, 0.0))
            full_prob.append(jnp.where(filled, prob[e], 0.0))
            inv.append(jnp.where(hits[e] > 0.0, 1.0 / jnp.maximum(prob[e], 1e-30), 0.0))
        ones = jnp.concatenate(ones, axis=0)
        sel[j] = ones.astype(bf16)
        back[j, 0] = ones.T.astype(bf16)
        back[j, 1] = jnp.concatenate(high, axis=0).T.astype(bf16)
        back[j, 2] = jnp.concatenate(low, axis=0).T.astype(bf16)
        row_prob[j] = jnp.sum(jnp.concatenate(full_prob, axis=0), axis=1, keepdims=True)
        inverse[j] = jnp.concatenate(inv + [jnp.zeros((4, rows), f32)], axis=0)

    def build_all(first, end):
        for j in range(first, end):
            if j:
                arrive(routes.at[j], rr_sem.at[j])

        @pl.loop(first, end)
        def _(j):
            build(j)

    tile = 512

    def select(dz):
        @pl.loop(0, 2)
        def _(dx):
            j = dz * 2 + dx
            at = pl.ds(pl.multiple_of(dx * CAP, CAP), CAP)

            @pl.loop(0, full // tile)
            def _(n):
                cols = pl.ds(pl.multiple_of(n * tile, tile), tile)
                for a in range(2):
                    picked = jnp.dot(sel[j], g[dz, dx, a, :, cols], preferred_element_type=f32)
                    if a:
                        picked = picked * row_prob[j]
                    picked = picked.astype(bf16)
                    for l in range(local):
                        x[a, l, dz, at, cols] = picked[l * CAP : (l + 1) * CAP]
                        m = local + l
                        xs[a, l, dz, at, cols] = picked[m * CAP : (m + 1) * CAP]

        sent["p", dz] = remote(
            xs.at[:, :, dz], x.at[:, :, dz, pl.ds(half, half)], px_sem.at[dz], pr_sem.at[dz], me(0, 0, 1)
        )

    def packed(dz):
        arrive(x.at[:, :, dz, pl.ds(half, half)], pr_sem.at[dz])
        for a, ref in enumerate((x_out, c_out)):
            sent["xo", a, dz] = start(
                pltpu.make_async_copy(x.at[a, :, dz], ref.at[:, dz], xo_sem.at[a, dz])
            )

    nt = (((1,), (1,)), ((), ()))
    tiles = [(h, min(256, hid - h)) for h in range(0, hid, 256)]

    def forward(dz, l):
        if dz == 0:
            for i in range(3):
                loads[i, l].wait()
        total = jnp.zeros((rows, 1), f32)
        for h, n in tiles:
            at = pl.ds(h, n)
            gate = lax.dot_general(x[0, l, dz], wg[l, at, :], nt, preferred_element_type=f32)
            upper = lax.dot_general(x[0, l, dz], wu[l, at, :], nt, preferred_element_type=f32)
            d_hidden = lax.dot_general(x[1, l, dz], wd[l, at, :], nt, preferred_element_type=f32)
            sigma = jax.nn.sigmoid(gate)
            active = gate * sigma
            hidden = active * upper
            total = total + jnp.sum(hidden * d_hidden, axis=1, keepdims=True)
            act[0, l, dz, :, at] = hidden.astype(bf16)
            act[1, l, dz, :, at] = (d_hidden * upper * sigma * (1.0 + gate * (1.0 - sigma))).astype(bf16)
            act[2, l, dz, :, at] = (d_hidden * active).astype(bf16)
        total = jnp.broadcast_to(total, (rows, rows))
        for dx in range(2):
            dr[dz, dx, l * CAP : (l + 1) * CAP, :] = total[dx * CAP : (dx + 1) * CAP]
            drs[dz, dx, l * CAP : (l + 1) * CAP, :] = total[half + dx * CAP : half + (dx + 1) * CAP]

    def handed(dz):
        sent["d", dz] = remote(
            drs.at[dz], dr.at[dz, :, pl.ds(half, half)], ds_sem.at[dz], dr_sem.at[dz], me(0, 0, 1)
        )
        sent.pop(("xo", 0, dz)).wait()
        sent.pop(("xo", 1, dz)).wait()
        pl.semaphore_signal(credit.at[dz], inc=1, device_id=me(0, 0, 1), device_id_type=MESH)
        sent.pop(("p", dz)).wait_send()

    def turn(dz):
        refs = (hid_out, dg_out, du_out)
        for i, ref in enumerate(refs):
            if dz:
                sent.pop(("ao", i, dz - 1)).wait()
            for l in range(local):
                turned[i, l] = act[i, l, dz].T
            sent["ao", i, dz] = start(
                pltpu.make_async_copy(
                    turned.at[i], ref.at[:, :, pl.ds(dz * rows, rows)], ao_sem.at[i, dz]
                )
            )

    def backward(dz, l):
        mine = pl.ds(l * CAP, CAP)

        @pl.loop(0, full // tile)
        def _(n):
            cols = pl.ds(pl.multiple_of(n * tile, tile), tile)
            out = jnp.dot(act[0, l, dz], wd[l, :, cols], preferred_element_type=f32)
            back_rows = jnp.dot(act[1, l, dz], wg[l, :, cols], preferred_element_type=f32)
            back_rows = back_rows + jnp.dot(act[2, l, dz], wu[l, :, cols], preferred_element_type=f32)
            for a, value in enumerate((out.astype(bf16), back_rows.astype(bf16))):
                for dx in range(2):
                    x[a, dx, dz, mine, cols] = value[dx * CAP : (dx + 1) * CAP]
                    xs[a, dx, dz, mine, cols] = value[half + dx * CAP : half + (dx + 1) * CAP]

    def returned(dz):
        pl.semaphore_wait(credit.at[dz], 1)
        sent["s", dz] = remote(
            xs.at[:, :, dz], x.at[:, :, dz, pl.ds(half, half)], st_sem.at[dz], sr_sem.at[dz], me(0, 0, 1)
        )

    def put_back(dz):
        for h in range(2):
            for key in (("x", h, dz, 0), ("y", h, dz, 0)):
                sent.pop(key).wait_send()
        sent.pop(("y", 0, dz, 1)).wait_send()
        sent.pop(("x", 1, dz, 1)).wait_send()
        if dz == 0:
            for h in range(2):
                sent.pop(("z", h, 0)).wait_send()
            passed_on(4)
        else:
            passed_on(dz)
        arrive(x.at[:, :, dz, pl.ds(half, half)], sr_sem.at[dz])
        arrive(dr.at[dz, :, pl.ds(half, half)], dr_sem.at[dz])

        @pl.loop(0, 2)
        def _(dx):
            j = dz * 2 + dx

            @pl.loop(0, full // tile)
            def _(n):
                cols = pl.ds(pl.multiple_of(n * tile, tile), tile)
                out = jnp.dot(back[j, 1], x[0, dx, dz, :, cols], preferred_element_type=f32)
                out = out + jnp.dot(back[j, 2], x[0, dx, dz, :, cols], preferred_element_type=f32)
                g[dz, dx, 0, :, cols] = out.astype(bf16)
                into = jnp.dot(back[j, 0], x[1, dx, dz, :, cols], preferred_element_type=f32)
                g[dz, dx, 1, :, cols] = into.astype(bf16)

            names = routes[j, :topk, :]
            weighted = dr[dz, dx] * sel[j].astype(f32)
            total = jnp.zeros((topk, rows), f32)
            for e, name in enumerate(experts):
                value = jnp.sum(weighted[e * CAP : (e + 1) * CAP], axis=0, keepdims=True)
                value = value * inverse[j, e : e + 1, :]
                total = total + jnp.where(names == name, value, 0.0)
            dpart[j] = jnp.concatenate([total, jnp.zeros((8 - topk, rows), f32)], axis=0)

        for dx in range(2):
            j = dz * 2 + dx
            if j:
                there = place.slot_there(dz) * 2 + dx
                sent["q", j] = remote(
                    dpart.at[j], dbuf.at[there], qs_sem.at[j], qr_sem.at[there], place.far(dz, dx)
                )

    def send_wide(dz):
        for h in range(2):
            across = me(0, 1) if h == 0 else me(1)
            for other in (1, 0):
                dx, dy = (other, 1) if h == 0 else (1, other)
                sent["w", h, dz, other] = remote(
                    piece(h, dz, dx, dy), wide.at[h, dz, other], ws_sem.at[h, dz, other],
                    wr_sem.at[h, dz, other], across,
                )

    def add(target, source):
        for a in range(2):
            @pl.loop(0, half // 16)
            def _(i):
                at = pl.ds(pl.multiple_of(i * 16, 16), 16)
                target[a, at, :] = target[a, at, :] + source[a, at, :]

    def send_near(dz):
        for other in (1, 0):
            for h in range(2):
                dx, dy = (other, 0) if h == 0 else (0, other)
                arrive(wide.at[h, dz, other], wr_sem.at[h, dz, other])
                add(wide.at[h, dz, other], piece(h, dz, dx, dy))
                if other:
                    along = me(1) if h == 0 else me(0, 1)
                    sent["n", h, dz] = remote(
                        wide.at[h, dz, 1], near.at[h, dz], ns_sem.at[h, dz], nr_sem.at[h, dz], along
                    )

    def send_z(dz):
        for h in range(2):
            arrive(near.at[h, dz], nr_sem.at[h, dz])
            add(near.at[h, dz], wide.at[h, dz, 0])
            if dz == 3:
                rows_there = pl.ds(h * half, half)
                sent["far", h] = start(
                    pltpu.make_async_copy(near.at[h, 3], far_out.at[:, rows_there], far_sem.at[h])
                )
            elif dz:
                there = place.slot_there(dz)
                sent["f", h, dz] = remote(
                    near.at[h, dz], zbuf.at[h, there - 1], ss_sem.at[h, dz], sz_sem.at[h, there],
                    place.far(dz),
                )

    def leave_own():
        gives, keeps = (give0, give1), (keep0, keep1)
        for h in range(2):
            for far, refs in ((1, gives), (0, keeps)):
                for other in range(2):
                    dx, dy = (other, far) if h == 0 else (far, other)
                    sent["own", h, far, other] = start(
                        pltpu.make_async_copy(
                            piece(h, 0, dx, dy), refs[h].at[other], own_out_sem.at[h, far, other]
                        )
                    )

    own_z()
    column(0)
    loads = {}
    for l in range(local):
        for i, (ref, to) in enumerate(((wg_in, wg), (wu_in, wu), (wd_in, wd))):
            loads[i, l] = start(pltpu.make_async_copy(ref.at[l], to.at[l], w_sem.at[i, l]))
    build_all(0, 8)
    plane(0)
    pass_on(1)
    column(1)
    pass_on(2)
    last(0)
    select(0)
    for dz in range(4):
        if dz < 3:
            plane(dz + 1)
        if dz == 2:
            send_wide(1)
        if dz == 0:
            pass_on(3)
        packed(dz)
        forward(dz, 0)
        if dz < 2:
            column(dz + 2)
        if dz == 3:
            send_near(1)
        forward(dz, 1)
        handed(dz)
        backward(dz, 0)
        backward(dz, 1)
        returned(dz)
        if dz == 3:
            send_near(2)
            send_z(1)
        if dz < 3:
            last(dz + 1)
            select(dz + 1)
        put_back(dz)
        if dz >= 2:
            send_wide(dz)
        if dz == 0:
            leave_own()
        turn(dz)
    send_z(2)
    send_near(3)
    send_z(3)

    total = dpart[0]
    for j in range(1, 8):
        arrive(dbuf.at[j], qr_sem.at[j])
        total = total + dbuf[j]
    dsum[0] = total
    peer = remote(dsum.at[0], dsum.at[1], qs_sem.at[0], qr_sem.at[0], me(0, 1))

    arrive(dsum.at[1], qr_sem.at[0])
    dprob_out[...] = dsum[0] + dsum[1]
    for h in range(2):
        arrive(zbuf.at[h, 0], sz_sem.at[h, 1])

    def finish(others):
        for a, ref in enumerate((layer_out, dtok_out)):
            for h in range(2):
                @pl.loop(0, half // 16)
                def _(i):
                    at = pl.ds(pl.multiple_of(i * 16, 16), 16)
                    total = zbuf[h, 0, a, at, :].astype(f32)
                    for dz in others:
                        total = total + zbuf[h, dz - 1, a, at, :].astype(f32)
                    to = pl.ds(pl.multiple_of(h * half + i * 16, 16), 16)
                    ref[to, :] = total

    @pl.when(inner)
    def _():
        for dz in (2, 3):
            for h in range(2):
                arrive(zbuf.at[h, dz - 1], sz_sem.at[h, dz])
        finish((2, 3))

    @pl.when(jnp.logical_not(inner))
    def _():
        finish(())

    peer.wait_send()
    for key, copy in sent.items():
        if key[0] in ("ao", "far", "own"):
            copy.wait()
        else:
            copy.wait_send()


def layer(tokens, grad_out, routes, w_gate, w_up, w_down):
    rows, width = tokens.shape
    local, hid, full = w_gate.shape
    half = rows // 2
    bf16, f32 = jnp.bfloat16, jnp.float32
    any_space = pl.BlockSpec(memory_space=pl.ANY)
    vmem = pl.BlockSpec(memory_space=pltpu.VMEM)
    shape = jax.ShapeDtypeStruct
    packed = shape((local, 4, rows, full), bf16)
    acts = shape((local, hid, 4 * rows), bf16)
    out = shape((rows, width), f32)
    far = shape((2, rows, width), bf16)
    quarter = shape((2, 2, half, width), bf16)
    dma = pltpu.SemaphoreType.DMA
    return pl.pallas_call(
        layer_kernel,
        out_shape=(packed, packed, acts, acts, acts, far) + (quarter,) * 4 + (out, out, shape((8, rows), f32)),
        in_specs=[any_space, any_space, vmem, any_space, any_space, any_space],
        out_specs=[any_space] * 10 + [vmem] * 3,
        scratch_shapes=[
            pltpu.VMEM((4, 2, 2, rows, full), bf16),
            pltpu.VMEM((2, 2, 4, rows, full), bf16),
            pltpu.VMEM((2, 2, 4, half, full), bf16),
            pltpu.VMEM((local, hid, full), bf16),
            pltpu.VMEM((local, hid, full), bf16),
            pltpu.VMEM((local, hid, full), bf16),
            pltpu.VMEM((3, local, 4, rows, hid), bf16),
            pltpu.VMEM((3, local, hid, rows), bf16),
            pltpu.VMEM((2, 4, 2, 2, half, width), bf16),
            pltpu.VMEM((2, 4, 2, half, width), bf16),
            pltpu.VMEM((2, 3, 2, half, width), bf16),
            pltpu.VMEM((8, 8, rows), f32),
            pltpu.VMEM((8, rows, rows), bf16),
            pltpu.VMEM((8, 3, rows, rows), bf16),
            pltpu.VMEM((8, rows, 1), f32),
            pltpu.VMEM((8, 8, rows), f32),
            pltpu.VMEM((4, 2, rows, rows), f32),
            pltpu.VMEM((4, 2, half, rows), f32),
            pltpu.VMEM((8, 8, rows), f32),
            pltpu.VMEM((8, 8, rows), f32),
            pltpu.VMEM((2, 8, rows), f32),
            dma((2,)), dma((3, local)), dma((2, 5)), dma((2, 4, 2)), dma((2, 4, 2)), dma((2, 4, 2, 2)),
            dma((8,)), dma((8,)), dma((4,)), dma((4,)), dma((4,)), dma((4,)), dma((4,)), dma((4,)),
            dma((2, 4)), dma((3, 4)), dma((2, 4, 2)), dma((2, 4, 2)), dma((2, 4)), dma((2, 4)),
            dma((2, 4)), dma((2, 4)), dma((8,)), dma((8,)), dma((2,)), dma((2, 2, 2)),
            pltpu.SemaphoreType.REGULAR((4,)),
        ],
        compiler_params=pltpu.CompilerParams(
            collective_id=0, has_side_effects=True, vmem_limit_bytes=61 * 2**20
        ),
    )(tokens, grad_out, routes, w_gate, w_up, w_down)


def weight_kernel(count, *refs):
    acts, rows, outs = refs[:count], refs[count], refs[count + 1 :]
    for act, out in zip(acts, outs):
        out[0] = jnp.dot(act[0], rows[0], preferred_element_type=jnp.float32)


def weights(acts, values):
    local, hid, rows = acts[0].shape
    full = values.shape[2]
    count, tile = len(acts), 512
    of_act = pl.BlockSpec((1, hid, rows), lambda l, n: (l, 0, 0))
    of_rows = pl.BlockSpec((1, rows, tile), lambda l, n: (l, 0, n))
    out = pl.BlockSpec((1, hid, tile), lambda l, n: (l, 0, n))
    return pl.pallas_call(
        functools.partial(weight_kernel, count),
        grid=(local, full // tile),
        out_shape=[jax.ShapeDtypeStruct((local, hid, full), jnp.float32)] * count,
        in_specs=[of_act] * count + [of_rows],
        out_specs=[out] * count,
        compiler_params=pltpu.CompilerParams(vmem_limit_bytes=60 * 2**20),
        cost_estimate=pl.CostEstimate(
            flops=2 * count * local * hid * rows * full,
            bytes_accessed=5 * count * local * hid * full,
            transcendentals=0,
        ),
    )(*acts, values)


def by_one_kernel(tokens, expert_ids, gate_probs, w_gate, w_up, w_down, grad_out):
    topk = expert_ids.shape[1]
    local, hid, full = w_gate.shape
    f32 = jnp.float32
    routes = jnp.concatenate([expert_ids.astype(f32).T, gate_probs.T], axis=0)
    x, c, hidden, d_gate, d_up, far, *own, part_out, part_in, d_prob = layer(
        tokens, grad_out, routes, w_gate, w_up, w_down
    )
    x, c = (v.reshape(local, -1, full) for v in (x, c))

    blocks = lax.axis_size("fsdp")
    by_y = functools.partial(lax.ppermute, axis_name="tok", perm=[(0, 1), (1, 0)])
    by_x = functools.partial(
        lax.ppermute, axis_name="fsdp", perm=[(i, i + 2 - i // 2 % 2 * 4) for i in range(blocks)]
    )
    give0, give1, keep0, keep1 = own
    near0, near1 = by_y(give0), by_x(give1)
    ends = [(z * 4 + i, (3 - z) * 4 + i) for z in (0, 3) for i in range(4)]
    inners = [(z * 4 + i, (6 - 3 * z) * 4 + i) for z in (1, 2) for i in range(4)]
    far = [lax.ppermute(far, "fsdp", pairs) for pairs in (ends, inners)]
    d_w_gate, d_w_up = weights((d_gate, d_up), x)
    sum0, sum1 = near0 + keep0, near1 + keep1
    sum0, sum1, hidden = lax.optimization_barrier((sum0, sum1, hidden))
    near0, near1 = by_x(sum0[1]), by_y(sum1[1])
    d_w_down = jnp.einsum("lhr,lrd->lhd", hidden, c, preferred_element_type=f32)

    def total(a, part):
        halves = [near[a].astype(f32) + held[0, a].astype(f32) for near, held in ((near0, sum0), (near1, sum1))]
        value = part + jnp.concatenate(halves, axis=0) + far[0][a].astype(f32) + far[1][a].astype(f32)
        return value.astype(tokens.dtype)

    layer_out, d_tokens = total(0, part_out), total(1, part_in)
    return (layer_out, d_tokens, d_prob[:topk].T, d_w_gate, d_w_up, d_w_down)


def gather_any(value):
    wide = lax.all_gather(value, "tok", axis=1, tiled=True)
    return lax.all_gather(wide, "fsdp", axis=0, tiled=False)


def scatter_any(value):
    blocks, rows, full = value.shape
    mine = lax.psum_scatter(
        value.reshape(blocks * rows, full), "fsdp", scatter_dimension=0, tiled=True
    )
    return lax.psum_scatter(mine, "tok", scatter_dimension=1, tiled=True)


def on_device(tokens, expert_ids, gate_probs, w_gate, w_up, w_down, grad_out):
    tok_rows, topk = expert_ids.shape
    local = w_gate.shape[0]
    f32 = jnp.float32
    me = lax.axis_index("fsdp")

    routes = jnp.concatenate([expert_ids.astype(f32).T, gate_probs.T], axis=0)
    routes = lax.all_gather(routes, "fsdp", axis=0, tiled=False)
    all_tokens, all_grads = gather_any(tokens), gather_any(grad_out)
    blocks = all_tokens.shape[0]

    names = routes[:, :topk]
    mine = (me * local + jnp.arange(local, dtype=jnp.int32)).astype(f32)
    chosen = names[None] == mine[:, None, None, None]
    hit = jnp.any(chosen, axis=2)
    prob = jnp.sum(jnp.where(chosen, routes[None, :, topk:], 0.0), axis=2)
    before = jnp.triu(jnp.ones((tok_rows, tok_rows), jnp.bfloat16), 1)
    place = jnp.einsum("ebs,st->ebt", hit.astype(jnp.bfloat16), before, preferred_element_type=f32)
    place = jnp.where(hit, place, -1.0)
    filled = place[:, :, None, :] == jnp.arange(CAP, dtype=jnp.int32).astype(f32)[None, None, :, None]
    select = filled.astype(jnp.bfloat16)
    row_prob = jnp.sum(jnp.where(filled, prob[:, :, None, :], 0.0), axis=3)
    row_prob = row_prob.reshape(local, blocks * CAP, 1)

    def pick(values):
        rows = jnp.einsum("ebrt,btd->ebrd", select, values, preferred_element_type=f32)
        return rows.astype(jnp.bfloat16).reshape(local, blocks * CAP, values.shape[-1])

    def place_back(rows):
        rows = rows.astype(jnp.bfloat16).reshape(local, blocks, CAP, rows.shape[-1])
        values = jnp.einsum("ebrt,ebrd->btd", select, rows, preferred_element_type=f32)
        return values.astype(jnp.bfloat16)

    inputs = pick(all_tokens)
    cotangent = pick(all_grads)
    gate = jnp.einsum("erd,ehd->erh", inputs, w_gate, preferred_element_type=f32)
    upper = jnp.einsum("erd,ehd->erh", inputs, w_up, preferred_element_type=f32)
    raw = jnp.einsum("erd,ehd->erh", cotangent, w_down, preferred_element_type=f32)
    sigma = jax.nn.sigmoid(gate)
    active = gate * sigma
    hidden = active * upper
    weighted = (row_prob * hidden).astype(jnp.bfloat16)
    d_hidden = row_prob * raw
    d_gate = (d_hidden * upper * sigma * (1.0 + gate * (1.0 - sigma))).astype(jnp.bfloat16)
    d_upper = (d_hidden * active).astype(jnp.bfloat16)
    d_rows = jnp.sum(hidden * raw, axis=2).reshape(local, blocks, CAP)

    out_rows = jnp.einsum("erh,ehd->erd", weighted, w_down, preferred_element_type=f32)
    in_rows = jnp.einsum("erh,ehd->erd", d_gate, w_gate, preferred_element_type=f32)
    in_rows = in_rows + jnp.einsum("erh,ehd->erd", d_upper, w_up, preferred_element_type=f32)
    part_out, part_in = place_back(out_rows), place_back(in_rows)
    layer_out, d_tokens = scatter_any(part_out), scatter_any(part_in)

    d_w_down = jnp.einsum("erh,erd->ehd", weighted, cotangent, preferred_element_type=f32)
    d_w_gate = jnp.einsum("erh,erd->ehd", d_gate, inputs, preferred_element_type=f32)
    d_w_up = jnp.einsum("erh,erd->ehd", d_upper, inputs, preferred_element_type=f32)

    d_prob = jnp.sum(jnp.where(filled, d_rows[:, :, :, None], 0.0), axis=2)
    d_prob = jnp.sum(jnp.where(chosen, d_prob[:, :, None, :], 0.0), axis=0)
    d_prob = d_prob.reshape(blocks, topk * tok_rows)
    d_prob = lax.all_to_all(d_prob, "fsdp", split_axis=0, concat_axis=0, tiled=True)
    d_prob = jnp.sum(d_prob, axis=0)
    size = lax.axis_size("tok")
    mine_only = d_prob
    for turn in range(1, size):
        pairs = [(i, (i + turn) % size) for i in range(size)]
        d_prob = d_prob + lax.ppermute(mine_only, "tok", pairs)
    d_gate_probs = d_prob.reshape(topk, tok_rows).T
    return (layer_out, d_tokens, d_gate_probs, d_w_gate, d_w_up, d_w_down)


def solution(mesh):
    by_kernel = mesh.shape["fsdp"] == 16 and mesh.shape["tok"] == 2
    return jax.shard_map(
        by_one_kernel if by_kernel else on_device,
        mesh=mesh,
        in_specs=(
            P("fsdp", "tok"),
            P("fsdp", None),
            P("fsdp", None),
            P("fsdp", "tok", None),
            P("fsdp", "tok", None),
            P("fsdp", "tok", None),
            P("fsdp", "tok"),
        ),
        out_specs=(
            P("fsdp", "tok"),
            P("fsdp", "tok"),
            P("fsdp", None),
            P("fsdp", "tok", None),
            P("fsdp", "tok", None),
            P("fsdp", "tok", None),
        ),
        check_vma=False,
    )
```

```python
import functools

import jax
import jax.numpy as jnp
from jax import lax
from jax.experimental import pallas as pl
from jax.experimental.pallas import tpu as pltpu
from jax.sharding import PartitionSpec as P

CAP = 32
MESH = pl.DeviceIdType.MESH


def flip(bit, change):
    return 1 - bit if change else bit


class Place:
    def __init__(self):
        f = lax.axis_index("fsdp")
        self.t = lax.axis_index("tok")
        self.core = f % 2
        self.x = (f // 2) % 2
        self.z0 = (f // 4) % 2
        self.z1 = f // 8

        self.inner = self.z0 + self.z1 - 2 * self.z0 * self.z1

    def index(self, z1, z0, dx, dc):
        return (z1 * 2 + z0) * 4 + flip(self.x, dx) * 2 + flip(self.core, dc)

    def block(self, dx=0, dc=0):
        return self.index(self.z1, self.z0, dx, dc)

    def far(self, slot, dx=0):
        if slot < 2:
            z1, z0 = self.z1, flip(self.z0, slot)
        else:
            turn = self.inner if slot == 2 else 1 - self.inner
            z1, z0 = 1 - self.z1, self.z0 + turn - 2 * self.z0 * turn
        return (self.index(z1, z0, dx, 0), self.t)

    def slot_there(self, slot):
        return slot if slot < 2 else 3 - self.inner

    def inward(self):
        z = self.inner * (2 - self.z1) + (1 - self.inner) * (1 + self.z1)
        return (z * 4 + self.x * 2 + self.core, self.t)

    def outward(self):
        return (3 * self.z1 * 4 + self.x * 2 + self.core, self.t)

    def device(self, dx=0, dy=0, dc=0):
        return (self.block(dx, dc), flip(self.t, dy))

    def columns(self, dy, width):
        return pl.ds(pl.multiple_of(flip(self.t, dy) * width, width), width)

    def partners(self):
        return (
            [self.far(slot) for slot in (1, 2, 3)]
            + [self.far(slot, 1) for slot in range(4)]
            + [self.device(dy=1), self.device(dc=1)]
        )


def greet(place):
    barrier = pltpu.get_barrier_semaphore()
    partners = place.partners()
    for partner in partners:
        pl.semaphore_signal(barrier, inc=1, device_id=partner, device_id_type=MESH)
    pl.semaphore_wait(barrier, len(partners))


def arrive(ref, sem):
    pltpu.make_async_copy(ref, ref, sem).wait()


def layer_kernel(
    tok_in, grad_in, routes_in, wg_in, wu_in, wd_in,
    x_out, c_out, hid_out, dg_out, du_out, far_out, give0, give1, keep0, keep1, layer_out, dtok_out, dprob_out,
    g, x, xs, wg, wu, wd, act, turned, wide, near, zbuf,
    routes, sel, back, row_prob, inverse, dr, drs, dpart, dbuf, dsum,
    own_sem, w_sem, zs_sem, xsend_sem, ysend_sem, recv_sem,
    rs_sem, rr_sem, px_sem, pr_sem, st_sem, sr_sem, ds_sem, dr_sem,
    xo_sem, ao_sem, ws_sem, wr_sem, ns_sem, nr_sem, ss_sem, sz_sem,
    qs_sem, qr_sem, far_sem, own_out_sem, credit,
):
    place = Place()
    f32, bf16 = jnp.float32, jnp.bfloat16
    rows, width = tok_in.shape
    full = 2 * width
    half = rows // 2
    local, hid = wg.shape[:2]
    topk = 4
    me = place.device

    def start(copy):
        copy.start()
        return copy

    def remote(source, target, ssem, rsem, to):
        return start(
            pltpu.make_async_remote_copy(
                src_ref=source, dst_ref=target, send_sem=ssem, recv_sem=rsem,
                device_id=to, device_id_type=MESH,
            )
        )

    own = [
        start(pltpu.make_async_copy(ref, g.at[0, 0, a, :, place.columns(0, width)], own_sem.at[a]))
        for a, ref in enumerate((tok_in, grad_in))
    ]
    greet(place)
    sent = {}

    for dz in range(4):
        for dx in range(2):
            if dz or dx:
                j = dz * 2 + dx
                there = place.slot_there(dz) * 2 + dx
                sent["r", j] = remote(
                    routes_in, routes.at[there], rs_sem.at[j], rr_sem.at[there], place.far(dz, dx)
                )
    routes[0] = routes_in[...]
    for copy in own:
        copy.wait()

    def piece(h, dz, dx, dy):
        return g.at[dz, dx, :, pl.ds(h * half, half), place.columns(dy, width)]

    def by_z(h, to, slot, there, k):
        return start(
            pltpu.make_async_remote_copy(
                src_ref=piece(h, slot, 0, 0), dst_ref=piece(h, there, 0, 0),
                send_sem=zs_sem.at[h, k], recv_sem=recv_sem.at[h, there, 0, 0],
                device_id=to, device_id_type=MESH,
            )
        )

    inner = place.inner == 1

    def own_z():
        for h in range(2):
            sent["z", h, 0] = by_z(h, place.inward(), 0, 1 + place.inner, 0)

            @pl.when(inner)
            def _():
                by_z(h, place.outward(), 0, 1, 4)

    def pass_on(slot):
        @pl.when(inner)
        def _():
            for h in range(2):
                got(h, slot, 0, 0)
                if slot == 1:
                    by_z(h, place.inward(), 1, 3, 1)
                else:
                    by_z(h, place.outward(), slot, slot, slot)

    def passed_on(k):
        slot = k % 4

        @pl.when(inner)
        def _():
            for h in range(2):
                pltpu.make_async_copy(piece(h, slot, 0, 0), piece(h, slot, 0, 0), zs_sem.at[h, k]).wait()

    def by_x(h, dz, dy):
        sent["x", h, dz, dy] = remote(
            piece(h, dz, 0, dy), piece(h, dz, 1, dy), xsend_sem.at[h, dz, dy],
            recv_sem.at[h, dz, 1, dy], me(1),
        )

    def by_y(h, dz, dx):
        sent["y", h, dz, dx] = remote(
            piece(h, dz, dx, 0), piece(h, dz, dx, 0), ysend_sem.at[h, dz, dx],
            recv_sem.at[h, dz, dx, 1], me(0, 1),
        )

    def got(h, dz, dx, dy):
        arrive(piece(h, dz, dx, dy), recv_sem.at[h, dz, dx, dy])

    def column(dz):
        for h in range(2):
            if dz:
                @pl.when(jnp.logical_not(inner))
                def _():
                    got(h, dz, 0, 0)

            if h == 0:
                by_x(h, dz, 0)
                by_y(h, dz, 0)
            else:
                by_y(h, dz, 0)
                by_x(h, dz, 0)

    def plane(dz):
        got(0, dz, 1, 0)
        by_y(0, dz, 1)
        got(1, dz, 0, 1)
        by_x(1, dz, 1)

    def last(dz):
        got(0, dz, 0, 1)
        got(1, dz, 1, 0)
        got(0, dz, 1, 1)
        got(1, dz, 1, 1)

    experts = [
        (place.block(0, e // local) * local + e % local).astype(f32) for e in range(2 * local)
    ]

    def build(j):
        names = routes[j, :topk, :]
        probs = routes[j, topk:, :]
        before = (
            lax.broadcasted_iota(jnp.int32, (rows, rows), 0)
            < lax.broadcasted_iota(jnp.int32, (rows, rows), 1)
        ).astype(f32).astype(bf16)
        hits, prob = [], []
        for e in experts:
            chosen = names == e
            hits.append(jnp.max(jnp.where(chosen, 1.0, 0.0), axis=0, keepdims=True))
            prob.append(jnp.sum(jnp.where(chosen, probs, 0.0), axis=0, keepdims=True))
        hit = jnp.concatenate(hits + [jnp.zeros((4, rows), f32)], axis=0)
        spot = jnp.dot(hit.astype(bf16), before, preferred_element_type=f32)
        spot = jnp.where(hit > 0.0, spot, -1.0)
        number = lax.broadcasted_iota(jnp.int32, (CAP, rows), 0).astype(f32)
        ones, high, low, full_prob, inv = [], [], [], [], []
        for e in range(2 * local):
            filled = jnp.broadcast_to(spot[e : e + 1], (CAP, rows)) == number
            top = prob[e].astype(bf16).astype(f32)
            ones.append(jnp.where(filled, 1.0, 0.0))
            high.append(jnp.where(filled, top, 0.0))
            low.append(jnp.where(filled, prob[e] - top, 0.0))
            full_prob.append(jnp.where(filled, prob[e], 0.0))
            inv.append(jnp.where(hits[e] > 0.0, 1.0 / jnp.maximum(prob[e], 1e-30), 0.0))
        ones = jnp.concatenate(ones, axis=0)
        sel[j] = ones.astype(bf16)
        back[j, 0] = ones.T.astype(bf16)
        back[j, 1] = jnp.concatenate(high, axis=0).T.astype(bf16)
        back[j, 2] = jnp.concatenate(low, axis=0).T.astype(bf16)
        row_prob[j] = jnp.sum(jnp.concatenate(full_prob, axis=0), axis=1, keepdims=True)
        inverse[j] = jnp.concatenate(inv + [jnp.zeros((4, rows), f32)], axis=0)

    def build_all(first, end):
        for j in range(first, end):
            if j:
                arrive(routes.at[j], rr_sem.at[j])

        @pl.loop(first, end)
        def _(j):
            build(j)

    tile = 512

    def select(dz):
        @pl.loop(0, 2)
        def _(dx):
            j = dz * 2 + dx
            at = pl.ds(pl.multiple_of(dx * CAP, CAP), CAP)

            @pl.loop(0, full // tile)
            def _(n):
                cols = pl.ds(pl.multiple_of(n * tile, tile), tile)
                for a in range(2):
                    picked = jnp.dot(sel[j], g[dz, dx, a, :, cols], preferred_element_type=f32)
                    if a:
                        picked = picked * row_prob[j]
                    picked = picked.astype(bf16)
                    for l in range(local):
                        x[a, l, dz, at, cols] = picked[l * CAP : (l + 1) * CAP]
                        m = local + l
                        xs[a, l, dz, at, cols] = picked[m * CAP : (m + 1) * CAP]

        sent["p", dz] = remote(
            xs.at[:, :, dz], x.at[:, :, dz, pl.ds(half, half)], px_sem.at[dz], pr_sem.at[dz], me(0, 0, 1)
        )

    def packed(dz):
        arrive(x.at[:, :, dz, pl.ds(half, half)], pr_sem.at[dz])
        for a, ref in enumerate((x_out, c_out)):
            sent["xo", a, dz] = start(
                pltpu.make_async_copy(x.at[a, :, dz], ref.at[:, dz], xo_sem.at[a, dz])
            )

    nt = (((1,), (1,)), ((), ()))
    tiles = [(h, min(256, hid - h)) for h in range(0, hid, 256)]

    def forward(dz, l):
        if dz == 0:
            for i in range(3):
                loads[i, l].wait()
        total = jnp.zeros((rows, 1), f32)
        for h, n in tiles:
            at = pl.ds(h, n)
            gate = lax.dot_general(x[0, l, dz], wg[l, at, :], nt, preferred_element_type=f32)
            upper = lax.dot_general(x[0, l, dz], wu[l, at, :], nt, preferred_element_type=f32)
            d_hidden = lax.dot_general(x[1, l, dz], wd[l, at, :], nt, preferred_element_type=f32)
            sigma = jax.nn.sigmoid(gate)
            active = gate * sigma
            hidden = active * upper
            total = total + jnp.sum(hidden * d_hidden, axis=1, keepdims=True)
            act[0, l, dz, :, at] = hidden.astype(bf16)
            act[1, l, dz, :, at] = (d_hidden * upper * sigma * (1.0 + gate * (1.0 - sigma))).astype(bf16)
            act[2, l, dz, :, at] = (d_hidden * active).astype(bf16)
        total = jnp.broadcast_to(total, (rows, rows))
        for dx in range(2):
            dr[dz, dx, l * CAP : (l + 1) * CAP, :] = total[dx * CAP : (dx + 1) * CAP]
            drs[dz, dx, l * CAP : (l + 1) * CAP, :] = total[half + dx * CAP : half + (dx + 1) * CAP]

    def handed(dz):
        sent["d", dz] = remote(
            drs.at[dz], dr.at[dz, :, pl.ds(half, half)], ds_sem.at[dz], dr_sem.at[dz], me(0, 0, 1)
        )
        sent.pop(("xo", 0, dz)).wait()
        sent.pop(("xo", 1, dz)).wait()
        pl.semaphore_signal(credit.at[dz], inc=1, device_id=me(0, 0, 1), device_id_type=MESH)
        sent.pop(("p", dz)).wait_send()

    def turn(dz):
        refs = (hid_out, dg_out, du_out)
        for i, ref in enumerate(refs):
            if dz:
                sent.pop(("ao", i, dz - 1)).wait()
            for l in range(local):
                turned[i, l] = act[i, l, dz].T
            sent["ao", i, dz] = start(
                pltpu.make_async_copy(
                    turned.at[i], ref.at[:, :, pl.ds(dz * rows, rows)], ao_sem.at[i, dz]
                )
            )

    def backward(dz, l):
        mine = pl.ds(l * CAP, CAP)

        @pl.loop(0, full // tile)
        def _(n):
            cols = pl.ds(pl.multiple_of(n * tile, tile), tile)
            out = jnp.dot(act[0, l, dz], wd[l, :, cols], preferred_element_type=f32)
            back_rows = jnp.dot(act[1, l, dz], wg[l, :, cols], preferred_element_type=f32)
            back_rows = back_rows + jnp.dot(act[2, l, dz], wu[l, :, cols], preferred_element_type=f32)
            for a, value in enumerate((out.astype(bf16), back_rows.astype(bf16))):
                for dx in range(2):
                    x[a, dx, dz, mine, cols] = value[dx * CAP : (dx + 1) * CAP]
                    xs[a, dx, dz, mine, cols] = value[half + dx * CAP : half + (dx + 1) * CAP]

    def returned(dz):
        pl.semaphore_wait(credit.at[dz], 1)
        sent["s", dz] = remote(
            xs.at[:, :, dz], x.at[:, :, dz, pl.ds(half, half)], st_sem.at[dz], sr_sem.at[dz], me(0, 0, 1)
        )

    def put_back(dz):
        for h in range(2):
            for key in (("x", h, dz, 0), ("y", h, dz, 0)):
                sent.pop(key).wait_send()
        sent.pop(("y", 0, dz, 1)).wait_send()
        sent.pop(("x", 1, dz, 1)).wait_send()
        if dz == 0:
            for h in range(2):
                sent.pop(("z", h, 0)).wait_send()
            passed_on(4)
        else:
            passed_on(dz)
        arrive(x.at[:, :, dz, pl.ds(half, half)], sr_sem.at[dz])
        arrive(dr.at[dz, :, pl.ds(half, half)], dr_sem.at[dz])

        @pl.loop(0, 2)
        def _(dx):
            j = dz * 2 + dx

            @pl.loop(0, full // tile)
            def _(n):
                cols = pl.ds(pl.multiple_of(n * tile, tile), tile)
                out = jnp.dot(back[j, 1], x[0, dx, dz, :, cols], preferred_element_type=f32)
                out = out + jnp.dot(back[j, 2], x[0, dx, dz, :, cols], preferred_element_type=f32)
                g[dz, dx, 0, :, cols] = out.astype(bf16)
                into = jnp.dot(back[j, 0], x[1, dx, dz, :, cols], preferred_element_type=f32)
                g[dz, dx, 1, :, cols] = into.astype(bf16)

            names = routes[j, :topk, :]
            weighted = dr[dz, dx] * sel[j].astype(f32)
            total = jnp.zeros((topk, rows), f32)
            for e, name in enumerate(experts):
                value = jnp.sum(weighted[e * CAP : (e + 1) * CAP], axis=0, keepdims=True)
                value = value * inverse[j, e : e + 1, :]
                total = total + jnp.where(names == name, value, 0.0)
            dpart[j] = jnp.concatenate([total, jnp.zeros((8 - topk, rows), f32)], axis=0)

        for dx in range(2):
            j = dz * 2 + dx
            if j:
                there = place.slot_there(dz) * 2 + dx
                sent["q", j] = remote(
                    dpart.at[j], dbuf.at[there], qs_sem.at[j], qr_sem.at[there], place.far(dz, dx)
                )

    def send_wide(dz):
        for h in range(2):
            across = me(0, 1) if h == 0 else me(1)
            for other in (1, 0):
                dx, dy = (other, 1) if h == 0 else (1, other)
                sent["w", h, dz, other] = remote(
                    piece(h, dz, dx, dy), wide.at[h, dz, other], ws_sem.at[h, dz, other],
                    wr_sem.at[h, dz, other], across,
                )

    def add(target, source):
        for a in range(2):
            @pl.loop(0, half // 16)
            def _(i):
                at = pl.ds(pl.multiple_of(i * 16, 16), 16)
                target[a, at, :] = target[a, at, :] + source[a, at, :]

    def send_near(dz):
        for other in (1, 0):
            for h in range(2):
                dx, dy = (other, 0) if h == 0 else (0, other)
                arrive(wide.at[h, dz, other], wr_sem.at[h, dz, other])
                add(wide.at[h, dz, other], piece(h, dz, dx, dy))
                if other:
                    along = me(1) if h == 0 else me(0, 1)
                    sent["n", h, dz] = remote(
                        wide.at[h, dz, 1], near.at[h, dz], ns_sem.at[h, dz], nr_sem.at[h, dz], along
                    )

    def send_z(dz):
        for h in range(2):
            arrive(near.at[h, dz], nr_sem.at[h, dz])
            add(near.at[h, dz], wide.at[h, dz, 0])
            if dz == 3:
                rows_there = pl.ds(h * half, half)
                sent["far", h] = start(
                    pltpu.make_async_copy(near.at[h, 3], far_out.at[:, rows_there], far_sem.at[h])
                )
            elif dz:
                there = place.slot_there(dz)
                sent["f", h, dz] = remote(
                    near.at[h, dz], zbuf.at[h, there - 1], ss_sem.at[h, dz], sz_sem.at[h, there],
                    place.far(dz),
                )

    def leave_own():
        gives, keeps = (give0, give1), (keep0, keep1)
        for h in range(2):
            for far, refs in ((1, gives), (0, keeps)):
                for other in range(2):
                    dx, dy = (other, far) if h == 0 else (far, other)
                    sent["own", h, far, other] = start(
                        pltpu.make_async_copy(
                            piece(h, 0, dx, dy), refs[h].at[other], own_out_sem.at[h, far, other]
                        )
                    )

    own_z()
    column(0)
    loads = {}
    for l in range(local):
        for i, (ref, to) in enumerate(((wg_in, wg), (wu_in, wu), (wd_in, wd))):
            loads[i, l] = start(pltpu.make_async_copy(ref.at[l], to.at[l], w_sem.at[i, l]))
    build_all(0, 8)
    plane(0)
    pass_on(1)
    column(1)
    pass_on(2)
    last(0)
    select(0)
    for dz in range(4):
        if dz < 3:
            plane(dz + 1)
        if dz == 2:
            send_wide(1)
        if dz == 0:
            pass_on(3)
        packed(dz)
        forward(dz, 0)
        if dz < 2:
            column(dz + 2)
        if dz == 3:
            send_near(1)
        forward(dz, 1)
        handed(dz)
        backward(dz, 0)
        backward(dz, 1)
        returned(dz)
        if dz == 3:
            send_near(2)
            send_z(1)
        if dz < 3:
            last(dz + 1)
            select(dz + 1)
        put_back(dz)
        if dz >= 2:
            send_wide(dz)
        if dz == 0:
            leave_own()
        if dz < 2:
            turn(dz)
    turn(2)
    turn(3)
    send_z(2)
    send_near(3)
    send_z(3)

    total = dpart[0]
    for j in range(1, 8):
        arrive(dbuf.at[j], qr_sem.at[j])
        total = total + dbuf[j]
    dsum[0] = total
    peer = remote(dsum.at[0], dsum.at[1], qs_sem.at[0], qr_sem.at[0], me(0, 1))

    arrive(dsum.at[1], qr_sem.at[0])
    dprob_out[...] = dsum[0] + dsum[1]
    for h in range(2):
        arrive(zbuf.at[h, 0], sz_sem.at[h, 1])

    def finish(others):
        for a, ref in enumerate((layer_out, dtok_out)):
            for h in range(2):
                @pl.loop(0, half // 16)
                def _(i):
                    at = pl.ds(pl.multiple_of(i * 16, 16), 16)
                    total = zbuf[h, 0, a, at, :].astype(f32)
                    for dz in others:
                        total = total + zbuf[h, dz - 1, a, at, :].astype(f32)
                    to = pl.ds(pl.multiple_of(h * half + i * 16, 16), 16)
                    ref[to, :] = total

    @pl.when(inner)
    def _():
        for dz in (2, 3):
            for h in range(2):
                arrive(zbuf.at[h, dz - 1], sz_sem.at[h, dz])
        finish((2, 3))

    @pl.when(jnp.logical_not(inner))
    def _():
        finish(())

    peer.wait_send()
    for key, copy in sent.items():
        if key[0] in ("ao", "far", "own"):
            copy.wait()
        else:
            copy.wait_send()


def layer(tokens, grad_out, routes, w_gate, w_up, w_down):
    rows, width = tokens.shape
    local, hid, full = w_gate.shape
    half = rows // 2
    bf16, f32 = jnp.bfloat16, jnp.float32
    any_space = pl.BlockSpec(memory_space=pl.ANY)
    vmem = pl.BlockSpec(memory_space=pltpu.VMEM)
    shape = jax.ShapeDtypeStruct
    packed = shape((local, 4, rows, full), bf16)
    acts = shape((local, hid, 4 * rows), bf16)
    out = shape((rows, width), f32)
    far = shape((2, rows, width), bf16)
    quarter = shape((2, 2, half, width), bf16)
    dma = pltpu.SemaphoreType.DMA
    return pl.pallas_call(
        layer_kernel,
        out_shape=(packed, packed, acts, acts, acts, far) + (quarter,) * 4 + (out, out, shape((8, rows), f32)),
        in_specs=[any_space, any_space, vmem, any_space, any_space, any_space],
        out_specs=[any_space] * 10 + [vmem] * 3,
        scratch_shapes=[
            pltpu.VMEM((4, 2, 2, rows, full), bf16),
            pltpu.VMEM((2, 2, 4, rows, full), bf16),
            pltpu.VMEM((2, 2, 4, half, full), bf16),
            pltpu.VMEM((local, hid, full), bf16),
            pltpu.VMEM((local, hid, full), bf16),
            pltpu.VMEM((local, hid, full), bf16),
            pltpu.VMEM((3, local, 4, rows, hid), bf16),
            pltpu.VMEM((3, local, hid, rows), bf16),
            pltpu.VMEM((2, 4, 2, 2, half, width), bf16),
            pltpu.VMEM((2, 4, 2, half, width), bf16),
            pltpu.VMEM((2, 3, 2, half, width), bf16),
            pltpu.VMEM((8, 8, rows), f32),
            pltpu.VMEM((8, rows, rows), bf16),
            pltpu.VMEM((8, 3, rows, rows), bf16),
            pltpu.VMEM((8, rows, 1), f32),
            pltpu.VMEM((8, 8, rows), f32),
            pltpu.VMEM((4, 2, rows, rows), f32),
            pltpu.VMEM((4, 2, half, rows), f32),
            pltpu.VMEM((8, 8, rows), f32),
            pltpu.VMEM((8, 8, rows), f32),
            pltpu.VMEM((2, 8, rows), f32),
            dma((2,)), dma((3, local)), dma((2, 5)), dma((2, 4, 2)), dma((2, 4, 2)), dma((2, 4, 2, 2)),
            dma((8,)), dma((8,)), dma((4,)), dma((4,)), dma((4,)), dma((4,)), dma((4,)), dma((4,)),
            dma((2, 4)), dma((3, 4)), dma((2, 4, 2)), dma((2, 4, 2)), dma((2, 4)), dma((2, 4)),
            dma((2, 4)), dma((2, 4)), dma((8,)), dma((8,)), dma((2,)), dma((2, 2, 2)),
            pltpu.SemaphoreType.REGULAR((4,)),
        ],
        compiler_params=pltpu.CompilerParams(
            collective_id=0, has_side_effects=True, vmem_limit_bytes=61 * 2**20
        ),
    )(tokens, grad_out, routes, w_gate, w_up, w_down)


def weight_kernel(count, *refs):
    acts, rows, outs = refs[:count], refs[count], refs[count + 1 :]
    for act, out in zip(acts, outs):
        out[0] = jnp.dot(act[0], rows[0], preferred_element_type=jnp.float32)


def weights(acts, values):
    local, hid, rows = acts[0].shape
    full = values.shape[2]
    count, tile = len(acts), 512
    of_act = pl.BlockSpec((1, hid, rows), lambda l, n: (l, 0, 0))
    of_rows = pl.BlockSpec((1, rows, tile), lambda l, n: (l, 0, n))
    out = pl.BlockSpec((1, hid, tile), lambda l, n: (l, 0, n))
    return pl.pallas_call(
        functools.partial(weight_kernel, count),
        grid=(local, full // tile),
        out_shape=[jax.ShapeDtypeStruct((local, hid, full), jnp.float32)] * count,
        in_specs=[of_act] * count + [of_rows],
        out_specs=[out] * count,
        compiler_params=pltpu.CompilerParams(vmem_limit_bytes=60 * 2**20),
        cost_estimate=pl.CostEstimate(
            flops=2 * count * local * hid * rows * full,
            bytes_accessed=5 * count * local * hid * full,
            transcendentals=0,
        ),
    )(*acts, values)


def by_one_kernel(tokens, expert_ids, gate_probs, w_gate, w_up, w_down, grad_out):
    topk = expert_ids.shape[1]
    local, hid, full = w_gate.shape
    f32 = jnp.float32
    routes = jnp.concatenate([expert_ids.astype(f32).T, gate_probs.T], axis=0)
    x, c, hidden, d_gate, d_up, far, *own, part_out, part_in, d_prob = layer(
        tokens, grad_out, routes, w_gate, w_up, w_down
    )
    x, c = (v.reshape(local, -1, full) for v in (x, c))

    blocks = lax.axis_size("fsdp")
    by_y = functools.partial(lax.ppermute, axis_name="tok", perm=[(0, 1), (1, 0)])
    by_x = functools.partial(
        lax.ppermute, axis_name="fsdp", perm=[(i, i + 2 - i // 2 % 2 * 4) for i in range(blocks)]
    )
    give0, give1, keep0, keep1 = own
    near0, near1 = by_y(give0), by_x(give1)
    ends = [(z * 4 + i, (3 - z) * 4 + i) for z in (0, 3) for i in range(4)]
    inners = [(z * 4 + i, (6 - 3 * z) * 4 + i) for z in (1, 2) for i in range(4)]
    far = [lax.ppermute(far, "fsdp", pairs) for pairs in (ends, inners)]
    d_w_gate, d_w_up = weights((d_gate, d_up), x)
    sum0, sum1 = near0 + keep0, near1 + keep1
    sum0, sum1, hidden = lax.optimization_barrier((sum0, sum1, hidden))
    near0, near1 = by_x(sum0[1]), by_y(sum1[1])
    d_w_down = jnp.einsum("lhr,lrd->lhd", hidden, c, preferred_element_type=f32)

    def total(a, part):
        halves = [near[a].astype(f32) + held[0, a].astype(f32) for near, held in ((near0, sum0), (near1, sum1))]
        value = part + jnp.concatenate(halves, axis=0) + far[0][a].astype(f32) + far[1][a].astype(f32)
        return value.astype(tokens.dtype)

    layer_out, d_tokens = total(0, part_out), total(1, part_in)
    return (layer_out, d_tokens, d_prob[:topk].T, d_w_gate, d_w_up, d_w_down)


def gather_any(value):
    wide = lax.all_gather(value, "tok", axis=1, tiled=True)
    return lax.all_gather(wide, "fsdp", axis=0, tiled=False)


def scatter_any(value):
    blocks, rows, full = value.shape
    mine = lax.psum_scatter(
        value.reshape(blocks * rows, full), "fsdp", scatter_dimension=0, tiled=True
    )
    return lax.psum_scatter(mine, "tok", scatter_dimension=1, tiled=True)


def on_device(tokens, expert_ids, gate_probs, w_gate, w_up, w_down, grad_out):
    tok_rows, topk = expert_ids.shape
    local = w_gate.shape[0]
    f32 = jnp.float32
    me = lax.axis_index("fsdp")

    routes = jnp.concatenate([expert_ids.astype(f32).T, gate_probs.T], axis=0)
    routes = lax.all_gather(routes, "fsdp", axis=0, tiled=False)
    all_tokens, all_grads = gather_any(tokens), gather_any(grad_out)
    blocks = all_tokens.shape[0]

    names = routes[:, :topk]
    mine = (me * local + jnp.arange(local, dtype=jnp.int32)).astype(f32)
    chosen = names[None] == mine[:, None, None, None]
    hit = jnp.any(chosen, axis=2)
    prob = jnp.sum(jnp.where(chosen, routes[None, :, topk:], 0.0), axis=2)
    before = jnp.triu(jnp.ones((tok_rows, tok_rows), jnp.bfloat16), 1)
    place = jnp.einsum("ebs,st->ebt", hit.astype(jnp.bfloat16), before, preferred_element_type=f32)
    place = jnp.where(hit, place, -1.0)
    filled = place[:, :, None, :] == jnp.arange(CAP, dtype=jnp.int32).astype(f32)[None, None, :, None]
    select = filled.astype(jnp.bfloat16)
    row_prob = jnp.sum(jnp.where(filled, prob[:, :, None, :], 0.0), axis=3)
    row_prob = row_prob.reshape(local, blocks * CAP, 1)

    def pick(values):
        rows = jnp.einsum("ebrt,btd->ebrd", select, values, preferred_element_type=f32)
        return rows.astype(jnp.bfloat16).reshape(local, blocks * CAP, values.shape[-1])

    def place_back(rows):
        rows = rows.astype(jnp.bfloat16).reshape(local, blocks, CAP, rows.shape[-1])
        values = jnp.einsum("ebrt,ebrd->btd", select, rows, preferred_element_type=f32)
        return values.astype(jnp.bfloat16)

    inputs = pick(all_tokens)
    cotangent = pick(all_grads)
    gate = jnp.einsum("erd,ehd->erh", inputs, w_gate, preferred_element_type=f32)
    upper = jnp.einsum("erd,ehd->erh", inputs, w_up, preferred_element_type=f32)
    raw = jnp.einsum("erd,ehd->erh", cotangent, w_down, preferred_element_type=f32)
    sigma = jax.nn.sigmoid(gate)
    active = gate * sigma
    hidden = active * upper
    weighted = (row_prob * hidden).astype(jnp.bfloat16)
    d_hidden = row_prob * raw
    d_gate = (d_hidden * upper * sigma * (1.0 + gate * (1.0 - sigma))).astype(jnp.bfloat16)
    d_upper = (d_hidden * active).astype(jnp.bfloat16)
    d_rows = jnp.sum(hidden * raw, axis=2).reshape(local, blocks, CAP)

    out_rows = jnp.einsum("erh,ehd->erd", weighted, w_down, preferred_element_type=f32)
    in_rows = jnp.einsum("erh,ehd->erd", d_gate, w_gate, preferred_element_type=f32)
    in_rows = in_rows + jnp.einsum("erh,ehd->erd", d_upper, w_up, preferred_element_type=f32)
    part_out, part_in = place_back(out_rows), place_back(in_rows)
    layer_out, d_tokens = scatter_any(part_out), scatter_any(part_in)

    d_w_down = jnp.einsum("erh,erd->ehd", weighted, cotangent, preferred_element_type=f32)
    d_w_gate = jnp.einsum("erh,erd->ehd", d_gate, inputs, preferred_element_type=f32)
    d_w_up = jnp.einsum("erh,erd->ehd", d_upper, inputs, preferred_element_type=f32)

    d_prob = jnp.sum(jnp.where(filled, d_rows[:, :, :, None], 0.0), axis=2)
    d_prob = jnp.sum(jnp.where(chosen, d_prob[:, :, None, :], 0.0), axis=0)
    d_prob = d_prob.reshape(blocks, topk * tok_rows)
    d_prob = lax.all_to_all(d_prob, "fsdp", split_axis=0, concat_axis=0, tiled=True)
    d_prob = jnp.sum(d_prob, axis=0)
    size = lax.axis_size("tok")
    mine_only = d_prob
    for turn in range(1, size):
        pairs = [(i, (i + turn) % size) for i in range(size)]
        d_prob = d_prob + lax.ppermute(mine_only, "tok", pairs)
    d_gate_probs = d_prob.reshape(topk, tok_rows).T
    return (layer_out, d_tokens, d_gate_probs, d_w_gate, d_w_up, d_w_down)


def solution(mesh):
    by_kernel = mesh.shape["fsdp"] == 16 and mesh.shape["tok"] == 2
    return jax.shard_map(
        by_one_kernel if by_kernel else on_device,
        mesh=mesh,
        in_specs=(
            P("fsdp", "tok"),
            P("fsdp", None),
            P("fsdp", None),
            P("fsdp", "tok", None),
            P("fsdp", "tok", None),
            P("fsdp", "tok", None),
            P("fsdp", "tok"),
        ),
        out_specs=(
            P("fsdp", "tok"),
            P("fsdp", "tok"),
            P("fsdp", None),
            P("fsdp", "tok", None),
            P("fsdp", "tok", None),
            P("fsdp", "tok", None),
        ),
        check_vma=False,
    )
```
